32 devices in a mesh: wide: 8 (over z, y), tp: 4 (over x, core).
Axes of the slice: x: 2, y: 2, z: 4, core: 2. Of those that a mesh axis runs over, the one named last changes fastest.
Arguments:
- tokens: bfloat16 [12800, 768], P(('wide', 'tp')), may hold values from -6 to 6
- norm_gains: bfloat16 [2, 768], P(None, ('wide', 'tp')), may hold values from 0.5 to 1.5
- shifts: bfloat16 [5, 768], P(None, ('wide', 'tp')), may hold values from -1 to 1
- attn_weight: bfloat16 [3, 768, 768], P(None, 'wide', 'tp'), may hold values from -0.3125 to 0.3125
- out_weight: bfloat16 [768, 768], P('tp', 'wide'), may hold values from -0.625 to 0.625
- router_weight: bfloat16 [8, 768], P(None, ('wide', 'tp')), may hold values from -0.15625 to 0.15625
- expert_in: bfloat16 [8, 768, 3072], P('wide', None, 'tp'), may hold values from -0.21875 to 0.21875
- expert_in_bias: bfloat16 [8, 3072], P('wide', 'tp'), may hold values from -1 to 1
- expert_down: bfloat16 [8, 768, 3072], P('wide', None, 'tp'), may hold values from -0.21875 to 0.21875
- expert_down_bias: bfloat16 [8, 768], P('wide', 'tp'), may hold values from -1 to 1
- routes: int32 [12800, 2], P('wide'), may hold values from 0 to 7, all different within a row; in each aligned block of 1600 rows (0 to 1599, 1600 to 3199, ...) at most 504 rows name the same one
- cotangent: bfloat16 [12800, 768], P(('wide', 'tp')), may hold values from -6 to 6
Outputs:
- activations: bfloat16 [12800, 768], P(('wide', 'tp'))
- tokens_grad: float32 [12800, 768], P(('wide', 'tp'))
- norm_gains_grad: float32 [2, 768], P(None, ('wide', 'tp'))
- shifts_grad: float32 [5, 768], P(None, ('wide', 'tp'))
- attn_weight_grad: float32 [3, 768, 768], P(None, 'wide', 'tp')
- out_weight_grad: float32 [768, 768], P('tp', 'wide')
- router_grad: float32 [8, 768], P(None, ('wide', 'tp'))
- expert_in_grad: float32 [8, 768, 3072], P('wide', None, 'tp')
- expert_in_bias_grad: float32 [8, 3072], P('wide', 'tp')
- expert_down_grad: float32 [8, 768, 3072], P('wide', None, 'tp')
- expert_down_bias_grad: float32 [8, 768], P('wide', 'tp')
The draws below stay inside these ranges and needn't reach their ends.
Inputs may be any that keep to these rules, and one draw needn't show every extreme that they name: `routes`: in each group of 1600 consecutive rows (one index of wide) no expert is named by more than 504 rows, a bound that some block reaches; the two experts of a row differ.
All inputs are finite; a program needn't handle non-finite values.
Results may differ from the reference program's by a relative error of at most 0.028.
Values may be sent and summed in bfloat16 or wider, within the bound.
No kernel may reach another device: no remote copies, remote signals or barrier semaphores. Data moves between devices by JAX's collectives and lax.ppermute only.
A program may use at most 192 MiB of HBM per device.

```python
import math
import jax
import jax.numpy as jnp
import numpy as np
from jax import lax

D = 768
HEADS = 12
HD = 64
FF = 3072
IMG = 8
SEQ = 200
VALID = 197
EXPERTS = 8
CAP = 504
TOKENS = 12800


def with_spikes(values, own_key, source, target, parts, factor):
    owner, partner = [(jnp.arange(values.shape[position]) // (values.shape[position] // parts)).reshape([-1 if axis == position else 1 for axis in range(values.ndim)]) for position in (source, target)]
    chosen = jax.random.permutation(own_key, parts)[partner]
    strong = (owner == chosen) | (owner == (partner + parts // 2) % parts)
    return jnp.where(strong, factor * values, values)


def levels(stream_key, dims, split, smallest, high):
    def one(position, shards_of):
        heights = jax.random.uniform(jax.random.fold_in(jax.random.fold_in(stream_key, 6), position), (shards_of,), jnp.float32, smallest / len(split), high / len(split))
        return jnp.repeat(jnp.exp(heights), dims[position] // shards_of).reshape((-1,) + (1,) * (len(dims) - position - 1))

    level = one(*split[0])
    for cut in split[1:]:
        level = level * one(*cut)
    return level


def deal_out(key, own, number, rows, amount, top, most, skew):
    order = jax.random.permutation(key, amount)
    packed, usual = shares(amount, rows * top, most, skew, True), shares(amount, rows * top, most, skew, False)
    places = jnp.arange(amount)

    def named(sizes, turn):
        used = int((sizes > 0).sum())
        fixed = max(1, used // 4)
        passed = fixed + (places - fixed + turn * (used - fixed)) % max(1, amount - fixed)
        return jnp.zeros((amount,), jnp.int32).at[order[jnp.where(places < fixed, places, passed)]].set(jnp.asarray(sizes, jnp.int32))

    sizes = jnp.where(number % 4 == 0, named(packed, number // 4), named(usual, number - number // 4 - 1))
    mixed = jax.random.permutation(jax.random.fold_in(own, 3), amount)
    giver, taker = mixed[0:amount // 2 * 2:2], mixed[1:amount // 2 * 2:2]
    room = jnp.minimum(sizes[giver] - 1, most - sizes[taker]) // 2
    room = jnp.where((giver == order[0]) | (taker == order[0]) | (sizes[taker] == 0), 0, jnp.maximum(room, 0))
    passed = jax.random.randint(jax.random.fold_in(own, 4), (amount // 2,), 0, 1 << 20) % (room + 1)
    sizes = sizes.at[giver].add(-passed).at[taker].add(passed)
    labels = jnp.searchsorted(jnp.cumsum(sizes), jnp.arange(rows * top), side="right").astype(jnp.int32)
    grid = labels.reshape(top, rows).T
    grid = grid[jax.random.permutation(jax.random.fold_in(own, 1), rows)]
    turn = jax.random.randint(jax.random.fold_in(own, 2), (rows, 1), 0, top)
    return jnp.take_along_axis(grid, (jnp.arange(top)[None, :] + turn) % top, axis=1)


def shares(amount, total, bound, lean, full):
    loads = [(1 << 20) // math.isqrt(rank ** lean) + 1 for rank in range(1, amount + 1)]
    largest = bound if full else min(bound, max(-(-total // amount), total * loads[0] // sum(loads)))
    least = 1 if total - largest >= amount - 1 else 0
    counts, rest = [largest] + [least] * (amount - 1), total - largest - least * (amount - 1)
    while rest > 0:
        movable = [i for i in range(1, amount) if counts[i] < largest] or [i for i in range(1, amount) if counts[i] < bound]
        pool, remaining = sum([loads[i] for i in movable]), rest
        for i in movable:
            more = min(bound - counts[i], max(1, remaining * loads[i] // pool), rest)
            counts[i] = counts[i] + more
            rest = rest - more
    return np.array(counts)


def normal_values(own_key, shape, deviation, limit, pieces=(), held_as=jnp.bfloat16):
    values = deviation * jax.random.normal(own_key, shape, jnp.float32)
    if pieces:
        values = values * levels(own_key, shape, pieces, -0.22, 0.18)
    return jnp.clip(values, -limit, limit).astype(held_as)


def bell_draw_with(key, extent, width, limit, cuts, heavy, kind=jnp.bfloat16):
    array = width * jax.random.normal(key, extent, jnp.float32)
    if cuts:
        array = array * levels(key, extent, cuts, -0.22, 0.18)
    return jnp.clip(with_spikes(array, jax.random.fold_in(key, 3), *heavy), -limit, limit).astype(kind)


def setup_inputs(seed: int = 0) -> dict:
    splits = jax.random.split(jax.random.key(seed), 13)
    tokens = normal_values(splits[0], (TOKENS, D), 1.0, 6.0, ((0, 32),))
    norm_gains = jnp.clip(1.0 + 0.1 * jax.random.normal(splits[1], (2, D), jnp.float32), 0.5, 1.5).astype(jnp.bfloat16)
    shifts = normal_values(splits[2], (5, D), 0.2, 1.0, ((1, 32),))
    attn_weight = normal_values(splits[3], (3, D, D), (D // 2) ** -0.5, 0.3125, ((1, 8), (2, 4)))
    out_weight = normal_values(splits[4], (D, D), (D // 8) ** -0.5, 0.625, ((0, 4), (1, 8)))
    router_weight = normal_values(splits[5], (EXPERTS, D), (2 * D) ** -0.5, 0.15625, ((1, 32),))
    expert_in = normal_values(splits[6], (EXPERTS, D, FF), D ** -0.5, 0.21875, ((0, 8), (2, 4)))
    expert_in_bias = normal_values(splits[7], (EXPERTS, FF), 0.2, 1.0, ((0, 8), (1, 4)))
    expert_down = normal_values(splits[8], (EXPERTS, D, FF), (FF // 4) ** -0.5, 0.21875, ((0, 8), (2, 4)))
    expert_down_bias = normal_values(splits[9], (EXPERTS, D), 0.2, 1.0, ((0, 8), (1, 4)))
    routes_keys = jax.random.split(jax.random.fold_in(splits[10], 1), TOKENS // (IMG * SEQ))
    routes_turns = jax.random.permutation(jax.random.fold_in(splits[10], 3), TOKENS // (IMG * SEQ))
    routes = jax.vmap(lambda own, number: deal_out(jax.random.fold_in(splits[10], 2), own, number, IMG * SEQ, EXPERTS, 2, CAP, 0))(routes_keys, routes_turns).reshape((TOKENS, 2))
    cotangent = bell_draw_with(splits[11], (TOKENS, D), 1.0, 6.0, ((0, 32),), (0, 1, 32, 2.75))
    return {"tokens": tokens, "norm_gains": norm_gains, "shifts": shifts, "attn_weight": attn_weight, "out_weight": out_weight, "router_weight": router_weight, "expert_in": expert_in, "expert_in_bias": expert_in_bias, "expert_down": expert_down, "expert_down_bias": expert_down_bias, "routes": routes, "cotangent": cotangent}


@jax.custom_vjp
def low(v):
    return lax.optimization_barrier(v.astype(jnp.bfloat16)).astype(jnp.float32)

@jax.custom_vjp
def low_back(v):
    return v

def low_keep(v):
    return (low(v), None)

def low_pass(kept, grad):
    return (grad,)

def back_keep(v):
    return (v, None)

def back_low(kept, grad):
    return (low(grad),)
low.defvjp(low_keep, low_pass)
low_back.defvjp(back_keep, back_low)
highest = lax.Precision.HIGHEST

def product(left, right):
    return jnp.dot(left, right, precision=highest)

def normalize(inputs, gain, shift):
    average = lax.optimization_barrier(jnp.mean(inputs, axis=-1, keepdims=True))
    centered = inputs - average
    variance = lax.optimization_barrier(jnp.mean(centered * centered, axis=-1, keepdims=True))
    return centered * lax.rsqrt(variance + 1e-06) * gain + shift

def slot_places(routes_group):
    flattened = routes_group.reshape(-1).astype(jnp.int32)
    onehot = (flattened[:, None] == jnp.arange(EXPERTS, dtype=jnp.int32)[None, :]).astype(jnp.int32)
    before = (jnp.cumsum(onehot, axis=0, dtype=jnp.int32) - onehot).astype(jnp.int32)
    places = lax.optimization_barrier(jnp.sum(before * onehot, axis=1, dtype=jnp.int32))
    return (flattened * CAP + places).astype(jnp.int32)

def group_forward(inputs, routes_group, parameters):
    gain_rows, shift_rows, attn_w, out_w, router_w, first_w, first_b, second_w, second_b = parameters
    row_count = inputs.shape[0]
    is_valid = (jnp.arange(row_count) % SEQ < VALID).astype(jnp.float32)
    normed = low(normalize(inputs, gain_rows[0], shift_rows[0]))
    queries = low_back(low(product(normed, attn_w[0]) + shift_rows[1]))
    key_rows = low_back(low(product(normed, attn_w[1])))
    value_rows = low_back(low(product(normed, attn_w[2]) + shift_rows[2]))
    split_shape = (row_count // SEQ, SEQ, HEADS, HD)
    scores = jnp.einsum('bqhd,bkhd->bhqk', queries.reshape(split_shape), key_rows.reshape(split_shape), precision=highest)
    scores = low_back(scores * HD ** (-0.5))
    key_valid = jnp.arange(SEQ) < VALID
    scores = jnp.where(key_valid[None, None, None, :], scores, -1000000000.0)
    attention = low(jax.nn.softmax(scores, axis=-1))
    mixed_heads = jnp.einsum('bhqk,bkhd->bqhd', attention, value_rows.reshape(split_shape), precision=highest)
    mixed_heads = low_back(low(mixed_heads.reshape(row_count, D)))
    branch = low_back(product(mixed_heads, out_w))
    residual = inputs + branch + shift_rows[3]
    normed_two = low(normalize(residual, gain_rows[1], shift_rows[4]))
    logits = low_back(product(normed_two, router_w.T))
    chosen = jnp.take_along_axis(logits, routes_group, axis=1)
    weight = jax.nn.softmax(chosen, axis=1) * is_valid[:, None]
    places = slot_places(routes_group)
    owners = (jnp.arange(2 * row_count, dtype=jnp.int32) // 2).astype(jnp.int32)
    slot_token = jnp.zeros((EXPERTS * CAP,), jnp.int32).at[places].set(owners)
    slot_weight = jnp.zeros((EXPERTS * CAP,), jnp.float32).at[places].set(weight.reshape(-1))
    dispatched = normed_two[slot_token].reshape(EXPERTS, CAP, D)
    pre_act = low_back(jnp.einsum('ecd,edf->ecf', dispatched, first_w, precision=highest) + first_b[:, None, :])
    hidden = low(jax.nn.gelu(pre_act, approximate=False))
    result = low_back(jnp.einsum('ecf,edf->ecd', hidden, second_w, precision=highest) + second_b[:, None, :])
    combined = jnp.zeros((row_count, D), jnp.float32).at[slot_token].add(slot_weight[:, None] * result.reshape(-1, D))
    return residual + low_back(combined)

def reference(tokens, norm_gains, shifts, attn_weight, out_weight, router_weight, expert_in, expert_in_bias, expert_down, expert_down_bias, routes, cotangent):
    parameters = tuple((weight_in.astype(jnp.float32) for weight_in in (norm_gains, shifts, attn_weight, out_weight, router_weight, expert_in, expert_in_bias, expert_down, expert_down_bias)))
    group_count = tokens.shape[0] // (IMG * SEQ)
    inputs_all = tokens.astype(jnp.float32).reshape(group_count, IMG * SEQ, D)
    routes_all = routes.reshape(group_count, IMG * SEQ, 2)

    def forward(inputs_in, weights_in):

        def group_step(group_pair):
            return group_forward(group_pair[0], group_pair[1], weights_in)
        return lax.map(jax.checkpoint(group_step), (inputs_in, routes_all))
    output, pullback = jax.vjp(forward, inputs_all, parameters)
    grad_inputs, gradients = pullback(cotangent.astype(jnp.float32).reshape(group_count, IMG * SEQ, D))
    return (output.reshape(-1, D).astype(jnp.bfloat16), grad_inputs.reshape(-1, D), gradients[0], gradients[1], gradients[2], gradients[3], gradients[4], gradients[5], gradients[6], gradients[7], gradients[8])
```

```python
import functools

import jax
import jax.numpy as jnp
from jax import lax
from jax.experimental import pallas as pl
from jax.experimental.pallas import tpu as pltpu
from jax.sharding import PartitionSpec as P

D = 768
FF = 3072
HD = 64
SEQ = 200
VALID = 197
GROUP = 192
SLOTS = (608, 384)
WINDOW = 224
NARROW = 96
EPSILON = 1e-06
MASKED = -1000000000.0
F32 = jnp.float32
BF16 = jnp.bfloat16
VALID_LANE = 64
MIB = 1 << 20


def params(megabytes, sizes=None):
    semantics = None if sizes is None else ("arbitrary",) * sizes
    return pltpu.CompilerParams(
        vmem_limit_bytes=megabytes * MIB, dimension_semantics=semantics
    )


def cost(flops, moved, slow=0):
    return pl.CostEstimate(flops=int(flops), bytes_accessed=int(moved), transcendentals=int(slow))


def dot(left, right):
    return jnp.dot(left, right, preferred_element_type=F32)


def dot_nt(left, right):
    return lax.dot_general(left, right, (((1,), (1,)), ((), ())), preferred_element_type=F32)


def dot_tn(left, right):
    return lax.dot_general(left, right, (((0,), (0,)), ((), ())), preferred_element_type=F32)


def standardize(inputs):
    average = jnp.mean(inputs, axis=-1, keepdims=True)
    centered = inputs - average
    inverse = lax.rsqrt(jnp.mean(centered * centered, axis=-1, keepdims=True) + EPSILON)
    return centered * inverse, inverse


def norm_back(upstream, scaled, inverse, gain):
    grad_hat = upstream * gain
    mean_grad = jnp.mean(grad_hat, axis=-1, keepdims=True)
    mean_cross = jnp.mean(grad_hat * scaled, axis=-1, keepdims=True)
    return inverse * (grad_hat - mean_grad - scaled * mean_cross)


class Ring:
    def __init__(self, count):
        self.count = count
        self.half = count // 2
        self.order = list(range(0, count, 2)) + list(range(count - 1, 0, -2))
        self.ahead = [(self.order[i], self.order[(i + 1) % count]) for i in range(count)]
        self.behind = [(self.order[i], self.order[i - 1]) for i in range(count)]

    def sources(self):
        me = lax.axis_index("wide")
        place = jnp.where(me % 2 == 0, me // 2, self.count - 1 - me // 2)

        def at(position):
            position = position % self.count
            return jnp.where(
                position < self.half, 2 * position, 2 * (self.count - 1 - position) + 1
            )

        found = [at(place)]
        for step in range(1, self.half):
            found += [at(place - step), at(place + step)]
        return jnp.stack(found + [at(place + self.half)]).astype(jnp.int32)

    def forward(self, block):
        return lax.ppermute(block, "wide", self.ahead)

    def backward(self, block):
        return lax.ppermute(block, "wide", self.behind)

    def gather(self, block, cut):
        found = [block]
        left = right = block
        for _ in range(1, self.half):
            left, right = self.forward(left), self.backward(right)
            found += [left, right]
        return found, (self.forward(left[:cut]), self.backward(right[cut:]))

    def scatter_first(self, last, cut):
        return self.backward(last[:cut]), self.forward(last[cut:])

    def scatter_next(self, pair):
        return self.backward(pair[0]), self.forward(pair[1])


def to_core(block):
    return lax.ppermute(block, "tp", [(i, i ^ 1) for i in range(4)])


def to_x(block):
    return lax.ppermute(block, "tp", [(i, i ^ 2) for i in range(4)])


def assemble_kernel(count, rows, cut, source_ref, *refs):
    blocks, first, second, weights, small = (
        refs[: count - 1],
        refs[count - 1],
        refs[count],
        refs[count + 1],
        refs[count + 2],
    )
    for i in range(count - 1):
        weights[source_ref[i]] = blocks[i][0:rows]
        small[source_ref[i]] = blocks[i][rows:]
    last = source_ref[count - 1]
    weights[last, 0:cut] = first[...]
    if rows > cut:
        weights[last, cut:rows] = second[0 : rows - cut]
    small[last] = second[rows - cut :]


def attend_kernel(index, tokens, norms, bias, *refs):
    weights = refs[:4]
    normed_ref, qkv_ref, mixed_ref, sums_ref, residual_ref, second_ref = refs[-6:]
    inputs = tokens[index].astype(F32)
    scaled, _ = standardize(inputs)
    normed = (scaled * norms[0:1] + norms[2:3]).astype(BF16)
    normed_ref[...] = normed
    residual = inputs + norms[5:6]
    lane = lax.broadcasted_iota(jnp.int32, (SEQ, 128), 1)
    key_valid = lax.broadcasted_iota(jnp.int32, (SEQ, SEQ), 1) < VALID
    sums = jnp.zeros((SEQ, 128), F32)
    for j in range(4):
        projected = (dot(normed, weights[j][...]) + bias[j : j + 1]).astype(BF16)
        qkv_ref[j] = projected
        mixed = [jnp.zeros((SEQ, HD), BF16)]
        for h in range(3):
            query = projected[:, HD * h : HD * (h + 1)]
            key_rows = projected[:, GROUP + HD * h : GROUP + HD * (h + 1)]
            value = projected[:, 2 * GROUP + HD * h : 2 * GROUP + HD * (h + 1)]
            scores = jnp.where(key_valid, dot_nt(query, key_rows) * HD ** (-0.5), MASKED)
            row_max = jnp.max(scores, axis=-1, keepdims=True)
            exponent = jnp.exp(scores - row_max)
            row_sum = jnp.sum(exponent, axis=-1, keepdims=True)
            attention = (exponent / row_sum).astype(BF16)
            mixed.append(dot(attention, value).astype(BF16))
            sums = jnp.where(lane == 3 * j + h, row_max + jnp.log(row_sum), sums)
        mixed = jnp.concatenate(mixed, axis=1)
        mixed_ref[j] = mixed
        residual = residual + dot_nt(mixed, weights[j][:, D - 256 :])
    sums_ref[...] = sums
    residual_ref[...] = residual
    scaled_two, _ = standardize(residual)
    second = (scaled_two * norms[1:2] + norms[6:7]).astype(BF16)
    if index:
        second_ref[0] = refs[4][...]
        second_ref[1] = second
    else:
        second_ref[...] = second


def attend_back_kernel(
    index, tokens, cotangent, mine, left, right, residual, sums_ref, norms, *refs
):
    weights = refs[:4]
    qkv_ref, input_grad, branch_ref, grads_ref, small_ref, bias_ref = refs[4:]
    grad_two = mine[index].astype(F32) + left[index].astype(F32) + right[index].astype(F32)
    scaled_two, inverse_two = standardize(residual[...])
    grad_mid = cotangent[index].astype(F32) + norm_back(
        grad_two, scaled_two, inverse_two, norms[1:2]
    )
    branch = grad_mid.astype(BF16)
    branch_ref[...] = branch
    key_valid = lax.broadcasted_iota(jnp.int32, (SEQ, SEQ), 1) < VALID
    grad_one = jnp.zeros((SEQ, D), F32)
    scale = HD ** (-0.5)
    for j in range(4):
        upstream = dot(branch, weights[j][:, D - 256 :]).astype(BF16)
        grads = [[], [], []]
        for h in range(3):
            query = qkv_ref[j, :, HD * h : HD * (h + 1)]
            key_rows = qkv_ref[j, :, GROUP + HD * h : GROUP + HD * (h + 1)]
            value = qkv_ref[j, :, 2 * GROUP + HD * h : 2 * GROUP + HD * (h + 1)]
            up = upstream[:, HD * (h + 1) : HD * (h + 2)]
            scores = jnp.where(key_valid, dot_nt(query, key_rows) * scale, MASKED)
            attention = jnp.exp(scores - sums_ref[:, 3 * j + h : 3 * j + h + 1])
            grad_attn = dot_nt(up, value)
            inner = jnp.sum(attention * grad_attn, axis=-1, keepdims=True)
            grad_scores = (attention * (grad_attn - inner)).astype(BF16)
            grads[0].append((dot(grad_scores, key_rows) * scale).astype(BF16))
            grads[1].append((dot_tn(grad_scores, query) * scale).astype(BF16))
            grads[2].append(dot_tn(attention.astype(BF16), up).astype(BF16))
        whole = jnp.concatenate(
            grads[0] + grads[1] + grads[2] + [jnp.zeros((SEQ, GROUP), BF16)], axis=1
        )
        grads_ref[j] = whole
        bias_ref[j : j + 1] = jnp.sum(whole.astype(F32), axis=0, keepdims=True)
        grad_one = grad_one + dot_nt(whole, weights[j][...])
    scaled_one, inverse_one = standardize(tokens[index].astype(F32))
    input_grad[...] = grad_mid + norm_back(grad_one, scaled_one, inverse_one, norms[0:1])
    small_ref[...] = jnp.concatenate(
        [
            jnp.sum(part, axis=0, keepdims=True)
            for part in (
                grad_one * scaled_one,
                grad_two * scaled_two,
                grad_one,
                grad_mid,
                grad_two,
            )
        ]
        + [jnp.zeros((3, D), F32)],
        axis=0,
    )


def weight_grad_kernel(groups, places, rows, sources, *refs):
    normed, grads, branch, mixed = refs[0:2], refs[2:4], refs[4:6], refs[6:8]
    outs, whole = refs[8:-1], refs[-1]
    for out, j in zip(outs, groups):
        whole[...] = dot_tn(normed[0][...], grads[0][j]) + dot_tn(normed[1][...], grads[1][j])
        whole[:, D - 256 :] += dot_tn(branch[0][...], mixed[0][j]) + dot_tn(
            branch[1][...], mixed[1][j]
        )
        for i, place in enumerate(places):
            start = pl.multiple_of(sources[place] * rows, 8)
            block = whole[pl.ds(start, rows)]
            missing = out.shape[1] - rows
            if missing:
                block = jnp.concatenate([block, jnp.zeros((missing, D), F32)], axis=0)
            out[i] = block.astype(BF16)


def pick_kernel(plan, slots, size_ref, offset_ref, places_ref, *refs):
    outs = refs[-len(plan) :]

    def clear(tile, carry):
        start = pl.multiple_of(tile * slots, 16)
        for out in outs:
            out[pl.ds(start, slots)] = jnp.zeros((slots, out.shape[1]), BF16)
        return carry

    lax.fori_loop(0, tiles_of(size_ref[0], slots), clear, 0)

    def some(i, base, height):
        slot = lax.broadcasted_iota(jnp.int32, (height, SEQ), 0) + base
        chosen = (places_ref[i : i + 1] == slot).astype(F32).astype(BF16)
        for out, stream in zip(outs, plan):
            which, index = stream[i]
            window = out.at[pl.ds(base, height)]
            window[...] += dot(chosen, refs[which][index]).astype(BF16)

    count = len(plan[0])
    for i in range(count):
        base = pl.multiple_of(offset_ref[i] // 16 * 16, 16)
        some(i, base, NARROW)
        pl.when(offset_ref[i + 1] > base + NARROW)(
            functools.partial(some, i, pl.multiple_of(base + NARROW, 16), WINDOW - NARROW)
        )


def unpick_kernel(size_ref, offset_ref, places_ref, slots_ref, *outs):
    def some(i, base, height):
        slot = lax.broadcasted_iota(jnp.int32, (height, SEQ), 0) + base
        chosen = (places_ref[i : i + 1] == slot).astype(F32).astype(BF16)
        row = lax.broadcasted_iota(jnp.int32, (height, D), 0) + base
        window = slots_ref[pl.ds(base, height)]
        window = jnp.where(row < size_ref[0], window, jnp.zeros_like(window))
        return dot_tn(chosen, window).astype(BF16)

    for i in range(2 * len(outs)):
        out = outs[i // 2].at[i % 2]
        base = pl.multiple_of(offset_ref[i] // 16 * 16, 16)
        out[...] = some(i, base, NARROW)

        @pl.when(offset_ref[i + 1] > base + NARROW)
        def _(i=i, out=out, base=base):
            more = pl.multiple_of(base + NARROW, 16)
            out[...] += some(i, more, WINDOW - NARROW)


def tiles_of(size, slots):
    return jnp.maximum(1, (size + slots - 1) // slots)


def moved(semaphores, *pairs):
    copies = [
        pltpu.make_async_copy(source, target, semaphores.at[i])
        for i, (source, target) in enumerate(pairs)
    ]
    for copy in copies:
        copy.start()
    for copy in copies:
        copy.wait()


def weight_block(which):
    return pl.BlockSpec((None, D, D), lambda f: (f, which, 0))


def expert_kernel(
    size, rows_hbm, grads_hbm, chosen_hbm, weights_hbm, second_bias, router,
    hidden_hbm, pre_hbm, gates_hbm, back_hbm, router_ref, bias_ref,
    rows, grads, chosen, gates, total, semaphores,
):
    slots = rows.shape[0]
    router_ref[...] = jnp.zeros_like(router_ref)
    bias_ref[...] = jnp.zeros_like(bias_ref)

    def tile(m, carry):
        at = pl.ds(pl.multiple_of(m * slots, 16), slots)
        moved(
            semaphores,
            (rows_hbm.at[at], rows),
            (grads_hbm.at[at], grads),
            (chosen_hbm.at[at], chosen),
        )
        lane = lax.broadcasted_iota(jnp.int32, (slots, 128), 1)
        signs = jnp.where(lane < VALID_LANE, chosen[...].astype(F32), 0.0)
        is_valid = chosen[:, VALID_LANE : VALID_LANE + 1].astype(F32)
        gap = jnp.sum(dot_nt(rows[...], router[...]) * signs, axis=1, keepdims=True)
        weight = is_valid / (1.0 + jnp.exp(-gap))
        slope = weight / (1.0 + jnp.exp(gap))
        direct = jnp.sum(grads[...].astype(F32) * second_bias[0:1], axis=1, keepdims=True)
        gates[...] = jnp.where(lane == 0, weight, jnp.where(lane == 1, slope, direct))
        total[...] = jnp.zeros_like(total)

        def step(first, second, first_bias, hidden_ref, pre_ref):
            pre = dot(rows[...], first[...]) + first_bias[0:1].astype(F32)
            back = dot(grads[...], second[...])
            below = 0.5 * (1.0 + lax.erf(pre * 0.5**0.5))
            density = jnp.exp(-0.5 * pre * pre) * (0.5 / 3.141592653589793) ** 0.5
            hidden = pre * below
            weight = gates[:, 0:1]
            added = jnp.sum(hidden * back, axis=1, keepdims=True)
            slope_pre = (weight * back * (below + pre * density)).astype(BF16)
            hidden_ref[...] = (weight * hidden).astype(BF16)
            pre_ref[...] = slope_pre
            gates[...] += jnp.where(lane == 2, added, 0.0)
            total[...] += dot_nt(slope_pre, first[...])

        part = pl.BlockSpec((slots, D), lambda f: (m, f))
        pltpu.emit_pipeline(
            step,
            grid=(FF // D,),
            in_specs=[
                weight_block(0),
                weight_block(1),
                pl.BlockSpec((None, 16, D), lambda f: (f, 2 * D // 16, 0)),
            ],
            out_specs=[part, part],
        )(weights_hbm, weights_hbm, weights_hbm, hidden_hbm, pre_hbm)
        logits_grad = (signs * gates[:, 1:2] * gates[:, 2:3]).astype(BF16)
        router_ref[...] += dot_tn(logits_grad, rows[...])
        bias_ref[0:1] += jnp.sum(weight * grads[...].astype(F32), axis=0, keepdims=True)
        rows[...] = (total[...] + dot(logits_grad, router[...])).astype(BF16)
        moved(semaphores, (rows, back_hbm.at[at]), (gates, gates_hbm.at[at]))
        return carry

    lax.fori_loop(0, tiles_of(size[0], slots), tile, 0)


def expert_rest_kernel(earlier, size, *refs):
    rows_hbm, grads_hbm, hidden_hbm, pre_hbm, gates_hbm, weights_hbm, second_bias = refs[:7]
    grad_hbm, result_hbm, rows, grads, gates, total, semaphores = refs[7 + earlier :]
    slots = rows.shape[0]

    def tile(m, carry):
        at = pl.ds(pl.multiple_of(m * slots, 16), slots)
        moved(
            semaphores,
            (rows_hbm.at[at], rows),
            (grads_hbm.at[at], grads),
            (gates_hbm.at[at], gates),
        )
        total[...] = gates[:, 0:1] * second_bias[0:1]

        def step(second, hidden, pre, *rest):
            out = rest[-1]
            total[...] += dot_nt(hidden[...], second[...])
            one = dot_tn(rows[...], pre[...])
            two = dot_tn(grads[...], hidden[...])
            sums = jnp.sum(pre[...].astype(F32), axis=0, keepdims=True)
            if len(rest) > 1:
                one = one + rest[0][0:D].astype(F32)
                two = two + rest[0][D : 2 * D].astype(F32)
                sums = sums + rest[0][2 * D : 2 * D + 1].astype(F32)
            out[0:D] = one.astype(BF16)
            out[D : 2 * D] = two.astype(BF16)
            out[2 * D :] = jnp.broadcast_to(sums, (16, D)).astype(BF16)

        def run(adds):
            part = pl.BlockSpec((slots, D), lambda f: (m, f))
            whole = pl.BlockSpec((None, 2 * D + 16, D), lambda f: (f, 0, 0))
            pltpu.emit_pipeline(
                step,
                grid=(FF // D,),
                in_specs=[weight_block(1), part, part] + [whole] * adds,
                out_specs=[whole],
            )(weights_hbm, hidden_hbm, pre_hbm, *[grad_hbm] * adds, grad_hbm)

        if earlier:
            run(True)
        else:
            pl.when(m == 0)(functools.partial(run, False))
            pl.when(m > 0)(functools.partial(run, True))
        rows[...] = total[...].astype(BF16)
        moved(semaphores, (rows, result_hbm.at[at]))
        return carry

    lax.fori_loop(0, tiles_of(size[0], slots), tile, 0)


def pack_kernel(first, second, small, out):
    out[0:D] = first[0]
    out[D : 2 * D] = second[0]
    out[2 * D :] = small[...]


def ring_add_kernel(is_first, mine_left, left, mine_right, right, out_left, out_right):
    def sums(one, other):
        return (one.astype(F32) + other.astype(F32)).astype(BF16)

    if is_first:
        out_left[0] = sums(mine_left[0], left[0])
        out_left[1] = mine_left[1]
        out_right[0] = mine_right[0]
        out_right[1] = sums(mine_right[1], right[0])
    else:
        out_left[...] = sums(mine_left[...], left[...])
        out_right[...] = sums(mine_right[...], right[...])


def sum_parts_kernel(one, other, *outs):
    start = 0
    for out in outs:
        part = slice(start, start + out.shape[0])
        out[...] = (one[part].astype(F32) + other[part].astype(F32)).astype(BF16)
        start += out.shape[0]


def tail_kernel(cut, entries, sources, small, *refs):
    outs = refs[-len(entries) :]
    refs = list(refs[: -len(entries)])
    near, far = refs.pop(0), refs.pop(0)
    rows = near.shape[1]
    for (place, index, kind), out in zip(entries, outs):
        whole = jnp.concatenate(
            [
                near[index].astype(F32) + far[index].astype(F32),
                small[sources[place]].astype(F32),
            ],
            axis=0,
        )
        if kind == "none":
            out[...] = whole.astype(out.dtype)
        elif kind == "low":
            out[0:cut] = (whole[0:cut] + refs.pop(0)[...].astype(F32)).astype(BF16)
            out[cut:] = whole[cut:].astype(BF16)
        elif kind == "high":
            out[0:cut] = whole[0:cut].astype(BF16)
            out[cut:] = (whole[cut:] + refs.pop(0)[...].astype(F32)).astype(BF16)
        elif kind == "full":
            out[...] = (whole + refs.pop(0)[...].astype(F32)).astype(BF16)
        else:
            left, right = refs.pop(0), refs.pop(0)
            out[...] = whole + left[...].astype(F32) + right[...].astype(F32)


def nothing_kernel(*refs):
    pass


SMEM = pl.BlockSpec(memory_space=pltpu.SMEM)
VMEM = pl.BlockSpec(memory_space=pltpu.VMEM)
ANY = pl.BlockSpec(memory_space=pl.ANY)


def shape(dims, kind=BF16):
    return jax.ShapeDtypeStruct(dims, kind)


def call(kernel, operands, specs, out_shape, out_specs, earlier=(), **settings):
    size = len(operands)
    waits = len(earlier)

    def stripped(*refs):
        kernel(*refs[:size], *refs[size + waits :])

    megabytes = settings.pop("megabytes", 32)
    work = settings.pop("work", (1e6, 1e6))
    return pl.pallas_call(
        stripped,
        in_specs=list(specs) + [ANY] * waits,
        out_specs=out_specs,
        out_shape=out_shape,
        compiler_params=params(megabytes),
        cost_estimate=cost(*work),
        **settings,
    )(*operands, *earlier)


def assemble(blocks, parts, sources, rows, cut):
    count = len(blocks) + 1
    tall = blocks[0].shape[0]
    return call(
        functools.partial(assemble_kernel, count, rows, cut),
        [sources, *blocks, *parts],
        [SMEM] + [VMEM] * (count + 1),
        [shape((count, rows, D)), shape((count, tall - rows, D))],
        [VMEM, VMEM],
        megabytes=16,
    )


def attend(tokens, index, norms, bias, weights, earlier, other=None):
    more = [] if other is None else [other]
    return call(
        functools.partial(attend_kernel, index),
        [tokens, norms, bias, *weights, *more],
        [VMEM] * (7 + len(more)),
        [
            shape((SEQ, D)),
            shape((4, SEQ, D)),
            shape((4, SEQ, 256)),
            shape((SEQ, 128), F32),
            shape((SEQ, D), F32),
            shape((2, SEQ, D) if more else (SEQ, D)),
        ],
        [VMEM] * 6,
        earlier,
        work=(6e9, 9e6),
    )


def attend_back(
    tokens, cotangent, index, parts, residual, sums, norms, weights, qkv, earlier
):
    return call(
        functools.partial(attend_back_kernel, index),
        [tokens, cotangent, *parts, residual, sums, norms, *weights, qkv],
        [VMEM] * 13,
        [
            shape((SEQ, D), F32),
            shape((SEQ, D)),
            shape((4, SEQ, D)),
            shape((8, D), F32),
            shape((4, D), F32),
        ],
        [VMEM] * 5,
        earlier,
        work=(8e9, 9e6),
    )


def weight_grads(normed, grads, branch, mixed, groups, places, sources, rows, rows_up, earlier):
    return call(
        functools.partial(weight_grad_kernel, groups, places, rows),
        [sources, *normed, *grads, *branch, *mixed],
        [SMEM] + [VMEM] * 8,
        [shape((len(places), rows_up, D))] * len(groups),
        [VMEM] * len(groups),
        earlier,
        scratch_shapes=[pltpu.VMEM((D, D), F32)],
        work=(2e9, 5e6),
    )


def sum_parts(one, other, sizes):
    return call(
        sum_parts_kernel,
        [one, other],
        [VMEM] * 2,
        [shape((size,) + one.shape[1:]) for size in sizes],
        [VMEM] * len(sizes),
    )


def tail(entries, sources, small, near, far, received, cut, kind=BF16):
    tall = near.shape[1] + small.shape[1]
    return call(
        functools.partial(tail_kernel, cut, entries),
        [sources, small, near, far, *received],
        [SMEM] + [VMEM] * (3 + len(received)),
        [shape((tall, D), kind)] * len(entries),
        [VMEM] * len(entries),
    )


def pick(size, offsets, places, sources, plan, widths, slots, most, earlier=()):
    return call(
        functools.partial(pick_kernel, plan, slots),
        [size, offsets, places, *sources],
        [SMEM, SMEM, VMEM] + [VMEM] * len(sources),
        [shape((most, width)) for width in widths],
        [VMEM] * len(widths),
        earlier,
        megabytes=48,
        work=(3e9, 6e6),
    )


def unpick(size, offsets, places, slots, earlier=()):
    count = places.shape[0] // 2
    return call(
        unpick_kernel,
        [size, offsets, places, slots],
        [SMEM, SMEM, VMEM, VMEM],
        [shape((2, SEQ, D))] * count,
        [VMEM] * count,
        earlier,
        megabytes=48,
        work=(3e9, 6e6),
    )


def expert(size, rows, grads, chosen, weights, second_bias, router, slots, earlier=()):
    most = rows.shape[0]
    return call(
        expert_kernel,
        [size, rows, grads, chosen, weights, second_bias, router],
        [SMEM, ANY, ANY, ANY, ANY, VMEM, VMEM],
        [
            shape((most, FF)),
            shape((most, FF)),
            shape((most, 128), F32),
            shape((most, D)),
            shape((128, D), F32),
            shape((8, D), F32),
        ],
        [ANY] * 4 + [VMEM] * 2,
        earlier,
        scratch_shapes=[
            pltpu.VMEM((slots, D), BF16),
            pltpu.VMEM((slots, D), BF16),
            pltpu.VMEM((slots, 128), BF16),
            pltpu.VMEM((slots, 128), F32),
            pltpu.VMEM((slots, D), F32),
            pltpu.SemaphoreType.DMA((3,)),
        ],
        megabytes=48,
        work=(1.4e10, 2e7),
    )


def expert_rest(size, side, weights, second_bias, slots, grad=None, earlier=()):
    most = side[0].shape[0]
    more = [] if grad is None else [grad]
    return call(
        functools.partial(expert_rest_kernel, len(more)),
        [size, *side, weights, second_bias, *more],
        [SMEM] + [ANY] * 6 + [VMEM] + [ANY] * len(more),
        [shape((4, 2 * D + 16, D)), shape((most, D))],
        [ANY, ANY],
        earlier,
        input_output_aliases={8: 0} if more else {},
        scratch_shapes=[
            pltpu.VMEM((slots, D), BF16),
            pltpu.VMEM((slots, D), BF16),
            pltpu.VMEM((slots, 128), F32),
            pltpu.VMEM((slots, D), F32),
            pltpu.SemaphoreType.DMA((3,)),
        ],
        megabytes=48,
        work=(1.4e10, 3e7),
    )


def pack(first, second, small, earlier):
    return call(
        pack_kernel,
        [first, second, small],
        [VMEM] * 3,
        shape((2 * D + 16, D)),
        VMEM,
        earlier,
    )


def ring_add(blocks, received, is_first, earlier=()):
    return call(
        functools.partial(ring_add_kernel, is_first),
        [blocks[0], received[0], blocks[1], received[1]],
        [VMEM] * 4,
        [shape(blocks[0].shape)] * 2,
        [VMEM] * 2,
        earlier,
    )


def after(value, *earlier):
    return call(
        nothing_kernel,
        [value],
        [ANY],
        shape(value.shape, value.dtype),
        ANY,
        earlier,
        input_output_aliases={0: 0},
        work=(0, 0),
    )


def body(
    count,
    tokens,
    norm_gains,
    shifts,
    attn_weight,
    out_weight,
    router_weight,
    expert_in,
    expert_in_bias,
    expert_down,
    expert_down_bias,
    routes,
    cotangent,
):
    ring = Ring(count)
    sources = ring.sources()
    wide, tp = lax.axis_index("wide"), lax.axis_index("tp")
    core, far = tp % 2, tp // 2
    rows = D // count
    rows_up = -(-rows // 16) * 16
    experts = router_weight.shape[0]
    group_rows = routes.shape[0]
    local_rows = tokens.shape[0]
    capacity = (10 * group_rows // (4 * experts) + 7) // 8 * 8
    near_steps = max(1, 5 * ring.half // 8)
    near_groups = 1 + 2 * near_steps
    sides = ((0, near_groups), (near_groups, count))
    most = [
        -(-(stop - start) * min(local_rows, capacity) // slots) * slots + WINDOW
        for (start, stop), slots in zip(sides, SLOTS)
    ]
    smalls = 7 + experts
    columns = D // count

    small = jnp.concatenate([norm_gains, shifts, router_weight], axis=0)
    near = to_core(small)
    small = jnp.where(
        core == 0,
        jnp.concatenate([small, near], axis=1),
        jnp.concatenate([near, small], axis=1),
    )
    near = to_x(small)
    small = jnp.where(
        far == 0,
        jnp.concatenate([small, near], axis=1),
        jnp.concatenate([near, small], axis=1),
    )
    small = jnp.pad(small.reshape(-1), (0, 2 * D - smalls * columns)).reshape(2, D)
    own_routes = lax.dynamic_slice_in_dim(routes, tp * local_rows, local_rows, 0)
    own_routes = jnp.pad(own_routes.T.astype(BF16), ((0, 0), (0, D - local_rows)))
    square = jnp.concatenate(
        [attn_weight[0], attn_weight[1], attn_weight[2], out_weight.T], axis=1
    )
    block = jnp.concatenate(
        [
            jnp.pad(square, ((0, rows_up - rows), (0, 0))),
            small,
            own_routes,
            jnp.zeros((12, D), BF16),
        ],
        axis=0,
    )
    tall = block.shape[0]
    cut = (tall // 2 + 15) // 16 * 16
    blocks, ends = ring.gather(block, cut)
    own, gathered_small = assemble(blocks, ends, sources, rows_up, cut)
    own = own[:, :rows].reshape(D, D)
    beside, across = to_core(own), to_x(own)
    opposite = to_core(across)
    weights = (own, beside, across, opposite)

    norms = (
        gathered_small[:, 0:2]
        .reshape(count, 2 * D)[:, : smalls * columns]
        .reshape(count, smalls, columns)
        .transpose(1, 0, 2)
        .reshape(smalls, D)
        .astype(F32)
    )
    router = jnp.pad(norms[7:].astype(BF16), ((0, 128 - experts), (0, 0)))

    def relative(values):
        values = values.reshape(2, 2, GROUP)
        values = jnp.where(far == 0, values, values[::-1])
        return jnp.where(core == 0, values, values[:, ::-1]).reshape(4, GROUP)

    nothing = jnp.zeros((4, GROUP), F32)
    bias = jnp.concatenate([relative(norms[3]), nothing, relative(norms[4]), nothing], axis=1)

    expert_block = jnp.concatenate(
        [
            expert_in_bias,
            jnp.pad(expert_down_bias, ((0, 0), (0, D - GROUP))),
            jnp.zeros((14, D), BF16),
        ],
        axis=0,
    )
    expert_block = pack(expert_in, expert_down, expert_block, [across])
    expert_all = lax.all_gather(expert_block, "tp", axis=0, tiled=True).reshape(4, -1, D)
    second_bias = jnp.broadcast_to(
        expert_all[:, 2 * D + 1, :GROUP].reshape(1, D).astype(F32), (8, D)
    )

    named = jnp.stack(
        [b[rows_up + 2 : rows_up + 4, :local_rows] for b in blocks]
        + [ends[1][rows_up + 2 - cut : rows_up + 4 - cut, :local_rows]]
    ).astype(F32)
    named = named.reshape(count, 2, 2, SEQ).transpose(1, 0, 2, 3).reshape(2, 2 * count, SEQ)
    mine = wide.astype(F32)
    is_first, is_second = named[0] == mine, named[1] == mine
    is_chosen = (is_first | is_second).astype(F32)
    other = jnp.where(is_first, named[1], named[0])
    lower = (jnp.arange(SEQ)[:, None] < jnp.arange(SEQ)[None, :]).astype(F32)
    rank = jnp.dot(is_chosen, lower)
    counts = jnp.sum(is_chosen, axis=-1)
    lane = jnp.arange(128).astype(F32)
    signs = (lane == mine).astype(F32) - (lane == other[..., None]).astype(F32)
    is_valid = (jnp.arange(SEQ) < VALID).astype(F32)
    signs = jnp.where(lane == VALID_LANE, is_valid[None, :, None], signs).astype(BF16)
    tables = []
    for start, stop in sides:
        part = slice(2 * start, 2 * stop)
        size = 2 * (stop - start)
        lower = jnp.arange(size)[:, None] < jnp.arange(size + 1)[None, :]
        offsets = jnp.sum(counts[part, None] * lower, axis=0)
        places = jnp.where(is_chosen[part] > 0, offsets[:size, None] + rank[part], -1.0)
        tables.append((
            offsets[size:].astype(jnp.int32), offsets.astype(jnp.int32), places.astype(jnp.int32)
        ))

    tokens = tokens.reshape(2, SEQ, D)
    cotangent = after(cotangent.reshape(2, SEQ, D), *ends)
    grad_blocks, grad_ends = ring.gather(cotangent, 1)
    first = attend(tokens, 0, norms, bias, weights, grad_blocks[3:5])
    second = attend(tokens, 1, norms, bias, weights, grad_blocks[-2:], first[5])
    forward = (first, second)

    def picked(side, blocks, last, widths, extra, earlier):
        start, stop = sides[side]
        groups = range(start, min(stop, count - 1))
        sources_ = [blocks[g] for g in groups]
        images = [(3 + i, index) for i in range(len(groups)) for index in range(2)]
        if stop == count:
            images += [(3 + len(groups), 0), (4 + len(groups), 0)]
            sources_ += list(last)
        plan = [[(which - 3, index) for which, index in images]]
        if extra is not None:
            plan.append([(len(sources_), 2 * start + i) for i in range(len(images))])
            sources_.append(extra)
        return pick(
            *tables[side], sources_, plan, widths, SLOTS[side], most[side], earlier
        )

    row_blocks, row_ends = ring.gather(second[5], 1)
    grad_slots = [
        picked(side, grad_blocks, grad_ends, (D, 128), signs, [second[0]]) for side in range(2)
    ]
    near_rows, = picked(0, row_blocks, row_ends, (D,), None, [])
    near = expert(
        tables[0][0], near_rows, *grad_slots[0], expert_all, second_bias, router, SLOTS[0],
        [grad_slots[1][0]],
    )
    far_rows, = picked(1, row_blocks, row_ends, (D,), None, [near[3]])
    distant = expert(
        tables[1][0], far_rows, *grad_slots[1], expert_all, second_bias, router, SLOTS[1]
    )
    router_grad = (near[4] + distant[4])[:experts]
    bias_grad = near[5][0] + distant[5][0]
    far_back = unpick(*tables[1], distant[3])
    near_back = unpick(*tables[0], near[3], [far_back[0]])

    def send_back(blocks, start, waits):
        pair = ring.scatter_first(start, 1)
        for step in range(ring.half - 1, 0, -1):
            total = ring_add(
                blocks[2 * step - 1 : 2 * step + 1], pair, step == ring.half - 1
            )
            waits(ring.half - 1 - step, total)
            pair = ring.scatter_next(total)
        return blocks[0], pair[0], pair[1]

    kept = {}

    def meanwhile(step, total):
        if step == 0:
            kept["near"] = expert_rest(
                tables[0][0],
                (near_rows, grad_slots[0][0], *near[:3]),
                expert_all,
                second_bias,
                SLOTS[0],
                None,
                total,
            )
        if step == 1:
            kept["far"] = expert_rest(
                tables[1][0],
                (far_rows, grad_slots[1][0], *distant[:3]),
                expert_all,
                second_bias,
                SLOTS[1],
                kept["near"][0],
                total,
            )
        if step == ring.half - 2:
            far_result = unpick(*tables[1], kept["far"][1], total)
            kept["result"] = unpick(*tables[0], kept["near"][1], [far_result[0]]) + far_result

    returned = send_back(near_back + far_back, far_back[-1], meanwhile)
    results = kept["result"]
    expert_grad = kept["far"][0]
    expert_grad = expert_grad.at[:, 2 * D + 1, :GROUP].set(
        bias_grad.reshape(4, GROUP).astype(BF16)
    )
    expert_grad = lax.psum_scatter(
        expert_grad.reshape(-1, D), "tp", scatter_dimension=0, tiled=True
    ).astype(F32)

    backward = []

    def attention_back(index, earlier):
        backward.append(
            attend_back(
                tokens, cotangent, index, returned, forward[index][4], forward[index][3], norms,
                weights, forward[index][1], earlier,
            )
        )

    def meanwhile(step, total):
        if step < 2:
            attention_back(step, total)

    start = after(results[-1], returned[1], returned[2])
    result = send_back(results, start, meanwhile)
    outputs = sum(part.astype(F32) for part in result)
    outputs = [(forward[i][4] + outputs[i]).astype(BF16) for i in range(2)]

    normed = [f[0] for f in forward]
    mixed = [f[2] for f in forward]
    branch = [b[1] for b in backward]
    grads = [b[2] for b in backward]
    order = [count - 1]
    for step in range(ring.half - 1, 0, -1):
        order += [2 * step - 1, 2 * step]
    order.append(0)
    sizes = (3 * count // 8, count // 4, count - 3 * count // 8 - count // 4)
    settings = (order, sources, rows, rows_up)
    opposite, across = weight_grads(normed, grads, branch, mixed, (3, 2), *settings, [])
    beside, own = weight_grads(normed, grads, branch, mixed, (1, 0), *settings, [across])
    far_parts = [to_x(part) for part in sum_parts(across, to_core(opposite), sizes)]
    near_parts = sum_parts(own, to_core(beside), sizes)

    def absolute(values):
        values = values.reshape(2, 2, GROUP)
        values = jnp.where(core == 0, values, values[:, ::-1])
        return jnp.where(far == 0, values, values[::-1]).reshape(1, D)

    sums = backward[0][3] + backward[1][3]
    bias_sums = backward[0][4] + backward[1][4]
    small = jnp.concatenate(
        [
            sums[0:3],
            absolute(bias_sums[:, :GROUP]),
            absolute(bias_sums[:, 2 * GROUP : 3 * GROUP]),
            sums[3:5],
            router_grad,
        ],
        axis=0,
    )
    small = small + to_core(small)
    small = small + to_x(small)
    small = small.reshape(smalls, count, columns).transpose(1, 0, 2).reshape(count, -1)
    small = jnp.pad(small, ((0, 0), (0, 16 * D - smalls * columns)))
    small = small.reshape(count, 16, D).astype(BF16)
    cut = (tall // 2 + 15) // 16 * 16
    found = [(part, i) for part in range(3) for i in range(sizes[part])]

    def step_of(entries, received, kind=BF16):
        part = found[entries[0][0]][0]
        return tail(
            [(order[at], found[at][1], how) for at, how in entries],
            sources,
            small,
            near_parts[part],
            far_parts[part],
            received,
            cut,
            kind,
        )

    pair = ring.scatter_first(step_of([(0, "none")], [])[0], cut)
    for step in range(ring.half - 1):
        how = ("low", "high") if step == 0 else ("full", "full")
        total = step_of([(2 * step + 1, how[0]), (2 * step + 2, how[1])], pair)
        pair = ring.scatter_next(total)
    (summed,) = step_of([(count - 1, "both")], pair, F32)
    attn_grad = summed[:rows, : 3 * GROUP].reshape(rows, 3, GROUP).transpose(1, 0, 2)
    out_grad = summed[:rows, 3 * GROUP :].T
    small = summed[rows_up : rows_up + 2].reshape(-1)[: smalls * columns]
    small = lax.dynamic_slice_in_dim(
        small.reshape(smalls, columns), tp * (columns // 4), columns // 4, 1
    )
    return (
        jnp.concatenate(outputs, axis=0),
        jnp.concatenate([b[0] for b in backward], axis=0),
        small[0:2],
        small[2:7],
        attn_grad,
        out_grad,
        small[7:],
        expert_grad[None, :D],
        expert_grad[2 * D : 2 * D + 1],
        expert_grad[None, D : 2 * D],
        expert_grad[2 * D + 1 : 2 * D + 2, :GROUP],
    )


def solution(mesh):
    both = ("wide", "tp")
    return jax.shard_map(
        functools.partial(body, mesh.shape["wide"]),
        mesh=mesh,
        in_specs=(
            P(both, None),
            P(None, both),
            P(None, both),
            P(None, "wide", "tp"),
            P("tp", "wide"),
            P(None, both),
            P("wide", None, "tp"),
            P("wide", "tp"),
            P("wide", None, "tp"),
            P("wide", "tp"),
            P("wide", None),
            P(both, None),
        ),
        out_specs=(
            P(both, None),
            P(both, None),
            P(None, both),
            P(None, both),
            P(None, "wide", "tp"),
            P("tp", "wide"),
            P(None, both),
            P("wide", None, "tp"),
            P("wide", "tp"),
            P("wide", None, "tp"),
            P("wide", "tp"),
        ),
        check_vma=False,
    )
```

```python
import functools

import jax
import jax.numpy as jnp
from jax import lax
from jax.experimental import pallas as pl
from jax.experimental.pallas import tpu as pltpu
from jax.sharding import PartitionSpec as P

D = 768
FF = 3072
HD = 64
SEQ = 200
VALID = 197
GROUP = 192
SLOTS = 960
WINDOW = 224
NARROW = 96
EPSILON = 1e-06
MASKED = -1000000000.0
F32 = jnp.float32
BF16 = jnp.bfloat16
VALID_LANE = 64
MIB = 1 << 20


def params(megabytes, sizes=None):
    semantics = None if sizes is None else ("arbitrary",) * sizes
    return pltpu.CompilerParams(
        vmem_limit_bytes=megabytes * MIB, dimension_semantics=semantics
    )


def cost(flops, moved, slow=0):
    return pl.CostEstimate(flops=int(flops), bytes_accessed=int(moved), transcendentals=int(slow))


def dot(left, right):
    return jnp.dot(left, right, preferred_element_type=F32)


def dot_nt(left, right):
    return lax.dot_general(left, right, (((1,), (1,)), ((), ())), preferred_element_type=F32)


def dot_tn(left, right):
    return lax.dot_general(left, right, (((0,), (0,)), ((), ())), preferred_element_type=F32)


def standardize(inputs):
    average = jnp.mean(inputs, axis=-1, keepdims=True)
    centered = inputs - average
    inverse = lax.rsqrt(jnp.mean(centered * centered, axis=-1, keepdims=True) + EPSILON)
    return centered * inverse, inverse


def norm_back(upstream, scaled, inverse, gain):
    grad_hat = upstream * gain
    mean_grad = jnp.mean(grad_hat, axis=-1, keepdims=True)
    mean_cross = jnp.mean(grad_hat * scaled, axis=-1, keepdims=True)
    return inverse * (grad_hat - mean_grad - scaled * mean_cross)


class Ring:
    def __init__(self, count):
        self.count = count
        self.half = count // 2
        self.order = list(range(0, count, 2)) + list(range(count - 1, 0, -2))
        self.ahead = [(self.order[i], self.order[(i + 1) % count]) for i in range(count)]
        self.behind = [(self.order[i], self.order[i - 1]) for i in range(count)]

    def sources(self):
        me = lax.axis_index("wide")
        place = jnp.where(me % 2 == 0, me // 2, self.count - 1 - me // 2)

        def at(position):
            position = position % self.count
            return jnp.where(
                position < self.half, 2 * position, 2 * (self.count - 1 - position) + 1
            )

        found = [at(place)]
        for step in range(1, self.half):
            found += [at(place - step), at(place + step)]
        return jnp.stack(found + [at(place + self.half)]).astype(jnp.int32)

    def forward(self, block):
        return lax.ppermute(block, "wide", self.ahead)

    def backward(self, block):
        return lax.ppermute(block, "wide", self.behind)

    def gather(self, block, ends, meanwhile=lambda step, found: ()):
        found = [block]
        left = right = block
        waits = meanwhile(0, found)
        for step in range(1, self.half):
            if waits and step == 1:
                left = right = found[0] = after(block, *waits)
            elif waits:
                left, right = found[-2:] = after(left, *waits), after(right, *waits)
            left, right = self.forward(left), self.backward(right)
            found += [left, right]
            waits = meanwhile(step, found)
        first, second = ends(left, right, waits)
        return found, (self.forward(first), self.backward(second))

    def scatter_first(self, first, second):
        return self.backward(first), self.forward(second)

    def scatter_next(self, pair):
        return self.backward(pair[0]), self.forward(pair[1])


def to_core(block):
    return lax.ppermute(block, "tp", [(i, i ^ 1) for i in range(4)])


def to_x(block):
    return lax.ppermute(block, "tp", [(i, i ^ 2) for i in range(4)])


def prepare_kernel(
    rows, width, start, queries, outward, gains, shifts, router, routes, out
):
    square = jnp.concatenate(
        [queries[i].astype(F32) for i in range(3)] + [outward[...].astype(F32).T], axis=1
    )
    missing = out.shape[0] - 16 - rows
    if missing:
        square = jnp.concatenate([square, jnp.zeros((missing, D), F32)], axis=0)
    out[0 : rows + missing] = square.astype(BF16)
    small = jnp.concatenate(
        [gains[...].astype(F32), shifts[...].astype(F32), router[...].astype(F32)], axis=0
    )
    amount = small.shape[0]
    small = jnp.concatenate([small, jnp.zeros((-amount % 16, width), F32)], axis=0)
    parts = []
    for i in range(0, amount, 16):
        parts += [small[i : i + 16], jnp.zeros((16, 32 - width), F32)]
    filled = 32 * len(range(0, amount, 16))
    parts.append(jnp.zeros((16, 128 - filled), F32))
    chosen = routes[pl.ds(pl.multiple_of(start[0], 8), 2 * SEQ)].astype(F32).T
    chosen = jnp.concatenate([chosen, jnp.zeros((14, 2 * SEQ), F32)], axis=0)
    parts += [chosen, jnp.zeros((16, D - 128 - 2 * SEQ), F32)]
    out[rows + missing :] = jnp.concatenate(parts, axis=1).astype(BF16)


def assemble_kernel(count, rows, source_ref, *refs):
    blocks, first, second = refs[: count - 1], refs[count - 1], refs[count]
    own, across, small, in_turn = refs[count + 1 :]
    for i in range(count):
        place = source_ref[i]
        for k, weights in enumerate((own, across)):
            block = blocks[i].at[k] if i < count - 1 else (first, second)[k].at[0]
            weights[place] = block[0:rows]
            small[k, place] = block[rows:, 0:128]
            if k == 0:
                in_turn[i] = block[rows:]


def tables_kernel(mine, named, spans, places, signs):
    count = named.shape[0]
    size = 2 * count
    parts = [named[i].astype(F32) for i in range(count)]
    one, other = (
        jnp.concatenate(
            [part[j : j + 1, 128 + SEQ * k : 128 + SEQ * (k + 1)] for part in parts for k in range(2)], axis=0
        )
        for j in (0, 1)
    )
    expert_id = mine[0].astype(F32)
    is_chosen = (one == expert_id) | (other == expert_id)
    other = jnp.where(one == expert_id, other, one).astype(BF16)
    chosen = is_chosen.astype(F32).astype(BF16)
    row = lax.broadcasted_iota(jnp.int32, (SEQ, SEQ), 0)
    column = lax.broadcasted_iota(jnp.int32, (SEQ, SEQ), 1)
    rank = dot(chosen, (row < column).astype(F32).astype(BF16))
    counts = dot_nt(jnp.ones((8, SEQ), BF16), chosen)
    row = lax.broadcasted_iota(jnp.int32, (size, size), 0)
    column = lax.broadcasted_iota(jnp.int32, (size, size), 1)
    starts = dot(counts.astype(BF16), (row < column).astype(F32).astype(BF16))
    line = lax.broadcasted_iota(jnp.int32, (8, size), 0)
    spans[...] = jnp.where(line == 0, starts, starts + counts).astype(jnp.int32)
    amounts = jnp.sum(chosen.astype(F32), axis=1, keepdims=True).astype(BF16)
    lower = (column < row).astype(F32).astype(BF16)
    starts = dot(lower, jnp.broadcast_to(amounts, (size, 128)))[:, 0:1]
    places[...] = jnp.where(is_chosen, starts + rank, -1.0).astype(jnp.int32)
    turned = dot_tn(other, (row == column).astype(F32).astype(BF16))
    lane = lax.broadcasted_iota(jnp.int32, (SEQ, 128), 1).astype(F32)
    is_valid = (lax.broadcasted_iota(jnp.int32, (SEQ, 128), 0) < VALID).astype(F32)
    for i in range(size):
        sign = (lane == expert_id).astype(F32) - (lane == turned[:, i : i + 1]).astype(F32)
        signs[i] = jnp.where(lane == VALID_LANE, is_valid, sign).astype(BF16)


def attend_kernel(groups, is_last, tokens, norms, bias, *refs):
    weights, refs = refs[: len(groups)], refs[len(groups) :]
    key_valid = lax.broadcasted_iota(jnp.int32, (SEQ, SEQ), 1) < VALID
    lane = lax.broadcasted_iota(jnp.int32, (SEQ, 128), 1)
    if is_last:
        normed_ref, sums_in, residual_in, qkv_ref, mixed_ref, sums_ref, residual_ref, second_ref = (
            refs
        )
    else:
        normed_ref, qkv_ref, mixed_ref, sums_ref, residual_ref = refs
    for i in range(2):
        if is_last:
            normed, residual, sums = normed_ref[i], residual_in[i], sums_in[i]
        else:
            inputs = tokens[i].astype(F32)
            scaled, _ = standardize(inputs)
            normed = (scaled * norms[0:1] + norms[2:3]).astype(BF16)
            normed_ref[i] = normed
            residual = inputs + norms[5:6]
            sums = jnp.zeros((SEQ, 128), F32)
        for k, j in enumerate(groups):
            projected = (dot(normed, weights[k][...]) + bias[j : j + 1]).astype(BF16)
            qkv_ref[i, k] = projected
            mixed = [jnp.zeros((SEQ, HD), BF16)]
            for h in range(3):
                query = projected[:, HD * h : HD * (h + 1)]
                key_rows = projected[:, GROUP + HD * h : GROUP + HD * (h + 1)]
                value = projected[:, 2 * GROUP + HD * h : 2 * GROUP + HD * (h + 1)]
                scores = jnp.where(key_valid, dot_nt(query, key_rows) * HD ** (-0.5), MASKED)
                row_max = jnp.max(scores, axis=-1, keepdims=True)
                exponent = jnp.exp(scores - row_max)
                row_sum = jnp.sum(exponent, axis=-1, keepdims=True)
                attention = (exponent / row_sum).astype(BF16)
                mixed.append(dot(attention, value).astype(BF16))
                sums = jnp.where(lane == 3 * j + h, row_max + jnp.log(row_sum), sums)
            mixed = jnp.concatenate(mixed, axis=1)
            mixed_ref[i, k] = mixed
            residual = residual + dot_nt(mixed, weights[k][:, D - 256 :])
        sums_ref[i] = sums
        residual_ref[i] = residual
        if is_last:
            scaled_two, _ = standardize(residual)
            second_ref[i] = (scaled_two * norms[1:2] + norms[6:7]).astype(BF16)


def attend_back_kernel(
    index, tokens, cotangent, one, other, left, right, residual_ref, sums_ref, norms, *refs
):
    weights = refs[:4]
    residual, sums_ref = residual_ref[index], sums_ref.at[index]
    halves_ = refs[4:6]
    input_grad, branch_ref, grads_ref, small_ref, bias_ref = refs[-5:]
    grad_two = (one, other)[index][0].astype(F32) + left[index].astype(F32) + right[index].astype(F32)
    scaled_two, inverse_two = standardize(residual)
    grad_mid = cotangent[index].astype(F32) + norm_back(
        grad_two, scaled_two, inverse_two, norms[1:2]
    )
    branch = grad_mid.astype(BF16)
    branch_ref[...] = branch
    key_valid = lax.broadcasted_iota(jnp.int32, (SEQ, SEQ), 1) < VALID
    grad_one = jnp.zeros((SEQ, D), F32)
    scale = HD ** (-0.5)
    for j in range(4):
        qkv_ref = halves_[j // 2].at[index, j % 2]
        upstream = dot(branch, weights[j][:, D - 256 :]).astype(BF16)
        grads = [[], [], []]
        for h in range(3):
            query = qkv_ref[:, HD * h : HD * (h + 1)]
            key_rows = qkv_ref[:, GROUP + HD * h : GROUP + HD * (h + 1)]
            value = qkv_ref[:, 2 * GROUP + HD * h : 2 * GROUP + HD * (h + 1)]
            up = upstream[:, HD * (h + 1) : HD * (h + 2)]
            scores = jnp.where(key_valid, dot_nt(query, key_rows) * scale, MASKED)
            attention = jnp.exp(scores - sums_ref[:, 3 * j + h : 3 * j + h + 1])
            grad_attn = dot_nt(up, value)
            inner = jnp.sum(attention * grad_attn, axis=-1, keepdims=True)
            grad_scores = (attention * (grad_attn - inner)).astype(BF16)
            grads[0].append((dot(grad_scores, key_rows) * scale).astype(BF16))
            grads[1].append((dot_tn(grad_scores, query) * scale).astype(BF16))
            grads[2].append(dot_tn(attention.astype(BF16), up).astype(BF16))
        whole = jnp.concatenate(
            grads[0] + grads[1] + grads[2] + [jnp.zeros((SEQ, GROUP), BF16)], axis=1
        )
        grads_ref[j] = whole
        bias_ref[j : j + 1] = jnp.sum(whole.astype(F32), axis=0, keepdims=True)
        grad_one = grad_one + dot_nt(whole, weights[j][...])
    scaled_one, inverse_one = standardize(tokens[index].astype(F32))
    input_back = grad_mid + norm_back(grad_one, scaled_one, inverse_one, norms[0:1])
    if index:
        input_grad[0] = refs[6][...]
        input_grad[1] = input_back
    else:
        input_grad[...] = input_back
    small_ref[...] = jnp.concatenate(
        [
            jnp.sum(part, axis=0, keepdims=True)
            for part in (
                grad_one * scaled_one,
                grad_two * scaled_two,
                grad_one,
                grad_mid,
                grad_two,
            )
        ]
        + [jnp.zeros((3, D), F32)],
        axis=0,
    )


def weight_grad_kernel(groups, places, rows, sources, normed, grads_one, grads_two, *refs):
    grads, branch, mixed = (grads_one, grads_two), refs[0:2], refs[2]
    outs, whole = refs[3:-1], refs[-1]
    for out, j in zip(outs, groups):
        whole[...] = dot_tn(normed[0], grads[0][j]) + dot_tn(normed[1], grads[1][j])
        whole[:, D - 256 :] += dot_tn(branch[0][...], mixed[0, j % 2]) + dot_tn(
            branch[1][...], mixed[1, j % 2]
        )
        for i, place in enumerate(places):
            start = pl.multiple_of(sources[place] * rows, 8)
            block = whole[pl.ds(start, rows)]
            missing = out.shape[1] - rows
            if missing:
                block = jnp.concatenate([block, jnp.zeros((missing, D), F32)], axis=0)
            out[i] = block.astype(BF16)


def tile_rows(tile):
    return pl.ds(pl.multiple_of(tile * SLOTS, 16), SLOTS)


def moved(semaphores, *pairs):
    copies = [
        pltpu.make_async_copy(source, target, semaphores.at[i])
        for i, (source, target) in enumerate(pairs)
    ]
    for copy in copies:
        copy.start()
    for copy in copies:
        copy.wait()


def pick_rows(spans, places_ref, begin, plan, sources, held):
    def some(i, start, height):
        slot = lax.broadcasted_iota(jnp.int32, (height, SEQ), 0) + start
        chosen = (places_ref[i : i + 1] == slot).astype(F32).astype(BF16)
        for target, stream in zip(held, plan):
            which, index = stream[i - begin]
            window = target.at[pl.ds(start, height)]
            window[...] += dot(chosen, sources[which][index]).astype(BF16)

    for i in range(begin, begin + len(plan[0])):
        start = pl.multiple_of(spans[0, i] // 16 * 16, 16)
        some(i, start, NARROW)
        pl.when(spans[1, i] > start + NARROW)(
            functools.partial(some, i, pl.multiple_of(start + NARROW, 16), WINDOW - NARROW)
        )


def unpick_rows(spans, places_ref, begin, held, outs):
    total = total_of(spans)

    def some(i, start, height):
        slot = lax.broadcasted_iota(jnp.int32, (height, SEQ), 0) + start
        chosen = (places_ref[i : i + 1] == slot).astype(F32).astype(BF16)
        row = lax.broadcasted_iota(jnp.int32, (height, D), 0) + start
        window = held[pl.ds(start, height)]
        window = jnp.where(row < total, window, jnp.zeros_like(window))
        return dot_tn(chosen, window).astype(BF16)

    for i in range(begin, begin + len(outs)):
        out = outs[i - begin].at[0]
        start = pl.multiple_of(spans[0, i] // 16 * 16, 16)
        out[...] = some(i, start, NARROW)

        @pl.when(spans[1, i] > start + NARROW)
        def _(i=i, out=out, start=start):
            more = pl.multiple_of(start + NARROW, 16)
            out[...] += some(i, more, WINDOW - NARROW)


def total_of(spans):
    return spans[1, spans.shape[1] - 1]


def tiles_of(spans):
    return jnp.maximum(1, (total_of(spans) + SLOTS - 1) // SLOTS)


def clear_rows(spans, held):
    def clear(tile, carry):
        for target in held:
            target[tile_rows(tile)] = jnp.zeros((SLOTS, target.shape[1]), BF16)
        return carry

    lax.fori_loop(0, tiles_of(spans), clear, 0)


def pick_kernel(plan, spans, places_ref, sources, outs, scratch, semaphores):
    clear_rows(spans, scratch)
    pick_rows(spans, places_ref, 0, plan, sources, scratch)

    def store(tile, carry):
        at = tile_rows(tile)
        moved(semaphores, *[(held.at[at], out.at[at]) for held, out in zip(scratch, outs)])
        return carry

    lax.fori_loop(0, tiles_of(spans), store, 0)


def unpick_kernel(spans, places_ref, array, *refs):
    outs, scratch, semaphores = refs[:-2], refs[-2], refs[-1]

    def load(tile, carry):
        at = tile_rows(tile)
        moved(semaphores, (array.at[at], scratch.at[at]))
        return carry

    lax.fori_loop(0, tiles_of(spans), load, 0)
    unpick_rows(spans, places_ref, 0, scratch, outs)


def expert_kernel(
    plan, count, spans, places_ref, near_hbm, grads_hbm, chosen_hbm, weights_hbm, second_bias,
    router, *refs,
):
    sources = refs[:count]
    (
        rows, weights, grads, chosen, gates, total, hidden, pre_back,
        weight_semaphores, in_semaphores, out_semaphores,
    ) = refs[-11:]
    rows_hbm, hidden_hbm, pre_hbm, gates_hbm, back_hbm, router_ref, bias_ref, *images = refs[
        count : -11
    ]
    begin = spans.shape[1] - len(plan)
    parts = FF // D
    loads = [
        pltpu.make_async_copy(weights_hbm.at[f], weights.at[f], weight_semaphores.at[f])
        for f in range(parts)
    ]
    start = tile_rows(0)
    early = [
        pltpu.make_async_copy(source.at[start], target, in_semaphores.at[2 + i])
        for i, (source, target) in enumerate(
            ((near_hbm, rows.at[start]), (chosen_hbm, chosen), (grads_hbm, grads))
        )
    ]
    early[0].start()
    loads[0].start()
    early[1].start()
    early[2].start()
    for load in loads[1:]:
        load.start()
    router_ref[...] = jnp.zeros_like(router_ref)
    bias_ref[...] = jnp.zeros_like(bias_ref)

    def fetch(tile, carry):
        at = tile_rows(tile)
        moved(in_semaphores, (near_hbm.at[at], rows.at[at]))
        return carry

    early[0].wait()
    lax.fori_loop(1, tiles_of(spans), fetch, 0)
    pick_rows(spans, places_ref, begin, [plan], sources, [rows])
    for load in loads + early[1:]:
        load.wait()

    def tile(m, carry):
        at = tile_rows(m)
        keep = pltpu.make_async_copy(rows.at[at], rows_hbm.at[at], out_semaphores.at[0])
        keep.start()

        @pl.when(m > 0)
        def _():
            moved(in_semaphores, (grads_hbm.at[at], grads), (chosen_hbm.at[at], chosen))

        lane = lax.broadcasted_iota(jnp.int32, (SLOTS, 128), 1)
        signs = jnp.where(lane < VALID_LANE, chosen[...].astype(F32), 0.0)
        is_valid = chosen[:, VALID_LANE : VALID_LANE + 1].astype(F32)
        gap = jnp.sum(dot_nt(rows[at], router[...]) * signs, axis=1, keepdims=True)
        weight = is_valid / (1.0 + jnp.exp(-gap))
        slope = weight / (1.0 + jnp.exp(gap))
        upstream = grads[...].astype(F32)
        direct = jnp.sum(upstream * second_bias[0:1], axis=1, keepdims=True)
        gates[...] = jnp.where(lane == 0, weight, jnp.where(lane == 1, slope, direct))
        bias_ref[0:1] += jnp.sum(weight * upstream, axis=0, keepdims=True)
        stores = []
        for f in range(parts):
            first, second = weights.at[f, 0:D], weights.at[f, D : 2 * D]
            bias = weights[f, 2 * D : 2 * D + 16][0:1].astype(F32)
            pre = dot(rows[at], first[...]) + bias
            upward = dot(grads[...], second[...])
            below = 0.5 * (1.0 + lax.erf(pre * 0.5**0.5))
            density = jnp.exp(-0.5 * pre * pre) * (0.5 / 3.141592653589793) ** 0.5
            activation = pre * below
            weight = gates[:, 0:1]
            added = jnp.sum(activation * upward, axis=1, keepdims=True)
            hidden[f] = (weight * activation).astype(BF16)
            pre_back[f] = (weight * upward * (below + pre * density)).astype(BF16)
            for k, (held, target) in enumerate(((hidden, hidden_hbm), (pre_back, pre_hbm))):
                stores.append(
                    pltpu.make_async_copy(
                        held.at[f],
                        target.at[at, pl.ds(f * D, D)],
                        out_semaphores.at[2 + 2 * f + k],
                    )
                )
                stores[-1].start()
            gates[...] += jnp.where(lane == 2, added, 0.0)
            if f:
                total[...] += dot_nt(pre_back[f], first[...])
            else:
                total[...] = dot_nt(pre_back[f], first[...])
        stores.append(pltpu.make_async_copy(gates, gates_hbm.at[at], out_semaphores.at[1]))
        stores[-1].start()
        logits_grad = (signs * gates[:, 1:2] * gates[:, 2:3]).astype(BF16)
        router_ref[...] += dot_tn(logits_grad, rows[at])
        keep.wait()
        rows[at] = (total[...] + dot(logits_grad, router[...])).astype(BF16)
        keep = pltpu.make_async_copy(rows.at[at], back_hbm.at[at], out_semaphores.at[0])
        keep.start()
        for store in [*stores, keep]:
            store.wait()
        return carry

    lax.fori_loop(0, tiles_of(spans), tile, 0)
    unpick_rows(spans, places_ref, begin, rows, images)


def gradient_kernel(with_result, spans, *refs):
    if with_result:
        left_hbm, right_hbm, gates_hbm, weights_hbm, second_bias = refs[:5]
        grad_hbm, result_hbm = refs[5:7]
        left, right, grad, gates, second, total, finished, in_semaphores, out_semaphores = refs[7:]
    else:
        left_hbm, right_hbm, bias, grad_hbm, left, right, grad, in_semaphores, out_semaphores = refs
    parts = FF // D

    def work(tile, adds):
        at = tile_rows(tile)
        pairs = [(left_hbm.at[at], left)]
        for f in range(parts):
            pairs.append((right_hbm.at[at, pl.ds(f * D, D)], right.at[f]))
            if with_result and f == 0:
                pairs.append((gates_hbm.at[at], gates))
            if with_result:
                pairs.append((weights_hbm.at[f, pl.ds(D, D)], second.at[f]))
            if adds:
                pairs.append((grad_hbm.at[f], grad.at[f]))
        loads = [
            pltpu.make_async_copy(source, target, in_semaphores.at[i])
            for i, (source, target) in enumerate(pairs)
        ]
        for load in loads:
            load.start()
        if adds:
            for load in loads:
                load.wait()
            loads = []

        def arrive(amount):
            for _ in range(min(amount, len(loads))):
                loads.pop(0).wait()

        stores = []
        for f in range(parts):
            arrive(2 if f == 0 else 1)
            one = dot_tn(left[...], right[f])
            if adds:
                one = one + grad[f, 0:D].astype(F32)
            grad[f, 0:D] = one.astype(BF16)
            if not with_result:
                sums = jnp.sum(right[f].astype(F32), axis=0, keepdims=True)
                if adds:
                    sums = sums + grad[f, D : D + 16].astype(F32)[0:1]
                line = lax.broadcasted_iota(jnp.int32, (16, D), 0)
                grad[f, D:] = jnp.where(line == 0, sums, bias[f : f + 1]).astype(BF16)
            stores.append(pltpu.make_async_copy(grad.at[f], grad_hbm.at[f], out_semaphores.at[f]))
            stores[-1].start()
            if with_result:
                arrive(2 if f == 0 else 1)
                result = dot_nt(right[f], second[f])
                if f:
                    total[...] += result
                else:
                    total[...] = gates[:, 0:1] * second_bias[0:1] + result
        if with_result:
            finished[...] = total[...].astype(BF16)
            stores.append(
                pltpu.make_async_copy(finished, result_hbm.at[at], out_semaphores.at[parts])
            )
            stores[-1].start()
        for store in stores:
            store.wait()

    work(0, False)

    def more(tile, carry):
        work(tile, True)
        return carry

    lax.fori_loop(1, tiles_of(spans), more, 0)


def finish_kernel(one, other, first, second, first_bias, second_bias):
    first[0] = one[0:D].astype(F32)
    second[0] = other[...].astype(F32)
    last = one[D:].astype(F32)
    first_bias[...] = last[0:1]
    second_bias[...] = last[1:2, :GROUP]


def output_kernel(residual, one, other, left, right, out):
    for i, mine in enumerate((one, other)):
        total = mine[0].astype(F32) + left[i].astype(F32) + right[i].astype(F32)
        out[i] = (residual[i] + total).astype(BF16)


def pack_kernel(first, second, small, out):
    out[0:D] = first[0]
    out[D : 2 * D] = second[0]
    out[2 * D :] = small[...]


def ring_add_kernel(is_first, *refs):
    outs = refs[-2:]

    def sums(one, other):
        return (one.astype(F32) + other.astype(F32)).astype(BF16)

    for k, out in enumerate(outs):
        first, second, received = refs[3 * k : 3 * k + 3]
        if is_first:
            out[k] = sums((first, second)[k][0], received[0])
            out[1 - k] = (first, second)[1 - k][0]
        else:
            out[0] = sums(first[0], received[0])
            out[1] = sums(second[0], received[1])


def sum_parts_kernel(one, other, *outs):
    start = 0
    for out in outs:
        part = slice(start, start + out.shape[0])
        out[...] = (one[part].astype(F32) + other[part].astype(F32)).astype(BF16)
        start += out.shape[0]


def tail_kernel(cut, entries, count, sources, small, *refs):
    outs = refs[-5:] if entries[0][2] == "both" else refs[-len(entries) :]
    refs = list(refs[: -len(outs)])
    near, far = refs.pop(0), refs.pop(0)
    for (place, index, kind), out in zip(entries, outs):
        whole = jnp.concatenate(
            [
                near[index].astype(F32) + far[index].astype(F32),
                small[sources[place]].astype(F32),
            ],
            axis=0,
        )
        if kind == "none":
            out[...] = whole.astype(out.dtype)
        elif kind == "low":
            out[0:cut] = (whole[0:cut] + refs.pop(0)[...].astype(F32)).astype(BF16)
            out[cut:] = whole[cut:].astype(BF16)
        elif kind == "high":
            out[0:cut] = whole[0:cut].astype(BF16)
            out[cut:] = (whole[cut:] + refs.pop(0)[...].astype(F32)).astype(BF16)
        elif kind == "full":
            out[...] = (whole + refs.pop(0)[...].astype(F32)).astype(BF16)
        else:
            whole = whole + refs[0][...].astype(F32) + refs[1][...].astype(F32)
            gains, shifts, router, queries, outward = outs
            rows, width = outward.shape[1], gains.shape[1]
            for i in range(3):
                queries[i] = whole[0:rows, GROUP * i : GROUP * (i + 1)]
            outward[...] = whole[0:rows, 3 * GROUP :].T
            low = whole[near.shape[1] :]
            mine = [
                pltpu.roll(low[:, 128 * i : 128 * (i + 1)], 128 - sources[count], 1)[:, 0:width]
                for i in range(4)
            ]
            mine = jnp.concatenate(mine, axis=0)
            gains[...] = mine[0:2]
            shifts[...] = mine[2:7]
            router[...] = mine[7 : 7 + router.shape[0]]


def nothing_kernel(*refs):
    pass


SMEM = pl.BlockSpec(memory_space=pltpu.SMEM)
VMEM = pl.BlockSpec(memory_space=pltpu.VMEM)
ANY = pl.BlockSpec(memory_space=pl.ANY)
HBM = pl.BlockSpec(memory_space=pltpu.HBM)


def shape(dims, kind=BF16):
    return jax.ShapeDtypeStruct(dims, kind)


def call(kernel, operands, specs, out_shape, out_specs, earlier=(), **settings):
    size = len(operands)
    waits = len(earlier)

    def stripped(*refs):
        kernel(*refs[:size], *refs[size + waits :])

    megabytes = settings.pop("megabytes", 32)
    work = settings.pop("work", (1e6, 1e6))
    if settings.pop("token", False):
        place = size + waits + len(out_shape)
        out_shape = list(out_shape) + [shape((8, 128), F32)]
        out_specs = list(out_specs) + [VMEM]

        def stripped(*refs):
            kernel(*refs[:size], *refs[size + waits : place], *refs[place + 1 :])
            refs[place][...] = jnp.zeros((8, 128), F32)

    return pl.pallas_call(
        stripped,
        in_specs=list(specs) + [ANY] * waits,
        out_specs=out_specs,
        out_shape=out_shape,
        compiler_params=params(megabytes),
        cost_estimate=cost(*work),
        **settings,
    )(*operands, *earlier)


def prepare(start, attn_weight, out_weight, gains, shifts, router, routes, rows_up):
    return call(
        functools.partial(prepare_kernel, attn_weight.shape[1], gains.shape[1]),
        [start, attn_weight, out_weight, gains, shifts, router, routes],
        [SMEM] + [VMEM] * 6,
        shape((rows_up + 16, D)),
        VMEM,
    )


def assemble(blocks, parts, sources, rows):
    count = len(blocks) + 1
    tall = blocks[0].shape[1]
    return call(
        functools.partial(assemble_kernel, count, rows),
        [sources, *blocks, *parts],
        [SMEM] + [VMEM] * (count + 1),
        [shape((count, rows, D))] * 2
        + [shape((2, count, tall - rows, 128)), shape((count, tall - rows, D))],
        [VMEM] * 4,
        megabytes=24,
    )


def make_tables(mine, named):
    size = 2 * named.shape[0]
    return call(
        tables_kernel,
        [mine, named],
        [SMEM, VMEM],
        [
            shape((8, size), jnp.int32),
            shape((size, SEQ), jnp.int32),
            shape((size, SEQ, 128)),
        ],
        [VMEM] * 3,
        work=(3e9, 1e6),
    )


def halves_kernel(left, right, first, second):
    first[0] = left[0]
    second[0] = right[1]


def halves(left, right, waits):
    return call(
        halves_kernel, [left, right], [VMEM] * 2, [shape((1, SEQ, D))] * 2, [VMEM] * 2, waits
    )


def attend(groups, tokens, norms, bias, weights, earlier, before=None):
    more = [] if before is None else [before[0], *before[3:5]]
    outs = [
        shape((2, len(groups), SEQ, D)),
        shape((2, len(groups), SEQ, 256)),
        shape((2, SEQ, 128), F32),
        shape((2, SEQ, D), F32),
    ]
    rows = [shape((2, SEQ, D))]
    return call(
        functools.partial(attend_kernel, groups, bool(more)),
        [tokens, norms, bias, *[weights[j] for j in groups], *more],
        [VMEM] * (3 + len(groups) + len(more)),
        outs + rows if more else rows + outs,
        [VMEM] * 5,
        earlier,
        work=(8e9, 9e6),
    )


def attend_back(
    tokens, cotangent, index, parts, residual, sums, norms, weights, qkv, earlier, other=None
):
    more = [] if other is None else [other]
    return call(
        functools.partial(attend_back_kernel, index),
        [tokens, cotangent, *parts, residual, sums, norms, *weights, *qkv, *more],
        [VMEM] * (15 + len(more)),
        [
            shape((2, SEQ, D) if more else (SEQ, D), F32),
            shape((SEQ, D)),
            shape((4, SEQ, D)),
            shape((8, D), F32),
            shape((4, D), F32),
        ],
        [VMEM] * 5,
        earlier,
        work=(3e10, 9e6),
    )


def weight_grads(normed, grads, branch, mixed, groups, places, sources, rows, rows_up, earlier):
    return call(
        functools.partial(weight_grad_kernel, groups, places, rows),
        [sources, normed, *grads, *branch, mixed],
        [SMEM] + [VMEM] * 6,
        [shape((len(places), rows_up, D))] * len(groups),
        [VMEM] * len(groups),
        earlier,
        scratch_shapes=[pltpu.VMEM((D, D), F32)],
        work=(2e10, 5e6),
    )


def sum_parts(one, other, sizes):
    return call(
        sum_parts_kernel,
        [one, other],
        [VMEM] * 2,
        [shape((size,) + one.shape[1:]) for size in sizes],
        [VMEM] * len(sizes),
    )


def tail(entries, sources, small, near, far, received, cut, last=None, earlier=()):
    tall = near.shape[1] + small.shape[1]
    outs = [shape((tall, D))] * len(entries)
    if last is not None:
        rows, width, experts = last
        outs = [
            shape((2, width), F32),
            shape((5, width), F32),
            shape((experts, width), F32),
            shape((3, rows, GROUP), F32),
            shape((GROUP, rows), F32),
        ]
    return call(
        functools.partial(tail_kernel, cut, entries, small.shape[0]),
        [sources, small, near, far, *received],
        [SMEM] + [VMEM] * (3 + len(received)),
        outs,
        [VMEM] * len(outs),
        earlier,
    )


def finish(one, other):
    return call(
        finish_kernel,
        [one, other],
        [VMEM] * 2,
        [shape((1, D, D), F32)] * 2 + [shape((1, D), F32), shape((1, GROUP), F32)],
        [VMEM] * 4,
    )


def output(residual, parts):
    return call(
        output_kernel, [residual, *parts], [VMEM] * 5, shape((2, SEQ, D)), VMEM
    )


def pick(plan, tables, sources, widths, most, earlier=()):
    streams = len(widths)

    def kernel(*refs):
        last = refs[-2 * streams - 1 :]
        pick_kernel(
            plan, refs[0], refs[1], refs[2:], last[:streams], last[streams : 2 * streams], last[-1]
        )

    return call(
        kernel,
        [*tables, *sources],
        [SMEM, VMEM] + [VMEM] * len(sources),
        [shape((most, width)) for width in widths],
        [HBM] * streams,
        earlier,
        token=True,
        scratch_shapes=[pltpu.VMEM((most + WINDOW, width), BF16) for width in widths]
        + [pltpu.SemaphoreType.DMA((streams,))],
        megabytes=48,
        work=(6e9, 6e6),
    )


def unpick(images, tables, array, earlier=()):
    return call(
        unpick_kernel,
        [*tables, array],
        [SMEM, VMEM, HBM],
        [shape((1, SEQ, D))] * images,
        [VMEM] * images,
        earlier,
        scratch_shapes=[
            pltpu.VMEM((array.shape[0] + WINDOW, D), BF16), pltpu.SemaphoreType.DMA((1,))
        ],
        megabytes=55,
        work=(2e10, 6e6),
    )


def expert(plan, tables, near, grads, chosen, weights, second_bias, router, sources, earlier=()):
    most = near.shape[0]
    parts = FF // D
    images = len(plan)
    return call(
        functools.partial(expert_kernel, plan, len(sources)),
        [*tables, near, grads, chosen, weights, second_bias, router, *sources],
        [SMEM, VMEM, HBM, HBM, HBM, HBM, VMEM, VMEM] + [VMEM] * len(sources),
        [
            shape((most, D)),
            shape((most, FF)),
            shape((most, FF)),
            shape((most, 128), F32),
            shape((most, D)),
            shape((128, D), F32),
            shape((8, D), F32),
        ]
        + [shape((1, SEQ, D))] * images,
        [HBM] * 5 + [VMEM] * (2 + images),
        earlier,
        scratch_shapes=[
            pltpu.VMEM((most + WINDOW, D), BF16),
            pltpu.VMEM((parts, 2 * D + 16, D), BF16),
            pltpu.VMEM((SLOTS, D), BF16),
            pltpu.VMEM((SLOTS, 128), BF16),
            pltpu.VMEM((SLOTS, 128), F32),
            pltpu.VMEM((SLOTS, D), F32),
            pltpu.VMEM((parts, SLOTS, D), BF16),
            pltpu.VMEM((parts, SLOTS, D), BF16),
            pltpu.SemaphoreType.DMA((parts,)),
            pltpu.SemaphoreType.DMA((5,)),
            pltpu.SemaphoreType.DMA((2 + 2 * parts,)),
        ],
        megabytes=60,
        work=(2.5e10, 2e7),
    )


def first_gradient(spans, rows, pre, bias, earlier):
    parts = FF // D
    return call(
        functools.partial(gradient_kernel, False),
        [spans, rows, pre, bias],
        [SMEM, HBM, HBM, VMEM],
        [shape((parts, D + 16, D))],
        [HBM],
        earlier,
        token=True,
        scratch_shapes=[
            pltpu.VMEM((SLOTS, D), BF16),
            pltpu.VMEM((parts, SLOTS, D), BF16),
            pltpu.VMEM((parts, D + 16, D), BF16),
            pltpu.SemaphoreType.DMA((1 + 2 * parts,)),
            pltpu.SemaphoreType.DMA((parts,)),
        ],
        megabytes=55,
        work=(1.2e10, 3e7),
    )


def second_gradient(spans, grads, hidden, gates, weights, second_bias, earlier):
    parts = FF // D
    return call(
        functools.partial(gradient_kernel, True),
        [spans, grads, hidden, gates, weights, second_bias],
        [SMEM, HBM, HBM, HBM, HBM, VMEM],
        [shape((parts, D, D)), shape((grads.shape[0], D))],
        [HBM] * 2,
        earlier,
        token=True,
        scratch_shapes=[
            pltpu.VMEM((SLOTS, D), BF16),
            pltpu.VMEM((parts, SLOTS, D), BF16),
            pltpu.VMEM((parts, D, D), BF16),
            pltpu.VMEM((SLOTS, 128), F32),
            pltpu.VMEM((parts, D, D), BF16),
            pltpu.VMEM((SLOTS, D), F32),
            pltpu.VMEM((SLOTS, D), BF16),
            pltpu.SemaphoreType.DMA((2 + 3 * parts,)),
            pltpu.SemaphoreType.DMA((parts + 1,)),
        ],
        megabytes=55,
        work=(1.6e10, 3e7),
    )


def pack(first, second, small, earlier):
    return call(
        pack_kernel,
        [first, second, small],
        [VMEM] * 3,
        [shape((2 * D + 16, D))],
        [VMEM],
        earlier,
        token=True,
    )


def ring_add(blocks, received, is_first, earlier=()):
    return call(
        functools.partial(ring_add_kernel, is_first),
        [*blocks[0:2], received[0], *blocks[2:4], received[1]],
        [VMEM] * 6,
        [shape((2, SEQ, D))] * 2,
        [VMEM] * 2,
        earlier,
    )


def token_kernel(out):
    out[...] = jnp.zeros_like(out)


def token_of(*earlier):
    return call(token_kernel, [], [], shape((8, 128), F32), VMEM, earlier, work=(0, 0))


def after(value, *earlier, megabytes=32):
    return call(
        nothing_kernel,
        [value],
        [ANY],
        shape(value.shape, value.dtype),
        ANY,
        earlier,
        input_output_aliases={0: 0},
        megabytes=megabytes,
        work=(0, 0),
    )


def body(
    count,
    tokens,
    norm_gains,
    shifts,
    attn_weight,
    out_weight,
    router_weight,
    expert_in,
    expert_in_bias,
    expert_down,
    expert_down_bias,
    routes,
    cotangent,
):
    ring = Ring(count)
    sources = ring.sources()
    wide, tp = lax.axis_index("wide"), lax.axis_index("tp")
    core, far = tp % 2, tp // 2
    rows = D // count
    rows_up = -(-rows // 16) * 16
    experts = router_weight.shape[0]
    group_rows = routes.shape[0]
    local_rows = tokens.shape[0]
    capacity = (10 * group_rows // (4 * experts) + 7) // 8 * 8
    most = -(-count * min(local_rows, capacity) // SLOTS) * SLOTS
    near_groups = 2 * ring.half - 3
    smalls = 7 + experts
    columns = D // count

    own_columns = columns // 4
    start = (tp * local_rows).reshape(1).astype(jnp.int32)
    block = prepare(
        start, attn_weight, out_weight, norm_gains, shifts, router_weight, routes, rows_up
    )
    tall = block.shape[0]
    expert_block = jnp.concatenate(
        [
            expert_in_bias,
            jnp.pad(expert_down_bias, ((0, 0), (0, D - GROUP))),
            jnp.zeros((14, D), BF16),
        ],
        axis=0,
    )
    packed = []

    def meanwhile(step, found):
        if step == 1:
            packed.extend(pack(expert_in, expert_down, expert_block, found[:1]))
            return packed[1:]
        return ()

    both = jnp.stack([block, to_x(block)])
    blocks, ends = ring.gather(both, lambda left, right, waits: (left[:1], right[1:]), meanwhile)
    own, across, small, in_turn = assemble(blocks, ends, sources, rows_up)
    own, across = (array[:, :rows].reshape(D, D) for array in (own, across))
    expert_all = after(packed[0], in_turn)
    expert_all = lax.all_gather(expert_all, "tp", axis=0, tiled=True).reshape(4, -1, D)
    second_bias = jnp.broadcast_to(
        expert_all[:, 2 * D + 1, :GROUP].reshape(1, D).astype(F32), (8, D)
    )
    beside, opposite = to_core(own), to_core(across)
    weights = (own, beside, across, opposite)
    small_beside, small_opposite = to_core(small)
    small, small_across = small

    def in_order(swap, one, other):
        return jnp.where(swap, jnp.stack([other, one]), jnp.stack([one, other]))

    small = in_order(
        far == 1,
        in_order(core == 1, small, small_beside),
        in_order(core == 1, small_across, small_opposite),
    )
    small = small.reshape(2, 2, count, 16, 4, 32)[..., :own_columns]
    norms = small.transpose(4, 3, 2, 0, 1, 5).reshape(64, D)[:smalls].astype(F32)
    router = jnp.pad(norms[7:].astype(BF16), ((0, 128 - experts), (0, 0)))

    def relative(values):
        values = values.reshape(2, 2, GROUP)
        values = jnp.where(far == 0, values, values[::-1])
        return jnp.where(core == 0, values, values[:, ::-1]).reshape(4, GROUP)

    nothing = jnp.zeros((4, GROUP), F32)
    bias = jnp.concatenate([relative(norms[3]), nothing, relative(norms[4]), nothing], axis=1)

    spans, places, signs = make_tables(wide.reshape(1).astype(jnp.int32), in_turn)
    tables = (spans, places)

    tokens = tokens.reshape(2, SEQ, D)
    cotangent = after(cotangent.reshape(2, SEQ, D), *ends)
    first, second = [], []

    def meanwhile(step, found):
        if step == 0:
            return (spans,)
        if step == 1:
            return (token_of(beside, opposite),)
        if step == 2:
            first.extend(attend((0, 1), tokens, norms, bias, weights, found[1:3]))
            return first[3:4]
        if step == 3:
            second.extend(attend((2, 3), tokens, norms, bias, weights, found[3:5], first))
            return second[2:3]
        return ()

    grad_blocks, grad_ends = ring.gather(cotangent, halves, meanwhile)
    qkv, mixed = (first[1], second[0]), (first[2], second[1])
    normed, sums, residual = first[0], second[2], second[3]

    def plan_of(groups):
        plan = []
        for at, group in enumerate(groups):
            plan += [(at, 0), (at, 1)] if group < count - 1 else [(at, 0), (at + 1, 0)]
        return plan

    everything = [plan_of(range(count)), [(count + 1, k) for k in range(2 * count)]]
    grad_slots, sign_slots, picked = pick(
        everything, tables, [*grad_blocks, *grad_ends, signs], (D, 128), most, [second[2]]
    )
    near = []

    def meanwhile(step, found):
        if step == 0:
            return grad_ends
        if step == 1:
            return (picked,)
        if step == ring.half - 1:
            groups = range(near_groups)
            near.extend(
                pick(
                    [plan_of(groups)], tables, found[:near_groups], (D,), most,
                    (picked, *found[-4:-2]),
                )
            )
            return near[1:]
        return ()

    row_blocks, row_ends = ring.gather(second[4], halves, meanwhile)
    rows_, hidden, pre, gates, back, router_grad, bias_grad, *far_back = expert(
        plan_of(range(near_groups, count)), tables, near[0], grad_slots, sign_slots, expert_all,
        second_bias, router, [*row_blocks[near_groups:], *row_ends],
    )
    router_grad = router_grad[:experts]
    bias_rows = jnp.pad(bias_grad[0].reshape(4, GROUP), ((0, 4), (0, D - GROUP)))
    near_back = unpick(2 * near_groups, tables, back, far_back[-1:])
    back = [*near_back, *far_back]

    def send_back(images, waits, meanwhile):
        first, second = images[-2:]
        if waits:
            first, second = after(first, *waits), after(second, *waits)
        pair = ring.scatter_first(first, second)
        waits = meanwhile(0, (first, second))
        for step in range(1, ring.half):
            at = ring.half - step
            total = ring_add(images[4 * at - 2 : 4 * at + 2], pair, step == 1, waits)
            pair = ring.scatter_next(total)
            waits = meanwhile(step, total)
        return (images[0], images[1], pair[0], pair[1])

    kept = {}

    def meanwhile(step, waits):
        if step == 0:
            return near_back[:1]
        if step == 1:
            kept["first"] = first_gradient(spans, rows_, pre, bias_rows, waits)
            return kept["first"][1:]
        if step == 2:
            kept["one"] = scatter_over_tp(after(kept["first"][0], waits[0], megabytes=55))
            kept["second"] = second_gradient(
                spans, grad_slots, hidden, gates, expert_all, second_bias, waits
            )
            return kept["second"][2:]
        if step == 3:
            kept["other"] = scatter_over_tp(after(kept["second"][0], waits[0], megabytes=55))
            kept["results"] = unpick(2 * count, tables, kept["second"][1], waits)
        return ()

    def scatter_over_tp(grad):
        return lax.psum_scatter(grad.reshape(-1, D), "tp", scatter_dimension=0, tiled=True)

    returned = send_back(back, (), meanwhile)
    results = kept["results"]

    order = [count - 1]
    for step in range(ring.half - 1, 0, -1):
        order += [2 * step - 1, 2 * step]
    order.append(0)
    backward = []
    grads = []

    def meanwhile(step, waits):
        if step < 2:
            backward.append(
                attend_back(
                    tokens, cotangent, step, returned, residual, sums, norms, weights, qkv, waits,
                    backward[0][0] if step else None,
                )
            )
            return (backward[step][1],)
        if step == 2:
            backward.append([after(backward[1][k], waits[0]) for k in (3, 4)])
            for groups in ((3, 2), (1, 0)):
                grads.extend(
                    weight_grads(
                        normed, [b[2] for b in backward[:2]], [b[1] for b in backward[:2]],
                        mixed[groups[0] // 2], groups, order, sources, rows, rows_up,
                        grads[1:] or waits,
                    )
                )
            return (grads[3],)
        if step == 3:
            grads[:] = [after(grad, waits[0]) for grad in grads]
        return ()

    result = send_back(results, returned[2:], meanwhile)
    outputs = output(residual, result).reshape(-1, D)

    opposite, across, beside, own = grads
    sizes = (3 * count // 8, count // 4, count - 3 * count // 8 - count // 4)
    far_parts = [to_x(part) for part in sum_parts(across, to_core(opposite), sizes)]
    near_parts = sum_parts(own, to_core(beside), sizes)
    finished = finish(kept["one"], kept["other"])

    def absolute(values):
        values = values.reshape(2, 2, GROUP)
        values = jnp.where(core == 0, values, values[:, ::-1])
        return jnp.where(far == 0, values, values[::-1]).reshape(1, D)

    sums = backward[0][3] + backward[2][0]
    bias_sums = backward[0][4] + backward[2][1]
    small = jnp.concatenate(
        [
            sums[0:3],
            absolute(bias_sums[:, :GROUP]),
            absolute(bias_sums[:, 2 * GROUP : 3 * GROUP]),
            sums[3:5],
            router_grad,
        ],
        axis=0,
    )
    small = small + to_core(small)
    small = small + to_x(small)
    small = jnp.pad(small, ((0, 64 - smalls), (0, 0))).reshape(4, 16, count, columns)
    small = jnp.pad(small, ((0, 0), (0, 0), (0, 0), (0, 128 - columns))).transpose(2, 1, 0, 3)
    small = jnp.pad(small.reshape(count, 16, 512), ((0, 0), (0, 0), (0, D - 512))).astype(BF16)
    cut = (tall // 2 + 15) // 16 * 16
    found = [(part, i) for part in range(3) for i in range(sizes[part])]

    def step_of(entries, received, earlier=()):
        part = found[entries[0][0]][0]
        return tail(
            [(order[at], found[at][1], how) for at, how in entries],
            sources,
            small,
            near_parts[part],
            far_parts[part],
            received,
            cut,
            None,
            earlier,
        )

    (whole,) = step_of([(0, "none")], [], (outputs,))
    pair = ring.scatter_first(whole[:cut], whole[cut:])
    for step in range(ring.half - 1):
        how = ("low", "high") if step == 0 else ("full", "full")
        total = step_of([(2 * step + 1, how[0]), (2 * step + 2, how[1])], pair)
        pair = ring.scatter_next(total)
    gains_grad, shifts_grad, router_grad, attn_grad, out_grad = tail(
        [(order[count - 1], found[count - 1][1], "both")],
        jnp.concatenate([sources, (tp * own_columns).reshape(1).astype(jnp.int32)]),
        small,
        near_parts[2],
        far_parts[2],
        pair,
        cut,
        (rows, own_columns, experts),
        finished[2:3],
    )
    return (
        outputs,
        backward[1][0].reshape(-1, D),
        gains_grad,
        shifts_grad,
        attn_grad,
        out_grad,
        router_grad,
        finished[0],
        finished[2],
        finished[1],
        finished[3],
    )


def solution(mesh):
    both = ("wide", "tp")
    return jax.shard_map(
        functools.partial(body, mesh.shape["wide"]),
        mesh=mesh,
        in_specs=(
            P(both, None),
            P(None, both),
            P(None, both),
            P(None, "wide", "tp"),
            P("tp", "wide"),
            P(None, both),
            P("wide", None, "tp"),
            P("wide", "tp"),
            P("wide", None, "tp"),
            P("wide", "tp"),
            P("wide", None),
            P(both, None),
        ),
        out_specs=(
            P(both, None),
            P(both, None),
            P(None, both),
            P(None, both),
            P(None, "wide", "tp"),
            P("tp", "wide"),
            P(None, both),
            P("wide", None, "tp"),
            P("wide", "tp"),
            P("wide", None, "tp"),
            P("wide", "tp"),
        ),
        check_vma=False,
    )
```

```python
import functools

import jax
import jax.numpy as jnp
from jax import lax
from jax.experimental import pallas as pl
from jax.experimental.pallas import tpu as pltpu
from jax.sharding import PartitionSpec as P

D = 768
FF = 3072
HD = 64
SEQ = 200
VALID = 197
GROUP = 192
SLOTS = 960
WINDOW = 224
NARROW = 96
EPSILON = 1e-06
MASKED = -1000000000.0
F32 = jnp.float32
BF16 = jnp.bfloat16
VALID_LANE = 64
MIB = 1 << 20


def params(megabytes, sizes=None):
    semantics = None if sizes is None else ("arbitrary",) * sizes
    return pltpu.CompilerParams(
        vmem_limit_bytes=megabytes * MIB, dimension_semantics=semantics
    )


def cost(flops, moved, slow=0):
    return pl.CostEstimate(flops=int(flops), bytes_accessed=int(moved), transcendentals=int(slow))


def dot(left, right):
    return jnp.dot(left, right, preferred_element_type=F32)


def dot_nt(left, right):
    return lax.dot_general(left, right, (((1,), (1,)), ((), ())), preferred_element_type=F32)


def dot_tn(left, right):
    return lax.dot_general(left, right, (((0,), (0,)), ((), ())), preferred_element_type=F32)


def standardize(inputs):
    average = jnp.mean(inputs, axis=-1, keepdims=True)
    centered = inputs - average
    inverse = lax.rsqrt(jnp.mean(centered * centered, axis=-1, keepdims=True) + EPSILON)
    return centered * inverse, inverse


def norm_back(upstream, scaled, inverse, gain):
    grad_hat = upstream * gain
    mean_grad = jnp.mean(grad_hat, axis=-1, keepdims=True)
    mean_cross = jnp.mean(grad_hat * scaled, axis=-1, keepdims=True)
    return inverse * (grad_hat - mean_grad - scaled * mean_cross)


class Ring:
    def __init__(self, count):
        self.count = count
        self.half = count // 2
        self.order = list(range(0, count, 2)) + list(range(count - 1, 0, -2))
        self.ahead = [(self.order[i], self.order[(i + 1) % count]) for i in range(count)]
        self.behind = [(self.order[i], self.order[i - 1]) for i in range(count)]

    def sources(self):
        me = lax.axis_index("wide")
        place = jnp.where(me % 2 == 0, me // 2, self.count - 1 - me // 2)

        def at(position):
            position = position % self.count
            return jnp.where(
                position < self.half, 2 * position, 2 * (self.count - 1 - position) + 1
            )

        found = [at(place)]
        for step in range(1, self.half):
            found += [at(place - step), at(place + step)]
        return jnp.stack(found + [at(place + self.half)]).astype(jnp.int32)

    def forward(self, block):
        return lax.ppermute(block, "wide", self.ahead)

    def backward(self, block):
        return lax.ppermute(block, "wide", self.behind)

    def gather(self, block, ends, meanwhile=lambda step, found: ()):
        found = [block]
        left = right = block
        waits = meanwhile(0, found)
        for step in range(1, self.half):
            if waits and step == 1:
                left = right = found[0] = after(block, *waits)
            elif waits:
                left, right = found[-2:] = after(left, *waits), after(right, *waits)
            left, right = self.forward(left), self.backward(right)
            found += [left, right]
            waits = meanwhile(step, found)
        first, second = ends(left, right, waits)
        return found, (self.forward(first), self.backward(second))

    def scatter_first(self, first, second):
        return self.backward(first), self.forward(second)

    def scatter_next(self, pair):
        return self.backward(pair[0]), self.forward(pair[1])


def to_core(block):
    return lax.ppermute(block, "tp", [(i, i ^ 1) for i in range(4)])


def to_x(block):
    return lax.ppermute(block, "tp", [(i, i ^ 2) for i in range(4)])


def prepare_kernel(
    rows, width, start, queries, outward, gains, shifts, router, routes, out
):
    square = jnp.concatenate(
        [queries[i].astype(F32) for i in range(3)] + [outward[...].astype(F32).T], axis=1
    )
    missing = out.shape[0] - 16 - rows
    if missing:
        square = jnp.concatenate([square, jnp.zeros((missing, D), F32)], axis=0)
    out[0 : rows + missing] = square.astype(BF16)
    small = jnp.concatenate(
        [gains[...].astype(F32), shifts[...].astype(F32), router[...].astype(F32)], axis=0
    )
    amount = small.shape[0]
    small = jnp.concatenate([small, jnp.zeros((-amount % 16, width), F32)], axis=0)
    parts = []
    for i in range(0, amount, 16):
        parts += [small[i : i + 16], jnp.zeros((16, 32 - width), F32)]
    filled = 32 * len(range(0, amount, 16))
    parts.append(jnp.zeros((16, 128 - filled), F32))
    chosen = routes[pl.ds(pl.multiple_of(start[0], 8), 2 * SEQ)].astype(F32).T
    chosen = jnp.concatenate([chosen, jnp.zeros((14, 2 * SEQ), F32)], axis=0)
    parts += [chosen, jnp.zeros((16, D - 128 - 2 * SEQ), F32)]
    out[rows + missing :] = jnp.concatenate(parts, axis=1).astype(BF16)


def assemble_kernel(count, rows, source_ref, *refs):
    blocks, first, second = refs[: count - 1], refs[count - 1], refs[count]
    own, across, small, in_turn = refs[count + 1 :]
    for i in range(count):
        place = source_ref[i]
        for k, weights in enumerate((own, across)):
            block = blocks[i].at[k] if i < count - 1 else (first, second)[k].at[0]
            weights[place] = block[0:rows]
            small[k, place] = block[rows:, 0:128]
            if k == 0:
                in_turn[i] = block[rows:]


def tables_kernel(mine, named, spans, places, signs):
    count = named.shape[0]
    size = 2 * count
    parts = [named[i].astype(F32) for i in range(count)]
    one, other = (
        jnp.concatenate(
            [part[j : j + 1, 128 + SEQ * k : 128 + SEQ * (k + 1)] for part in parts for k in range(2)], axis=0
        )
        for j in (0, 1)
    )
    expert_id = mine[0].astype(F32)
    is_chosen = (one == expert_id) | (other == expert_id)
    other = jnp.where(one == expert_id, other, one).astype(BF16)
    chosen = is_chosen.astype(F32).astype(BF16)
    row = lax.broadcasted_iota(jnp.int32, (SEQ, SEQ), 0)
    column = lax.broadcasted_iota(jnp.int32, (SEQ, SEQ), 1)
    rank = dot(chosen, (row < column).astype(F32).astype(BF16))
    counts = dot_nt(jnp.ones((8, SEQ), BF16), chosen)
    row = lax.broadcasted_iota(jnp.int32, (size, size), 0)
    column = lax.broadcasted_iota(jnp.int32, (size, size), 1)
    starts = dot(counts.astype(BF16), (row < column).astype(F32).astype(BF16))
    line = lax.broadcasted_iota(jnp.int32, (8, size), 0)
    spans[...] = jnp.where(line == 0, starts, starts + counts).astype(jnp.int32)
    amounts = jnp.sum(chosen.astype(F32), axis=1, keepdims=True).astype(BF16)
    lower = (column < row).astype(F32).astype(BF16)
    starts = dot(lower, jnp.broadcast_to(amounts, (size, 128)))[:, 0:1]
    places[...] = jnp.where(is_chosen, starts + rank, -1.0).astype(jnp.int32)
    turned = dot_tn(other, (row == column).astype(F32).astype(BF16))
    lane = lax.broadcasted_iota(jnp.int32, (SEQ, 128), 1).astype(F32)
    is_valid = (lax.broadcasted_iota(jnp.int32, (SEQ, 128), 0) < VALID).astype(F32)
    for i in range(size):
        sign = (lane == expert_id).astype(F32) - (lane == turned[:, i : i + 1]).astype(F32)
        signs[i] = jnp.where(lane == VALID_LANE, is_valid, sign).astype(BF16)


def norms_kernel(width, place, own, beside, norms, router, bias):
    tp = place[0]
    blocks, count = norms.shape[0] // 16, own.shape[1]
    found = [[] for _ in range(blocks)]
    for w in range(count):
        for t in range(4):
            far = t // 2 + (1 - 2 * (t // 2)) * (tp // 2)
            here = t % 2 + (1 - 2 * (t % 2)) * (tp % 2)
            values = jnp.where(
                here == 0, own[far, w].astype(F32), beside[far, w].astype(F32)
            )
            for k in range(blocks):
                found[k].append(values[:, 32 * k : 32 * k + width])
    for k in range(blocks):
        norms[16 * k : 16 * k + 16] = jnp.concatenate(found[k], axis=1)
    router[...] = jnp.zeros_like(router)
    rows = jnp.concatenate([norms[7:], jnp.zeros((7, D), F32)], axis=0)
    router[0 : 16 * blocks] = rows.astype(BF16)
    nothing = jnp.zeros((1, GROUP), F32)
    for j in range(4):
        t = tp + (1 - 2 * (tp % 2)) * (j % 2)
        t = t + (2 - 4 * (t // 2)) * (j // 2)
        queries, values = (
            pltpu.roll(norms[k : k + 1], D - t * GROUP, 1)[:, 0:GROUP] for k in (3, 4)
        )
        bias[j : j + 1] = jnp.concatenate([queries, nothing, values, nothing], axis=1)


def attend_kernel(groups, is_last, tokens, norms, bias, *refs):
    weights, refs = refs[: len(groups)], refs[len(groups) :]
    key_valid = lax.broadcasted_iota(jnp.int32, (SEQ, SEQ), 1) < VALID
    lane = lax.broadcasted_iota(jnp.int32, (SEQ, 128), 1)
    if is_last:
        normed_ref, sums_in, residual_in, qkv_ref, mixed_ref, sums_ref, residual_ref, second_ref = (
            refs
        )
    else:
        normed_ref, qkv_ref, mixed_ref, sums_ref, residual_ref = refs
    for i in range(2):
        if is_last:
            normed, residual, sums = normed_ref[i], residual_in[i], sums_in[i]
        else:
            inputs = tokens[i].astype(F32)
            scaled, _ = standardize(inputs)
            normed = (scaled * norms[0:1] + norms[2:3]).astype(BF16)
            normed_ref[i] = normed
            residual = inputs + norms[5:6]
            sums = jnp.zeros((SEQ, 128), F32)
        for k, j in enumerate(groups):
            projected = (dot(normed, weights[k][...]) + bias[j : j + 1]).astype(BF16)
            qkv_ref[i, k] = projected
            mixed = [jnp.zeros((SEQ, HD), BF16)]
            for h in range(3):
                query = projected[:, HD * h : HD * (h + 1)]
                key_rows = projected[:, GROUP + HD * h : GROUP + HD * (h + 1)]
                value = projected[:, 2 * GROUP + HD * h : 2 * GROUP + HD * (h + 1)]
                scores = jnp.where(key_valid, dot_nt(query, key_rows) * HD ** (-0.5), MASKED)
                row_max = jnp.max(scores, axis=-1, keepdims=True)
                exponent = jnp.exp(scores - row_max)
                row_sum = jnp.sum(exponent, axis=-1, keepdims=True)
                attention = (exponent / row_sum).astype(BF16)
                mixed.append(dot(attention, value).astype(BF16))
                sums = jnp.where(lane == 3 * j + h, row_max + jnp.log(row_sum), sums)
            mixed = jnp.concatenate(mixed, axis=1)
            mixed_ref[i, k] = mixed
            residual = residual + dot_nt(mixed, weights[k][:, D - 256 :])
        sums_ref[i] = sums
        residual_ref[i] = residual
        if is_last:
            scaled_two, _ = standardize(residual)
            second_ref[i] = (scaled_two * norms[1:2] + norms[6:7]).astype(BF16)


def attend_back_kernel(
    index, tokens, cotangent, one, other, left, right, residual_ref, sums_ref, norms, *refs
):
    weights = refs[:4]
    residual, sums_ref = residual_ref[index], sums_ref.at[index]
    halves_ = refs[4:6]
    input_grad, branch_ref, grads_ref, small_ref, bias_ref = refs[-5:]
    grad_two = (one, other)[index][0].astype(F32) + left[index].astype(F32) + right[index].astype(F32)
    scaled_two, inverse_two = standardize(residual)
    grad_mid = cotangent[index].astype(F32) + norm_back(
        grad_two, scaled_two, inverse_two, norms[1:2]
    )
    branch = grad_mid.astype(BF16)
    branch_ref[...] = branch
    key_valid = lax.broadcasted_iota(jnp.int32, (SEQ, SEQ), 1) < VALID
    grad_one = jnp.zeros((SEQ, D), F32)
    scale = HD ** (-0.5)
    for j in range(4):
        qkv_ref = halves_[j // 2].at[index, j % 2]
        upstream = dot(branch, weights[j][:, D - 256 :]).astype(BF16)
        grads = [[], [], []]
        for h in range(3):
            query = qkv_ref[:, HD * h : HD * (h + 1)]
            key_rows = qkv_ref[:, GROUP + HD * h : GROUP + HD * (h + 1)]
            value = qkv_ref[:, 2 * GROUP + HD * h : 2 * GROUP + HD * (h + 1)]
            up = upstream[:, HD * (h + 1) : HD * (h + 2)]
            scores = jnp.where(key_valid, dot_nt(query, key_rows) * scale, MASKED)
            attention = jnp.exp(scores - sums_ref[:, 3 * j + h : 3 * j + h + 1])
            grad_attn = dot_nt(up, value)
            inner = jnp.sum(attention * grad_attn, axis=-1, keepdims=True)
            grad_scores = (attention * (grad_attn - inner)).astype(BF16)
            grads[0].append((dot(grad_scores, key_rows) * scale).astype(BF16))
            grads[1].append((dot_tn(grad_scores, query) * scale).astype(BF16))
            grads[2].append(dot_tn(attention.astype(BF16), up).astype(BF16))
        whole = jnp.concatenate(
            grads[0] + grads[1] + grads[2] + [jnp.zeros((SEQ, GROUP), BF16)], axis=1
        )
        grads_ref[j] = whole
        bias_ref[j : j + 1] = jnp.sum(whole.astype(F32), axis=0, keepdims=True)
        grad_one = grad_one + dot_nt(whole, weights[j][...])
    scaled_one, inverse_one = standardize(tokens[index].astype(F32))
    input_back = grad_mid + norm_back(grad_one, scaled_one, inverse_one, norms[0:1])
    if index:
        input_grad[0] = refs[6][...]
        input_grad[1] = input_back
    else:
        input_grad[...] = input_back
    small_ref[...] = jnp.concatenate(
        [
            jnp.sum(part, axis=0, keepdims=True)
            for part in (
                grad_one * scaled_one,
                grad_two * scaled_two,
                grad_one,
                grad_mid,
                grad_two,
            )
        ]
        + [jnp.zeros((3, D), F32)],
        axis=0,
    )


def small_kernel(place, sums_one, sums_two, bias_one, bias_two, router, out):
    sums = sums_one[...] + sums_two[...]
    tp = place[0]
    queries, values = [], []
    for t in range(4):
        first = t % 2 + (1 - 2 * (t % 2)) * (tp % 2)
        second = t // 2 + (1 - 2 * (t // 2)) * (tp // 2)
        row = pl.ds(2 * second + first, 1)
        both = bias_one[row] + bias_two[row]
        queries.append(both[:, 0:GROUP])
        values.append(both[:, 2 * GROUP : 3 * GROUP])
    rows = [
        sums[0:3],
        jnp.concatenate(queries, axis=1),
        jnp.concatenate(values, axis=1),
        sums[3:5],
        router[0 : out.shape[0] - 7],
    ]
    out[...] = jnp.concatenate(rows, axis=0)


def weight_grad_kernel(groups, places, rows, width, sources, small, normed, grads_one, grads_two, *refs):
    grads, branch, mixed = (grads_one, grads_two), refs[0:2], refs[2]
    outs, whole = refs[3:-1], refs[-1]
    for out, j in zip(outs, groups):
        whole[...] = dot_tn(normed[0], grads[0][j]) + dot_tn(normed[1], grads[1][j])
        whole[:, D - 256 :] += dot_tn(branch[0][...], mixed[0, j % 2]) + dot_tn(
            branch[1][...], mixed[1, j % 2]
        )
        tp = sources[len(places)]
        tp = tp + (1 - 2 * (tp % 2)) * (j % 2)
        tp = tp + (2 - 4 * (tp // 2)) * (j // 2)
        missing = out.shape[1] - rows - 16
        for i, place in enumerate(places):
            start = pl.multiple_of(sources[place] * rows, 8)
            block = whole[pl.ds(start, rows)]
            if missing:
                block = jnp.concatenate([block, jnp.zeros((missing, D), F32)], axis=0)
            out[i, 0 : rows + missing] = block.astype(BF16)
            turned = pltpu.roll(small[...], D - (sources[place] * 4 + tp) * width, 1)
            low = [turned[k : k + 16, 0:32] for k in range(0, small.shape[0], 16)]
            low.append(jnp.zeros((16, D - 32 * len(low)), F32))
            out[i, rows + missing :] = jnp.concatenate(low, axis=1).astype(BF16)


def tile_rows(tile):
    return pl.ds(pl.multiple_of(tile * SLOTS, 16), SLOTS)


def moved(semaphores, *pairs):
    copies = [
        pltpu.make_async_copy(source, target, semaphores.at[i])
        for i, (source, target) in enumerate(pairs)
    ]
    for copy in copies:
        copy.start()
    for copy in copies:
        copy.wait()


def window_of(spans, image):
    return pl.multiple_of(spans[0, image] // 16 * 16, 16)


def any_wide(spans, images):
    found = jnp.int32(0)
    for i in images:
        found = jnp.maximum(found, spans[1, i] - window_of(spans, i))
    return found > NARROW


def pick_rows(spans, places_ref, begin, plan, sources, held):
    def some(i, start, height):
        slot = lax.broadcasted_iota(jnp.int32, (height, SEQ), 0) + start
        chosen = (places_ref[i : i + 1] == slot).astype(F32).astype(BF16)
        for target, stream in zip(held, plan):
            which, index = stream[i - begin]
            window = target.at[pl.ds(start, height)]
            window[...] += dot(chosen, sources[which][index]).astype(BF16)

    images = range(begin, begin + len(plan[0]))
    for i in images:
        some(i, window_of(spans, i), NARROW)

    @pl.when(any_wide(spans, images))
    def _():
        for i in images:
            more = pl.multiple_of(window_of(spans, i) + NARROW, 16)
            pl.when(spans[1, i] > more)(functools.partial(some, i, more, WINDOW - NARROW))


def unpick_rows(spans, places_ref, begin, held, outs):
    total = total_of(spans)

    def some(i, start, height):
        slot = lax.broadcasted_iota(jnp.int32, (height, SEQ), 0) + start
        chosen = (places_ref[i : i + 1] == slot).astype(F32).astype(BF16)
        row = lax.broadcasted_iota(jnp.int32, (height, D), 0) + start
        window = held[pl.ds(start, height)]
        window = jnp.where(row < total, window, jnp.zeros_like(window))
        return dot_tn(chosen, window).astype(BF16)

    images = range(begin, begin + len(outs))
    for i in images:
        outs[i - begin][0] = some(i, window_of(spans, i), NARROW)

    @pl.when(any_wide(spans, images))
    def _():
        for i in images:
            more = pl.multiple_of(window_of(spans, i) + NARROW, 16)

            @pl.when(spans[1, i] > more)
            def _(i=i, more=more):
                outs[i - begin][0] += some(i, more, WINDOW - NARROW)


def total_of(spans):
    return spans[1, spans.shape[1] - 1]


def tiles_of(spans):
    return jnp.maximum(1, (total_of(spans) + SLOTS - 1) // SLOTS)


def clear_rows(spans, held):
    def clear(tile, carry):
        for target in held:
            target[tile_rows(tile)] = jnp.zeros((SLOTS, target.shape[1]), BF16)
        return carry

    lax.fori_loop(0, tiles_of(spans), clear, 0)


def pick_kernel(plan, spans, places_ref, sources, outs, scratch, semaphores):
    clear_rows(spans, scratch)
    pick_rows(spans, places_ref, 0, plan, sources, scratch)

    def store(tile, carry):
        at = tile_rows(tile)
        moved(semaphores, *[(held.at[at], out.at[at]) for held, out in zip(scratch, outs)])
        return carry

    lax.fori_loop(0, tiles_of(spans), store, 0)


def unpick_kernel(begin, spans, places_ref, array, *refs):
    outs, scratch, semaphores = refs[:-2], refs[-2], refs[-1]

    def load(tile, carry):
        at = tile_rows(tile)
        moved(semaphores, (array.at[at], scratch.at[at]))
        return carry

    lax.fori_loop(0, tiles_of(spans), load, 0)
    unpick_rows(spans, places_ref, begin, scratch, outs)


def expert_kernel(
    plan, count, spans, places_ref, near_hbm, grads_hbm, chosen_hbm, weights_hbm, second_bias,
    router, *refs,
):
    sources = refs[:count]
    (
        rows, weights, grads, chosen, gates, total, hidden, pre_back,
        weight_semaphores, in_semaphores, out_semaphores,
    ) = refs[-11:]
    rows_hbm, hidden_hbm, pre_hbm, gates_hbm, back_hbm, router_ref, bias_ref, *images = refs[
        count : -11
    ]
    begin = spans.shape[1] - len(plan)
    parts = FF // D
    loads = [
        pltpu.make_async_copy(weights_hbm.at[f], weights.at[f], weight_semaphores.at[f])
        for f in range(parts)
    ]
    start = tile_rows(0)
    early = [
        pltpu.make_async_copy(source.at[start], target, in_semaphores.at[2 + i])
        for i, (source, target) in enumerate(
            ((near_hbm, rows.at[start]), (chosen_hbm, chosen), (grads_hbm, grads))
        )
    ]
    early[0].start()
    loads[0].start()
    early[1].start()
    early[2].start()
    for load in loads[1:]:
        load.start()
    router_ref[...] = jnp.zeros_like(router_ref)
    bias_ref[...] = jnp.zeros_like(bias_ref)

    def fetch(tile, carry):
        at = tile_rows(tile)
        moved(in_semaphores, (near_hbm.at[at], rows.at[at]))
        return carry

    early[0].wait()
    lax.fori_loop(1, tiles_of(spans), fetch, 0)
    pick_rows(spans, places_ref, begin, [plan], sources, [rows])
    for load in loads + early[1:]:
        load.wait()

    def tile(m, carry):
        at = tile_rows(m)
        keep = pltpu.make_async_copy(rows.at[at], rows_hbm.at[at], out_semaphores.at[0])
        keep.start()

        @pl.when(m > 0)
        def _():
            moved(in_semaphores, (grads_hbm.at[at], grads), (chosen_hbm.at[at], chosen))

        lane = lax.broadcasted_iota(jnp.int32, (SLOTS, 128), 1)
        signs = jnp.where(lane < VALID_LANE, chosen[...].astype(F32), 0.0)
        is_valid = chosen[:, VALID_LANE : VALID_LANE + 1].astype(F32)
        gap = jnp.sum(dot_nt(rows[at], router[...]) * signs, axis=1, keepdims=True)
        weight = is_valid / (1.0 + jnp.exp(-gap))
        slope = weight / (1.0 + jnp.exp(gap))
        upstream = grads[...].astype(F32)
        direct = jnp.sum(upstream * second_bias[0:1], axis=1, keepdims=True)
        gates[...] = jnp.where(lane == 0, weight, jnp.where(lane == 1, slope, direct))
        bias_ref[0:1] += jnp.sum(weight * upstream, axis=0, keepdims=True)
        stores = []
        for f in range(parts):
            first, second = weights.at[f, 0:D], weights.at[f, D : 2 * D]
            bias = weights[f, 2 * D : 2 * D + 16][0:1].astype(F32)
            pre = dot(rows[at], first[...]) + bias
            upward = dot(grads[...], second[...])
            below = 0.5 * (1.0 + lax.erf(pre * 0.5**0.5))
            density = jnp.exp(-0.5 * pre * pre) * (0.5 / 3.141592653589793) ** 0.5
            activation = pre * below
            weight = gates[:, 0:1]
            added = jnp.sum(activation * upward, axis=1, keepdims=True)
            hidden[f] = (weight * activation).astype(BF16)
            pre_back[f] = (weight * upward * (below + pre * density)).astype(BF16)
            for k, (held, target) in enumerate(((hidden, hidden_hbm), (pre_back, pre_hbm))):
                stores.append(
                    pltpu.make_async_copy(
                        held.at[f],
                        target.at[at, pl.ds(f * D, D)],
                        out_semaphores.at[2 + 2 * f + k],
                    )
                )
                stores[-1].start()
            gates[...] += jnp.where(lane == 2, added, 0.0)
            if f:
                total[...] += dot_nt(pre_back[f], first[...])
            else:
                total[...] = dot_nt(pre_back[f], first[...])
        stores.append(pltpu.make_async_copy(gates, gates_hbm.at[at], out_semaphores.at[1]))
        stores[-1].start()
        logits_grad = (signs * gates[:, 1:2] * gates[:, 2:3]).astype(BF16)
        router_ref[...] += dot_tn(logits_grad, rows[at])
        keep.wait()
        rows[at] = (total[...] + dot(logits_grad, router[...])).astype(BF16)
        keep = pltpu.make_async_copy(rows.at[at], back_hbm.at[at], out_semaphores.at[0])
        keep.start()
        for store in [*stores, keep]:
            store.wait()
        return carry

    lax.fori_loop(0, tiles_of(spans), tile, 0)
    unpick_rows(spans, places_ref, begin, rows, images)


def gradient_kernel(with_bias, spans, *refs):
    if with_bias:
        left_hbm, right_hbm, bias, grad_hbm, left, right, grad, in_semaphores, out_semaphores = refs
    else:
        left_hbm, right_hbm, grad_hbm, left, right, grad, in_semaphores, out_semaphores = refs
    parts = FF // D

    def work(tile, adds):
        at = tile_rows(tile)
        pairs = [(left_hbm.at[at], left)]
        for f in range(parts):
            pairs.append((right_hbm.at[at, pl.ds(f * D, D)], right.at[f]))
            if adds:
                pairs.append((grad_hbm.at[f], grad.at[f]))
        loads = [
            pltpu.make_async_copy(source, target, in_semaphores.at[i])
            for i, (source, target) in enumerate(pairs)
        ]
        for load in loads:
            load.start()
        if adds:
            for load in loads:
                load.wait()
        else:
            loads[0].wait()
        stores = []
        for f in range(parts):
            if not adds:
                loads[1 + f].wait()
            one = dot_tn(left[...], right[f])
            if adds:
                one = one + grad[f, 0:D].astype(F32)
            grad[f, 0:D] = one.astype(BF16)
            if with_bias:
                sums = jnp.sum(right[f].astype(F32), axis=0, keepdims=True)
                if adds:
                    sums = sums + grad[f, D : D + 16].astype(F32)[0:1]
                line = lax.broadcasted_iota(jnp.int32, (16, D), 0)
                grad[f, D:] = jnp.where(line == 0, sums, bias[f : f + 1]).astype(BF16)
            stores.append(pltpu.make_async_copy(grad.at[f], grad_hbm.at[f], out_semaphores.at[f]))
            stores[-1].start()
        for store in stores:
            store.wait()

    work(0, False)

    def more(tile, carry):
        work(tile, True)
        return carry

    lax.fori_loop(1, tiles_of(spans), more, 0)


def result_kernel(
    begin, spans, places_ref, hidden_hbm, gates_hbm, weights_hbm, second_bias, back_hbm, *refs
):
    images, result_hbm = refs[:-9], refs[-9]
    hidden, second, gates, total, finished, back, in_semaphores, out_semaphores = refs[-8:]
    parts = FF // D

    def work(tile, carry):
        at = tile_rows(tile)
        pairs = [(back_hbm.at[at], back.at[at]), (gates_hbm.at[at], gates)]
        for f in range(parts):
            pairs.append((hidden_hbm.at[at, pl.ds(f * D, D)], hidden.at[f]))
            pairs.append((weights_hbm.at[f, pl.ds(D, D)], second.at[f]))
        loads = [
            pltpu.make_async_copy(source, target, in_semaphores.at[i])
            for i, (source, target) in enumerate(pairs)
        ]
        for load in loads:
            load.start()
        loads[0].wait()
        loads[1].wait()
        for f in range(parts):
            loads[2 + 2 * f].wait()
            loads[3 + 2 * f].wait()
            result = dot_nt(hidden[f], second[f])
            if f:
                total[...] += result
            else:
                total[...] = gates[:, 0:1] * second_bias[0:1] + result
        finished[...] = total[...].astype(BF16)
        moved(out_semaphores, (finished, result_hbm.at[at]))
        return carry

    lax.fori_loop(0, tiles_of(spans), work, 0)
    unpick_rows(spans, places_ref, begin, back, images)


def finish_kernel(one, other, first, second, first_bias, second_bias):
    first[0] = one[0:D].astype(F32)
    second[0] = other[...].astype(F32)
    last = one[D:].astype(F32)
    first_bias[...] = last[0:1]
    second_bias[...] = last[1:2, :GROUP]


def output_kernel(residual, one, other, left, right, out):
    for i, mine in enumerate((one, other)):
        total = mine[0].astype(F32) + left[i].astype(F32) + right[i].astype(F32)
        out[i] = (residual[i] + total).astype(BF16)


def pack_kernel(first, second, small, out):
    out[0:D] = first[0]
    out[D : 2 * D] = second[0]
    out[2 * D :] = small[...]


def ring_add_kernel(is_first, *refs):
    outs = refs[-2:]

    def sums(one, other):
        return (one.astype(F32) + other.astype(F32)).astype(BF16)

    for k, out in enumerate(outs):
        first, second, received = refs[3 * k : 3 * k + 3]
        if is_first:
            out[k] = sums((first, second)[k][0], received[0])
            out[1 - k] = (first, second)[1 - k][0]
        else:
            out[0] = sums(first[0], received[0])
            out[1] = sums(second[0], received[1])


def sum_parts_kernel(one, other, *outs):
    start = 0
    for out in outs:
        part = slice(start, start + out.shape[0])
        out[...] = (one[part].astype(F32) + other[part].astype(F32)).astype(BF16)
        start += out.shape[0]


def tail_kernel(cut, entries, *refs):
    outs = refs[-{"both": 5, "none": 2}.get(entries[0][1], len(entries)) :]
    refs = list(refs[: -len(outs)])
    near, far = refs.pop(0), refs.pop(0)
    for (index, kind), out in zip(entries, outs):
        whole = near[index].astype(F32) + far[index].astype(F32)
        if kind == "none":
            outs[0][...] = whole[0:cut].astype(BF16)
            outs[1][...] = whole[cut:].astype(BF16)
        elif kind == "low":
            out[0:cut] = (whole[0:cut] + refs.pop(0)[...].astype(F32)).astype(BF16)
            out[cut:] = whole[cut:].astype(BF16)
        elif kind == "high":
            out[0:cut] = whole[0:cut].astype(BF16)
            out[cut:] = (whole[cut:] + refs.pop(0)[...].astype(F32)).astype(BF16)
        elif kind == "full":
            out[...] = (whole + refs.pop(0)[...].astype(F32)).astype(BF16)
        else:
            whole = whole + refs[0][...].astype(F32) + refs[1][...].astype(F32)
            gains, shifts, router, queries, outward = outs
            rows, width = outward.shape[1], gains.shape[1]
            for i in range(3):
                queries[i] = whole[0:rows, GROUP * i : GROUP * (i + 1)]
            outward[...] = whole[0:rows, 3 * GROUP :].T
            low = whole[near.shape[1] - 16 :]
            mine = [low[:, 32 * i : 32 * i + width] for i in range(4)]
            mine = jnp.concatenate(mine, axis=0)
            gains[...] = mine[0:2]
            shifts[...] = mine[2:7]
            router[...] = mine[7 : 7 + router.shape[0]]


def nothing_kernel(*refs):
    pass


SMEM = pl.BlockSpec(memory_space=pltpu.SMEM)
VMEM = pl.BlockSpec(memory_space=pltpu.VMEM)
ANY = pl.BlockSpec(memory_space=pl.ANY)
HBM = pl.BlockSpec(memory_space=pltpu.HBM)


def shape(dims, kind=BF16):
    return jax.ShapeDtypeStruct(dims, kind)


def call(kernel, operands, specs, out_shape, out_specs, earlier=(), **settings):
    size = len(operands)
    waits = len(earlier)

    def stripped(*refs):
        kernel(*refs[:size], *refs[size + waits :])

    megabytes = settings.pop("megabytes", 32)
    work = settings.pop("work", (1e6, 1e6))
    if settings.pop("token", False):
        place = size + waits + len(out_shape)
        out_shape = list(out_shape) + [shape((8, 128), F32)]
        out_specs = list(out_specs) + [VMEM]

        def stripped(*refs):
            kernel(*refs[:size], *refs[size + waits : place], *refs[place + 1 :])
            refs[place][...] = jnp.zeros((8, 128), F32)

    return pl.pallas_call(
        stripped,
        in_specs=list(specs) + [ANY] * waits,
        out_specs=out_specs,
        out_shape=out_shape,
        compiler_params=params(megabytes),
        cost_estimate=cost(*work),
        **settings,
    )(*operands, *earlier)


def prepare(start, attn_weight, out_weight, gains, shifts, router, routes, rows_up):
    return call(
        functools.partial(prepare_kernel, attn_weight.shape[1], gains.shape[1]),
        [start, attn_weight, out_weight, gains, shifts, router, routes],
        [SMEM] + [VMEM] * 6,
        shape((rows_up + 16, D)),
        VMEM,
    )


def assemble(blocks, parts, sources, rows):
    count = len(blocks) + 1
    tall = blocks[0].shape[1]
    return call(
        functools.partial(assemble_kernel, count, rows),
        [sources, *blocks, *parts],
        [SMEM] + [VMEM] * (count + 1),
        [shape((count, rows, D))] * 2
        + [shape((2, count, tall - rows, 128)), shape((count, tall - rows, D))],
        [VMEM] * 4,
        megabytes=24,
    )


def make_tables(mine, named):
    size = 2 * named.shape[0]
    return call(
        tables_kernel,
        [mine, named],
        [SMEM, VMEM],
        [
            shape((8, size), jnp.int32),
            shape((size, SEQ), jnp.int32),
            shape((size, SEQ, 128)),
        ],
        [VMEM] * 3,
        work=(3e9, 1e6),
    )


def halves_kernel(left, right, first, second):
    first[0] = left[0]
    second[0] = right[1]


def halves(left, right, waits):
    return call(
        halves_kernel, [left, right], [VMEM] * 2, [shape((1, SEQ, D))] * 2, [VMEM] * 2, waits
    )


def gather_norms(place, own, beside, smalls, width):
    return call(
        functools.partial(norms_kernel, width),
        [place, own, beside],
        [SMEM, VMEM, VMEM],
        [shape((-(-smalls // 16) * 16, D), F32), shape((128, D)), shape((8, D), F32)],
        [VMEM] * 3,
    )


def attend(groups, tokens, norms, bias, weights, earlier, before=None):
    more = [] if before is None else [before[0], *before[3:5]]
    outs = [
        shape((2, len(groups), SEQ, D)),
        shape((2, len(groups), SEQ, 256)),
        shape((2, SEQ, 128), F32),
        shape((2, SEQ, D), F32),
    ]
    rows = [shape((2, SEQ, D))]
    return call(
        functools.partial(attend_kernel, groups, bool(more)),
        [tokens, norms, bias, *[weights[j] for j in groups], *more],
        [VMEM] * (3 + len(groups) + len(more)),
        outs + rows if more else rows + outs,
        [VMEM] * 5,
        earlier,
        work=(8e9, 9e6),
    )


def attend_back(
    tokens, cotangent, index, parts, residual, sums, norms, weights, qkv, earlier, other=None
):
    more = [] if other is None else [other]
    return call(
        functools.partial(attend_back_kernel, index),
        [tokens, cotangent, *parts, residual, sums, norms, *weights, *qkv, *more],
        [VMEM] * (15 + len(more)),
        [
            shape((2, SEQ, D) if more else (SEQ, D), F32),
            shape((SEQ, D)),
            shape((4, SEQ, D)),
            shape((8, D), F32),
            shape((4, D), F32),
        ],
        [VMEM] * 5,
        earlier,
        work=(3e10, 9e6),
    )


def weight_grads(
    normed, grads, branch, mixed, groups, places, sources, small, rows, rows_up, width, earlier
):
    return call(
        functools.partial(weight_grad_kernel, groups, places, rows, width),
        [sources, small, normed, *grads, *branch, mixed],
        [SMEM] + [VMEM] * 7,
        [shape((len(places), rows_up + 16, D))] * len(groups),
        [VMEM] * len(groups),
        earlier,
        scratch_shapes=[pltpu.VMEM((D, D), F32)],
        work=(2e10, 5e6),
    )


def small_terms(place, backward, router, rows, earlier):
    return call(
        small_kernel,
        [place, backward[0][3], backward[1][3], backward[0][4], backward[1][4], router],
        [SMEM] + [VMEM] * 5,
        shape((rows, D), F32),
        VMEM,
        earlier,
    )


def sum_parts(one, other, sizes):
    return call(
        sum_parts_kernel,
        [one, other],
        [VMEM] * 2,
        [shape((size,) + one.shape[1:]) for size in sizes],
        [VMEM] * len(sizes),
    )


def tail(entries, near, far, received, cut, last=None, earlier=()):
    outs = [shape((near.shape[1], D))] * len(entries)
    if entries[0][1] == "none":
        outs = [shape((cut, D)), shape((near.shape[1] - cut, D))]
    if last is not None:
        rows, width, experts = last
        outs = [
            shape((2, width), F32),
            shape((5, width), F32),
            shape((experts, width), F32),
            shape((3, rows, GROUP), F32),
            shape((GROUP, rows), F32),
        ]
    return call(
        functools.partial(tail_kernel, cut, entries),
        [near, far, *received],
        [VMEM] * (2 + len(received)),
        outs,
        [VMEM] * len(outs),
        earlier,
    )


def finish(one, other):
    return call(
        finish_kernel,
        [one, other],
        [VMEM] * 2,
        [shape((1, D, D), F32)] * 2 + [shape((1, D), F32), shape((1, GROUP), F32)],
        [VMEM] * 4,
    )


def output(residual, parts):
    return call(
        output_kernel, [residual, *parts], [VMEM] * 5, shape((2, SEQ, D)), VMEM
    )


def pick(plan, tables, sources, widths, most, earlier=()):
    streams = len(widths)

    def kernel(*refs):
        last = refs[-2 * streams - 1 :]
        pick_kernel(
            plan, refs[0], refs[1], refs[2:], last[:streams], last[streams : 2 * streams], last[-1]
        )

    return call(
        kernel,
        [*tables, *sources],
        [SMEM, VMEM] + [VMEM] * len(sources),
        [shape((most, width)) for width in widths],
        [HBM] * streams,
        earlier,
        token=True,
        scratch_shapes=[pltpu.VMEM((most + WINDOW, width), BF16) for width in widths]
        + [pltpu.SemaphoreType.DMA((streams,))],
        megabytes=48,
        work=(6e9, 6e6),
    )


def unpick(begin, end, tables, array, earlier=()):
    images = end - begin
    return call(
        functools.partial(unpick_kernel, begin),
        [*tables, array],
        [SMEM, VMEM, HBM],
        [shape((1, SEQ, D))] * images,
        [VMEM] * images,
        earlier,
        scratch_shapes=[
            pltpu.VMEM((array.shape[0] + WINDOW, D), BF16), pltpu.SemaphoreType.DMA((1,))
        ],
        megabytes=50,
        work=(2e10, 6e6),
    )


def expert(plan, tables, near, grads, chosen, weights, second_bias, router, sources, earlier=()):
    most = near.shape[0]
    parts = FF // D
    images = len(plan)
    return call(
        functools.partial(expert_kernel, plan, len(sources)),
        [*tables, near, grads, chosen, weights, second_bias, router, *sources],
        [SMEM, VMEM, HBM, HBM, HBM, HBM, VMEM, VMEM] + [VMEM] * len(sources),
        [
            shape((most, D)),
            shape((most, FF)),
            shape((most, FF)),
            shape((most, 128), F32),
            shape((most, D)),
            shape((128, D), F32),
            shape((8, D), F32),
        ]
        + [shape((1, SEQ, D))] * images,
        [HBM] * 5 + [VMEM] * (2 + images),
        earlier,
        scratch_shapes=[
            pltpu.VMEM((most + WINDOW, D), BF16),
            pltpu.VMEM((parts, 2 * D + 16, D), BF16),
            pltpu.VMEM((SLOTS, D), BF16),
            pltpu.VMEM((SLOTS, 128), BF16),
            pltpu.VMEM((SLOTS, 128), F32),
            pltpu.VMEM((SLOTS, D), F32),
            pltpu.VMEM((parts, SLOTS, D), BF16),
            pltpu.VMEM((parts, SLOTS, D), BF16),
            pltpu.SemaphoreType.DMA((parts,)),
            pltpu.SemaphoreType.DMA((5,)),
            pltpu.SemaphoreType.DMA((2 + 2 * parts,)),
        ],
        megabytes=60,
        work=(2.5e10, 2e7),
    )


def gradient(spans, left, right, bias, earlier):
    parts = FF // D
    more = [] if bias is None else [bias]
    tall = D + 16 * len(more)
    return call(
        functools.partial(gradient_kernel, bool(more)),
        [spans, left, right, *more],
        [SMEM, HBM, HBM] + [VMEM] * len(more),
        [shape((parts, tall, D))],
        [HBM],
        earlier,
        token=True,
        scratch_shapes=[
            pltpu.VMEM((SLOTS, D), BF16),
            pltpu.VMEM((parts, SLOTS, D), BF16),
            pltpu.VMEM((parts, tall, D), BF16),
            pltpu.SemaphoreType.DMA((1 + 2 * parts,)),
            pltpu.SemaphoreType.DMA((parts,)),
        ],
        megabytes=50,
        work=(1.2e10, 3e7),
    )


def expert_result(begin, end, tables, hidden, gates, weights, second_bias, back, earlier):
    parts = FF // D
    most = hidden.shape[0]
    return call(
        functools.partial(result_kernel, begin),
        [*tables, hidden, gates, weights, second_bias, back],
        [SMEM, VMEM, HBM, HBM, HBM, VMEM, HBM],
        [shape((1, SEQ, D))] * (end - begin) + [shape((most, D))],
        [VMEM] * (end - begin) + [HBM],
        earlier,
        token=True,
        scratch_shapes=[
            pltpu.VMEM((parts, SLOTS, D), BF16),
            pltpu.VMEM((parts, D, D), BF16),
            pltpu.VMEM((SLOTS, 128), F32),
            pltpu.VMEM((SLOTS, D), F32),
            pltpu.VMEM((SLOTS, D), BF16),
            pltpu.VMEM((most + WINDOW, D), BF16),
            pltpu.SemaphoreType.DMA((2 + 2 * parts,)),
            pltpu.SemaphoreType.DMA((1,)),
        ],
        megabytes=50,
        work=(1.6e10, 3e7),
    )


def pack(first, second, small, earlier):
    return call(
        pack_kernel,
        [first, second, small],
        [VMEM] * 3,
        [shape((2 * D + 16, D))],
        [VMEM],
        earlier,
        token=True,
    )


def ring_add(blocks, received, is_first, earlier=()):
    return call(
        functools.partial(ring_add_kernel, is_first),
        [*blocks[0:2], received[0], *blocks[2:4], received[1]],
        [VMEM] * 6,
        [shape((2, SEQ, D))] * 2,
        [VMEM] * 2,
        earlier,
    )


def token_kernel(out):
    out[...] = jnp.zeros_like(out)


def token_of(*earlier):
    return call(token_kernel, [], [], shape((8, 128), F32), VMEM, earlier, work=(0, 0))


def after(value, *earlier, megabytes=32):
    return call(
        nothing_kernel,
        [value],
        [ANY],
        shape(value.shape, value.dtype),
        ANY,
        earlier,
        input_output_aliases={0: 0},
        megabytes=megabytes,
        work=(0, 0),
    )


def body(
    count,
    tokens,
    norm_gains,
    shifts,
    attn_weight,
    out_weight,
    router_weight,
    expert_in,
    expert_in_bias,
    expert_down,
    expert_down_bias,
    routes,
    cotangent,
):
    ring = Ring(count)
    sources = ring.sources()
    wide, tp = lax.axis_index("wide"), lax.axis_index("tp")
    core, far = tp % 2, tp // 2
    rows = D // count
    rows_up = -(-rows // 16) * 16
    experts = router_weight.shape[0]
    group_rows = routes.shape[0]
    local_rows = tokens.shape[0]
    capacity = (10 * group_rows // (4 * experts) + 7) // 8 * 8
    most = -(-count * min(local_rows, capacity) // SLOTS) * SLOTS
    near_groups = count - 1
    smalls = 7 + experts
    columns = D // count

    own_columns = columns // 4
    start = (tp * local_rows).reshape(1).astype(jnp.int32)
    block = prepare(
        start, attn_weight, out_weight, norm_gains, shifts, router_weight, routes, rows_up
    )
    tall = block.shape[0]
    expert_block = jnp.concatenate(
        [
            expert_in_bias,
            jnp.pad(expert_down_bias, ((0, 0), (0, D - GROUP))),
            jnp.zeros((14, D), BF16),
        ],
        axis=0,
    )
    packed = []

    def meanwhile(step, found):
        if step == 1:
            packed.extend(pack(expert_in, expert_down, expert_block, found[:1]))
            return packed[1:]
        return ()

    both = jnp.stack([block, to_x(block)])
    blocks, ends = ring.gather(both, lambda left, right, waits: (left[:1], right[1:]), meanwhile)
    own, across, small, in_turn = assemble(blocks, ends, sources, rows_up)
    own, across = (array[:, :rows].reshape(D, D) for array in (own, across))
    expert_all = after(packed[0], in_turn)
    expert_all = lax.all_gather(expert_all, "tp", axis=0, tiled=True).reshape(4, -1, D)
    second_bias = jnp.broadcast_to(
        expert_all[:, 2 * D + 1, :GROUP].reshape(1, D).astype(F32), (8, D)
    )
    beside, opposite = to_core(own), to_core(across)
    weights = (own, beside, across, opposite)
    place = tp.reshape(1).astype(jnp.int32)
    norms, router, bias = gather_norms(place, small, to_core(small), smalls, own_columns)

    spans, places, signs = make_tables(wide.reshape(1).astype(jnp.int32), in_turn)
    tables = (spans, places)

    tokens = tokens.reshape(2, SEQ, D)
    cotangent = after(cotangent.reshape(2, SEQ, D), *ends)
    first, second = [], []

    def meanwhile(step, found):
        if step == 0:
            return (spans,)
        if step == 1:
            first.extend(attend((0, 1), tokens, norms, bias, weights, found[:1]))
            return first[3:4]
        if step == 2:
            second.extend(attend((2, 3), tokens, norms, bias, weights, found[1:3], first))
            return second[2:3]
        return ()

    grad_blocks, grad_ends = ring.gather(cotangent, halves, meanwhile)
    qkv, mixed = (first[1], second[0]), (first[2], second[1])
    normed, sums, residual = first[0], second[2], second[3]

    def plan_of(groups):
        plan = []
        for at, group in enumerate(groups):
            plan += [(at, 0), (at, 1)] if group < count - 1 else [(at, 0), (at + 1, 0)]
        return plan

    everything = [plan_of(range(count)), [(count + 1, k) for k in range(2 * count)]]
    grad_slots, sign_slots, picked = pick(
        everything, tables, [*grad_blocks, *grad_ends, signs], (D, 128), most, [second[2]]
    )
    def meanwhile(step, found):
        if step == 0:
            return grad_ends
        if step == 1:
            return (picked,)
        return ()

    row_blocks, row_ends = ring.gather(second[4], halves, meanwhile)
    near = pick([plan_of(range(near_groups))], tables, row_blocks, (D,), most, (picked,))
    rows_, hidden, pre, gates, back, router_grad, bias_grad, *far_back = expert(
        plan_of(range(near_groups, count)), tables, near[0], grad_slots, sign_slots, expert_all,
        second_bias, router, [*row_blocks[near_groups:], *row_ends],
    )
    bias_rows = jnp.pad(bias_grad[0].reshape(4, GROUP), ((0, 4), (0, D - GROUP)))
    first_images = 2 * count - 6
    images = [None] * (2 * near_groups) + list(far_back)

    def send_back(images, waits, meanwhile):
        first, second = images[-2:]
        if waits:
            first, second = after(first, *waits), after(second, *waits)
        pair = ring.scatter_first(first, second)
        waits = meanwhile(0, (first, second))
        for step in range(1, ring.half):
            at = ring.half - step
            total = ring_add(images[4 * at - 2 : 4 * at + 2], pair, step == 1, waits)
            pair = ring.scatter_next(total)
            waits = meanwhile(step, total)
        return (images[0], images[1], pair[0], pair[1])

    kept = {}

    def meanwhile(step, waits):
        if step == 0:
            images[first_images:-2] = unpick(first_images, 2 * near_groups, tables, back, waits)
            kept["first"] = gradient(spans, rows_, pre, bias_rows, images[first_images : first_images + 1])
            return kept["first"][1:]
        if step == 1:
            kept["one"] = scatter_over_tp(after(kept["first"][0], waits[0], megabytes=50))
            *images[:first_images], kept["result"], token = expert_result(
                0, first_images, tables, hidden, gates, expert_all, second_bias, back, waits
            )
            return (token,)
        if step == 2:
            kept["second"] = gradient(spans, grad_slots, hidden, None, waits)
            return kept["second"][1:]
        if step == 3:
            kept["other"] = scatter_over_tp(after(kept["second"][0], waits[0], megabytes=50))
            kept["results"] = unpick(0, 2 * count, tables, kept["result"], waits)
        return ()

    def scatter_over_tp(grad):
        return lax.psum_scatter(grad.reshape(-1, D), "tp", scatter_dimension=0, tiled=True)

    returned = send_back(images, (), meanwhile)
    results = kept["results"]

    order = [count - 1]
    for step in range(ring.half - 1, 0, -1):
        order += [2 * step - 1, 2 * step]
    order.append(0)
    backward = []
    grads = []
    sources_tp = jnp.concatenate([sources, tp.reshape(1).astype(jnp.int32)])

    def meanwhile(step, waits):
        if step < 2:
            backward.append(
                attend_back(
                    tokens, cotangent, step, returned, residual, sums, norms, weights, qkv, waits,
                    backward[0][0] if step else None,
                )
            )
            return (backward[step][1],)
        if step == 2:
            small = [small_terms(place, backward, router_grad, -(-smalls // 16) * 16, waits)]
            for groups in ((3, 2), (1, 0)):
                grads.extend(
                    weight_grads(
                        normed, [b[2] for b in backward[:2]], [b[1] for b in backward[:2]],
                        mixed[groups[0] // 2], groups, order, sources_tp, small[0], rows, rows_up,
                        own_columns, grads[1:] or waits,
                    )
                )
            return (grads[3],)
        if step == 3:
            grads[:] = [after(grad, waits[0]) for grad in grads]
        return ()

    result = send_back(results, returned[2:], meanwhile)
    outputs = output(residual, result).reshape(-1, D)

    opposite, across, beside, own = grads
    sizes = (3 * count // 8, count // 4, count - 3 * count // 8 - count // 4)
    far_parts = [to_x(part) for part in sum_parts(across, to_core(opposite), sizes)]
    near_parts = sum_parts(own, to_core(beside), sizes)
    finished = finish(kept["one"], kept["other"])

    cut = (tall // 2 + 15) // 16 * 16
    found = [(part, i) for part in range(3) for i in range(sizes[part])]

    def step_of(entries, received, earlier=()):
        part = found[entries[0][0]][0]
        return tail(
            [(found[at][1], how) for at, how in entries],
            near_parts[part],
            far_parts[part],
            received,
            cut,
            None,
            earlier,
        )

    pair = ring.scatter_first(*step_of([(0, "none")], []))
    for step in range(ring.half - 1):
        how = ("low", "high") if step == 0 else ("full", "full")
        waits = (outputs,) if step == 1 else ()
        total = step_of([(2 * step + 1, how[0]), (2 * step + 2, how[1])], pair, waits)
        pair = ring.scatter_next(total)
    gains_grad, shifts_grad, router_grad, attn_grad, out_grad = tail(
        [(found[count - 1][1], "both")],
        near_parts[2],
        far_parts[2],
        pair,
        cut,
        (rows, own_columns, experts),
        finished[2:3],
    )
    return (
        outputs,
        backward[1][0].reshape(-1, D),
        gains_grad,
        shifts_grad,
        attn_grad,
        out_grad,
        router_grad,
        finished[0],
        finished[2],
        finished[1],
        finished[3],
    )


def solution(mesh):
    both = ("wide", "tp")
    return jax.shard_map(
        functools.partial(body, mesh.shape["wide"]),
        mesh=mesh,
        in_specs=(
            P(both, None),
            P(None, both),
            P(None, both),
            P(None, "wide", "tp"),
            P("tp", "wide"),
            P(None, both),
            P("wide", None, "tp"),
            P("wide", "tp"),
            P("wide", None, "tp"),
            P("wide", "tp"),
            P("wide", None),
            P(both, None),
        ),
        out_specs=(
            P(both, None),
            P(both, None),
            P(None, both),
            P(None, both),
            P(None, "wide", "tp"),
            P("tp", "wide"),
            P(None, both),
            P("wide", None, "tp"),
            P("wide", "tp"),
            P("wide", None, "tp"),
            P("wide", "tp"),
        ),
        check_vma=False,
    )
```

```python
import functools
import math

import jax
import jax.numpy as jnp
from jax import lax
from jax.experimental import pallas as pl
from jax.experimental.pallas import tpu as pltpu
from jax.sharding import PartitionSpec as P

D = 768
FF = 3072
HD = 64
SEQ = 200
VALID = 197
GROUP = 192
SLOTS = 960
WINDOW = 224
NARROW = 96
EPSILON = 1e-06
MASKED = -1000000000.0
F32 = jnp.float32
BF16 = jnp.bfloat16
VALID_LANE = 64
MIB = 1 << 20


def params(megabytes, sizes=None):
    semantics = None if sizes is None else ("arbitrary",) * sizes
    return pltpu.CompilerParams(
        vmem_limit_bytes=megabytes * MIB, dimension_semantics=semantics
    )


def cost(flops, moved, slow=0):
    return pl.CostEstimate(flops=int(flops), bytes_accessed=int(moved), transcendentals=int(slow))


def dot(left, right):
    return jnp.dot(left, right, preferred_element_type=F32)


def dot_nt(left, right):
    return lax.dot_general(left, right, (((1,), (1,)), ((), ())), preferred_element_type=F32)


def dot_tn(left, right):
    return lax.dot_general(left, right, (((0,), (0,)), ((), ())), preferred_element_type=F32)


def standardize(inputs):
    average = jnp.mean(inputs, axis=-1, keepdims=True)
    centered = inputs - average
    inverse = lax.rsqrt(jnp.mean(centered * centered, axis=-1, keepdims=True) + EPSILON)
    return centered * inverse, inverse


def norm_back(upstream, scaled, inverse, gain):
    grad_hat = upstream * gain
    mean_grad = jnp.mean(grad_hat, axis=-1, keepdims=True)
    mean_cross = jnp.mean(grad_hat * scaled, axis=-1, keepdims=True)
    return inverse * (grad_hat - mean_grad - scaled * mean_cross)


class Ring:
    def __init__(self, count):
        self.count = count
        self.half = count // 2
        self.order = list(range(0, count, 2)) + list(range(count - 1, 0, -2))
        self.ahead = [(self.order[i], self.order[(i + 1) % count]) for i in range(count)]
        self.behind = [(self.order[i], self.order[i - 1]) for i in range(count)]

    def sources(self):
        me = lax.axis_index("wide")
        place = jnp.where(me % 2 == 0, me // 2, self.count - 1 - me // 2)

        def at(position):
            position = position % self.count
            return jnp.where(
                position < self.half, 2 * position, 2 * (self.count - 1 - position) + 1
            )

        found = [at(place)]
        for step in range(1, self.half):
            found += [at(place - step), at(place + step)]
        return jnp.stack(found + [at(place + self.half)]).astype(jnp.int32)

    def forward(self, block):
        return lax.ppermute(block, "wide", self.ahead)

    def backward(self, block):
        return lax.ppermute(block, "wide", self.behind)

    def gather(self, block, ends, meanwhile=lambda step, found: (), begun=None):
        found = [block]
        left = right = block
        waits = meanwhile(0, found)
        for step in range(1, self.half):
            if waits and step == 1:
                left = right = found[0] = after(block, *waits)
            elif waits:
                left, right = found[-2:] = after(left, *waits), after(right, *waits)
            if step == 1 and begun is not None:
                left, right = begun
            else:
                left, right = self.forward(left), self.backward(right)
            found += [left, right]
            waits = meanwhile(step, found)
        first, second = ends(left, right, waits)
        return found, (self.forward(first), self.backward(second))

    def scatter_first(self, first, second):
        return self.backward(first), self.forward(second)

    def scatter_next(self, pair):
        return self.backward(pair[0]), self.forward(pair[1])


def to_core(block):
    return lax.ppermute(block, "tp", [(i, i ^ 1) for i in range(4)])


def to_x(block):
    return lax.ppermute(block, "tp", [(i, i ^ 2) for i in range(4)])


def prepare_kernel(
    rows, width, start, queries, outward, gains, shifts, router, routes, out
):
    square = jnp.concatenate(
        [queries[i].astype(F32) for i in range(3)] + [outward[...].astype(F32).T], axis=1
    )
    missing = out.shape[0] - 16 - rows
    if missing:
        square = jnp.concatenate([square, jnp.zeros((missing, D), F32)], axis=0)
    out[0 : rows + missing] = square.astype(BF16)
    small = jnp.concatenate(
        [gains[...].astype(F32), shifts[...].astype(F32), router[...].astype(F32)], axis=0
    )
    amount = small.shape[0]
    small = jnp.concatenate([small, jnp.zeros((-amount % 16, width), F32)], axis=0)
    parts = []
    for i in range(0, amount, 16):
        parts += [small[i : i + 16], jnp.zeros((16, 32 - width), F32)]
    filled = 32 * len(range(0, amount, 16))
    parts.append(jnp.zeros((16, 128 - filled), F32))
    chosen = routes[pl.ds(pl.multiple_of(start[0], 8), 2 * SEQ)].astype(F32).T
    chosen = jnp.concatenate([chosen, jnp.zeros((14, 2 * SEQ), F32)], axis=0)
    parts += [chosen, jnp.zeros((16, D - 128 - 2 * SEQ), F32)]
    out[rows + missing :] = jnp.concatenate(parts, axis=1).astype(BF16)


def assemble_kernel(count, rows, source_ref, *refs):
    blocks, first, second = refs[: count - 1], refs[count - 1], refs[count]
    own, across, small, in_turn = refs[count + 1 :]
    for i in range(count):
        place = source_ref[i]
        for k, weights in enumerate((own, across)):
            block = blocks[i].at[k] if i < count - 1 else (first, second)[k].at[0]
            weights[place] = block[0:rows]
            small[k, place] = block[rows:, 0:128]
            if k == 0:
                in_turn[i] = block[rows:]


def tables_kernel(mine, named, spans, places, signs):
    count = named.shape[0]
    size = 2 * count
    parts = [named[i].astype(F32) for i in range(count)]
    one, other = (
        jnp.concatenate(
            [part[j : j + 1, 128 + SEQ * k : 128 + SEQ * (k + 1)] for part in parts for k in range(2)], axis=0
        )
        for j in (0, 1)
    )
    expert_id = mine[0].astype(F32)
    is_chosen = (one == expert_id) | (other == expert_id)
    other = jnp.where(one == expert_id, other, one).astype(BF16)
    chosen = is_chosen.astype(F32).astype(BF16)
    row = lax.broadcasted_iota(jnp.int32, (SEQ, SEQ), 0)
    column = lax.broadcasted_iota(jnp.int32, (SEQ, SEQ), 1)
    rank = dot(chosen, (row < column).astype(F32).astype(BF16))
    counts = dot_nt(jnp.ones((8, SEQ), BF16), chosen)
    row = lax.broadcasted_iota(jnp.int32, (size, size), 0)
    column = lax.broadcasted_iota(jnp.int32, (size, size), 1)
    starts = dot(counts.astype(BF16), (row < column).astype(F32).astype(BF16))
    line = lax.broadcasted_iota(jnp.int32, (8, size), 0)
    spans[...] = jnp.where(line == 0, starts, starts + counts).astype(jnp.int32)
    amounts = jnp.sum(chosen.astype(F32), axis=1, keepdims=True).astype(BF16)
    lower = (column < row).astype(F32).astype(BF16)
    starts = dot(lower, jnp.broadcast_to(amounts, (size, 128)))[:, 0:1]
    places[...] = jnp.where(is_chosen, starts + rank, -1.0).astype(jnp.int32)
    turned = dot_tn(other, (row == column).astype(F32).astype(BF16))
    lane = lax.broadcasted_iota(jnp.int32, (SEQ, 128), 1).astype(F32)
    is_valid = (lax.broadcasted_iota(jnp.int32, (SEQ, 128), 0) < VALID).astype(F32)
    for i in range(size):
        sign = (lane == expert_id).astype(F32) - (lane == turned[:, i : i + 1]).astype(F32)
        signs[i] = jnp.where(lane == VALID_LANE, is_valid, sign).astype(BF16)


def norms_kernel(width, place, own, beside, norms, router, bias):
    tp = place[0]
    blocks, count = norms.shape[0] // 16, own.shape[1]
    found = [[] for _ in range(blocks)]
    for w in range(count):
        for t in range(4):
            far = t // 2 + (1 - 2 * (t // 2)) * (tp // 2)
            here = t % 2 + (1 - 2 * (t % 2)) * (tp % 2)
            values = jnp.where(
                here == 0, own[far, w].astype(F32), beside[far, w].astype(F32)
            )
            for k in range(blocks):
                found[k].append(values[:, 32 * k : 32 * k + width])
    for k in range(blocks):
        norms[16 * k : 16 * k + 16] = jnp.concatenate(found[k], axis=1)
    router[...] = jnp.zeros_like(router)
    rows = jnp.concatenate([norms[7:], jnp.zeros((7, D), F32)], axis=0)
    router[0 : 16 * blocks] = rows.astype(BF16)
    nothing = jnp.zeros((1, GROUP), F32)
    for j in range(4):
        t = tp + (1 - 2 * (tp % 2)) * (j % 2)
        t = t + (2 - 4 * (t // 2)) * (j // 2)
        queries, values = (
            pltpu.roll(norms[k : k + 1], D - t * GROUP, 1)[:, 0:GROUP] for k in (3, 4)
        )
        bias[j : j + 1] = jnp.concatenate([queries, nothing, values, nothing], axis=1)


def attend_kernel(groups, is_last, tokens, norms, bias, *refs):
    weights, refs = refs[: len(groups)], refs[len(groups) :]
    key_valid = lax.broadcasted_iota(jnp.int32, (SEQ, SEQ), 1) < VALID
    lane = lax.broadcasted_iota(jnp.int32, (SEQ, 128), 1)
    if is_last:
        normed_ref, sums_in, residual_in, qkv_ref, mixed_ref, sums_ref, residual_ref, second_ref = (
            refs
        )
    else:
        normed_ref, qkv_ref, mixed_ref, sums_ref, residual_ref = refs
    for i in range(2):
        if is_last:
            normed, residual, sums = normed_ref[i], residual_in[i], sums_in[i]
        else:
            inputs = tokens[i].astype(F32)
            scaled, _ = standardize(inputs)
            normed = (scaled * norms[0:1] + norms[2:3]).astype(BF16)
            normed_ref[i] = normed
            residual = inputs + norms[5:6]
            sums = jnp.zeros((SEQ, 128), F32)
        for k, j in enumerate(groups):
            projected = (dot(normed, weights[k][...]) + bias[j : j + 1]).astype(BF16)
            qkv_ref[i, k] = projected
            mixed = [jnp.zeros((SEQ, HD), BF16)]
            for h in range(3):
                query = projected[:, HD * h : HD * (h + 1)]
                key_rows = projected[:, GROUP + HD * h : GROUP + HD * (h + 1)]
                value = projected[:, 2 * GROUP + HD * h : 2 * GROUP + HD * (h + 1)]
                scores = jnp.where(key_valid, dot_nt(query, key_rows) * HD ** (-0.5), MASKED)
                row_max = jnp.max(scores, axis=-1, keepdims=True)
                exponent = jnp.exp(scores - row_max)
                row_sum = jnp.sum(exponent, axis=-1, keepdims=True)
                attention = (exponent / row_sum).astype(BF16)
                mixed.append(dot(attention, value).astype(BF16))
                sums = jnp.where(lane == 3 * j + h, row_max + jnp.log(row_sum), sums)
            mixed = jnp.concatenate(mixed, axis=1)
            mixed_ref[i, k] = mixed
            residual = residual + dot_nt(mixed, weights[k][:, D - 256 :])
        sums_ref[i] = sums
        residual_ref[i] = residual
        if is_last:
            scaled_two, _ = standardize(residual)
            second_ref[i] = (scaled_two * norms[1:2] + norms[6:7]).astype(BF16)


def attend_back_kernel(
    index, tokens, cotangent, one, other, left, right, residual_ref, sums_ref, norms, *refs
):
    weights = refs[:4]
    residual, sums_ref = residual_ref[index], sums_ref.at[index]
    halves_ = refs[4:6]
    input_grad, branch_ref, grads_ref, small_ref, bias_ref = refs[-5:]
    grad_two = (one, other)[index][0].astype(F32) + left[index].astype(F32) + right[index].astype(F32)
    scaled_two, inverse_two = standardize(residual)
    grad_mid = cotangent[index].astype(F32) + norm_back(
        grad_two, scaled_two, inverse_two, norms[1:2]
    )
    branch = grad_mid.astype(BF16)
    branch_ref[...] = branch
    key_valid = lax.broadcasted_iota(jnp.int32, (SEQ, SEQ), 1) < VALID
    grad_one = jnp.zeros((SEQ, D), F32)
    scale = HD ** (-0.5)
    for j in range(4):
        qkv_ref = halves_[j // 2].at[index, j % 2]
        upstream = dot(branch, weights[j][:, D - 256 :]).astype(BF16)
        grads = [[], [], []]
        for h in range(3):
            query = qkv_ref[:, HD * h : HD * (h + 1)]
            key_rows = qkv_ref[:, GROUP + HD * h : GROUP + HD * (h + 1)]
            value = qkv_ref[:, 2 * GROUP + HD * h : 2 * GROUP + HD * (h + 1)]
            up = upstream[:, HD * (h + 1) : HD * (h + 2)]
            scores = jnp.where(key_valid, dot_nt(query, key_rows) * scale, MASKED)
            attention = jnp.exp(scores - sums_ref[:, 3 * j + h : 3 * j + h + 1])
            grad_attn = dot_nt(up, value)
            inner = jnp.sum(attention * grad_attn, axis=-1, keepdims=True)
            grad_scores = (attention * (grad_attn - inner)).astype(BF16)
            grads[0].append((dot(grad_scores, key_rows) * scale).astype(BF16))
            grads[1].append((dot_tn(grad_scores, query) * scale).astype(BF16))
            grads[2].append(dot_tn(attention.astype(BF16), up).astype(BF16))
        whole = jnp.concatenate(
            grads[0] + grads[1] + grads[2] + [jnp.zeros((SEQ, GROUP), BF16)], axis=1
        )
        grads_ref[j] = whole
        bias_ref[j : j + 1] = jnp.sum(whole.astype(F32), axis=0, keepdims=True)
        grad_one = grad_one + dot_nt(whole, weights[j][...])
    scaled_one, inverse_one = standardize(tokens[index].astype(F32))
    input_back = grad_mid + norm_back(grad_one, scaled_one, inverse_one, norms[0:1])
    if index:
        input_grad[0] = refs[6][...]
        input_grad[1] = input_back
    else:
        input_grad[...] = input_back
    small_ref[...] = jnp.concatenate(
        [
            jnp.sum(part, axis=0, keepdims=True)
            for part in (
                grad_one * scaled_one,
                grad_two * scaled_two,
                grad_one,
                grad_mid,
                grad_two,
            )
        ]
        + [jnp.zeros((3, D), F32)],
        axis=0,
    )


def small_kernel(place, sums_one, sums_two, bias_one, bias_two, router, out):
    sums = sums_one[...] + sums_two[...]
    tp = place[0]
    queries, values = [], []
    for t in range(4):
        first = t % 2 + (1 - 2 * (t % 2)) * (tp % 2)
        second = t // 2 + (1 - 2 * (t // 2)) * (tp // 2)
        row = pl.ds(2 * second + first, 1)
        both = bias_one[row] + bias_two[row]
        queries.append(both[:, 0:GROUP])
        values.append(both[:, 2 * GROUP : 3 * GROUP])
    rows = [
        sums[0:3],
        jnp.concatenate(queries, axis=1),
        jnp.concatenate(values, axis=1),
        sums[3:5],
        router[0 : out.shape[0] - 7],
    ]
    out[...] = jnp.concatenate(rows, axis=0)


def weight_grad_kernel(groups, places, rows, width, sources, small, normed, grads_one, grads_two, *refs):
    grads, branch, mixed = (grads_one, grads_two), refs[0:2], refs[2]
    outs, whole = refs[3:-1], refs[-1]
    for out, j in zip(outs, groups):
        whole[...] = dot_tn(normed[0], grads[0][j]) + dot_tn(normed[1], grads[1][j])
        whole[:, D - 256 :] += dot_tn(branch[0][...], mixed[0, j % 2]) + dot_tn(
            branch[1][...], mixed[1, j % 2]
        )
        tp = sources[len(places)]
        tp = tp + (1 - 2 * (tp % 2)) * (j % 2)
        tp = tp + (2 - 4 * (tp // 2)) * (j // 2)
        missing = out.shape[1] - rows - 16
        for i, place in enumerate(places):
            start = pl.multiple_of(sources[place] * rows, 8)
            block = whole[pl.ds(start, rows)]
            if missing:
                block = jnp.concatenate([block, jnp.zeros((missing, D), F32)], axis=0)
            out[i, 0 : rows + missing] = block.astype(BF16)
            turned = pltpu.roll(small[...], D - (sources[place] * 4 + tp) * width, 1)
            low = [turned[k : k + 16, 0:32] for k in range(0, small.shape[0], 16)]
            low.append(jnp.zeros((16, D - 32 * len(low)), F32))
            out[i, rows + missing :] = jnp.concatenate(low, axis=1).astype(BF16)


def tile_rows(tile):
    return pl.ds(pl.multiple_of(tile * SLOTS, 16), SLOTS)


def moved(semaphores, *pairs):
    copies = [
        pltpu.make_async_copy(source, target, semaphores.at[i])
        for i, (source, target) in enumerate(pairs)
    ]
    for copy in copies:
        copy.start()
    for copy in copies:
        copy.wait()


def window_of(spans, image):
    return pl.multiple_of(spans[0, image] // 16 * 16, 16)


def any_wide(spans, images):
    found = jnp.int32(0)
    for i in images:
        found = jnp.maximum(found, spans[1, i] - window_of(spans, i))
    return found > NARROW


def pick_rows(spans, places_ref, begin, plan, sources, held):
    def some(i, start, height):
        slot = lax.broadcasted_iota(jnp.int32, (height, SEQ), 0) + start
        chosen = (places_ref[i : i + 1] == slot).astype(F32).astype(BF16)
        for target, stream in zip(held, plan):
            which, index = stream[i - begin]
            window = target.at[pl.ds(start, height)]
            window[...] += dot(chosen, sources[which][index]).astype(BF16)

    images = range(begin, begin + len(plan[0]))
    for i in images:
        some(i, window_of(spans, i), NARROW)

    @pl.when(any_wide(spans, images))
    def _():
        for i in images:
            more = pl.multiple_of(window_of(spans, i) + NARROW, 16)
            pl.when(spans[1, i] > more)(functools.partial(some, i, more, WINDOW - NARROW))


def unpick_rows(spans, places_ref, begin, held, outs):
    total = total_of(spans)

    def some(i, start, height):
        slot = lax.broadcasted_iota(jnp.int32, (height, SEQ), 0) + start
        chosen = (places_ref[i : i + 1] == slot).astype(F32).astype(BF16)
        row = lax.broadcasted_iota(jnp.int32, (height, D), 0) + start
        window = held[pl.ds(start, height)]
        window = jnp.where(row < total, window, jnp.zeros_like(window))
        return dot_tn(chosen, window).astype(BF16)

    images = range(begin, begin + len(outs))
    for i in images:
        outs[i - begin][0] = some(i, window_of(spans, i), NARROW)

    @pl.when(any_wide(spans, images))
    def _():
        for i in images:
            more = pl.multiple_of(window_of(spans, i) + NARROW, 16)

            @pl.when(spans[1, i] > more)
            def _(i=i, more=more):
                outs[i - begin][0] += some(i, more, WINDOW - NARROW)


def total_of(spans):
    return spans[1, spans.shape[1] - 1]


def tiles_of(spans):
    return jnp.maximum(1, (total_of(spans) + SLOTS - 1) // SLOTS)


def clear_rows(spans, held):
    def clear(tile, carry):
        for target in held:
            target[tile_rows(tile)] = jnp.zeros((SLOTS, target.shape[1]), BF16)
        return carry

    lax.fori_loop(0, tiles_of(spans), clear, 0)


def pick_kernel(plan, spans, places_ref, sources, outs, scratch, semaphores):
    clear_rows(spans, scratch)
    pick_rows(spans, places_ref, 0, plan, sources, scratch)

    def store(tile, carry):
        at = tile_rows(tile)
        moved(semaphores, *[(held.at[at], out.at[at]) for held, out in zip(scratch, outs)])
        return carry

    lax.fori_loop(0, tiles_of(spans), store, 0)


def unpick_kernel(begin, spans, places_ref, array, *refs):
    outs, scratch, semaphores = refs[:-2], refs[-2], refs[-1]

    def load(tile, carry):
        at = tile_rows(tile)
        moved(semaphores, (array.at[at], scratch.at[at]))
        return carry

    lax.fori_loop(0, tiles_of(spans), load, 0)
    unpick_rows(spans, places_ref, begin, scratch, outs)


def expert_kernel(
    plan, count, spans, places_ref, near_hbm, grads_hbm, chosen_hbm, weights_hbm, second_bias,
    router, *refs,
):
    sources = refs[:count]
    (
        rows, weights, grads, chosen, gates, total, hidden, pre_back,
        weight_semaphores, in_semaphores, out_semaphores,
    ) = refs[-11:]
    rows_hbm, hidden_hbm, pre_hbm, gates_hbm, back_hbm, router_ref, bias_ref, *images = refs[
        count : -11
    ]
    begin = spans.shape[1] - len(plan)
    parts = FF // D
    loads = [
        pltpu.make_async_copy(weights_hbm.at[f], weights.at[f], weight_semaphores.at[f])
        for f in range(parts)
    ]
    start = tile_rows(0)
    early = [
        pltpu.make_async_copy(source.at[start], target, in_semaphores.at[2 + i])
        for i, (source, target) in enumerate(
            ((near_hbm, rows.at[start]), (chosen_hbm, chosen), (grads_hbm, grads))
        )
    ]
    early[0].start()
    loads[0].start()
    early[1].start()
    early[2].start()
    for load in loads[1:]:
        load.start()
    router_ref[...] = jnp.zeros_like(router_ref)
    bias_ref[...] = jnp.zeros_like(bias_ref)

    def fetch(tile, carry):
        at = tile_rows(tile)
        moved(in_semaphores, (near_hbm.at[at], rows.at[at]))
        return carry

    early[0].wait()
    lax.fori_loop(1, tiles_of(spans), fetch, 0)
    pick_rows(spans, places_ref, begin, [plan], sources, [rows])
    for load in loads + early[1:]:
        load.wait()

    def tile(m, carry):
        at = tile_rows(m)
        keep = pltpu.make_async_copy(rows.at[at], rows_hbm.at[at], out_semaphores.at[0])
        keep.start()

        @pl.when(m > 0)
        def _():
            moved(in_semaphores, (grads_hbm.at[at], grads), (chosen_hbm.at[at], chosen))

        lane = lax.broadcasted_iota(jnp.int32, (SLOTS, 128), 1)
        signs = jnp.where(lane < VALID_LANE, chosen[...].astype(F32), 0.0)
        is_valid = chosen[:, VALID_LANE : VALID_LANE + 1].astype(F32)
        gap = jnp.sum(dot_nt(rows[at], router[...]) * signs, axis=1, keepdims=True)
        weight = is_valid / (1.0 + jnp.exp(-gap))
        slope = weight / (1.0 + jnp.exp(gap))
        upstream = grads[...].astype(F32)
        direct = jnp.sum(upstream * second_bias[0:1], axis=1, keepdims=True)
        gates[...] = jnp.where(lane == 0, weight, jnp.where(lane == 1, slope, direct))
        bias_ref[0:1] += jnp.sum(weight * upstream, axis=0, keepdims=True)
        stores = []
        for f in range(parts):
            first, second = weights.at[f, 0:D], weights.at[f, D : 2 * D]
            bias = weights[f, 2 * D : 2 * D + 16][0:1].astype(F32)
            pre = dot(rows[at], first[...]) + bias
            upward = dot(grads[...], second[...])
            below = 0.5 * (1.0 + lax.erf(pre * 0.5**0.5))
            density = jnp.exp(-0.5 * pre * pre) * (0.5 / 3.141592653589793) ** 0.5
            activation = pre * below
            weight = gates[:, 0:1]
            added = jnp.sum(activation * upward, axis=1, keepdims=True)
            hidden[f] = (weight * activation).astype(BF16)
            pre_back[f] = (weight * upward * (below + pre * density)).astype(BF16)
            for k, (held, target) in enumerate(((hidden, hidden_hbm), (pre_back, pre_hbm))):
                stores.append(
                    pltpu.make_async_copy(
                        held.at[f],
                        target.at[at, pl.ds(f * D, D)],
                        out_semaphores.at[2 + 2 * f + k],
                    )
                )
                stores[-1].start()
            gates[...] += jnp.where(lane == 2, added, 0.0)
            if f:
                total[...] += dot_nt(pre_back[f], first[...])
            else:
                total[...] = dot_nt(pre_back[f], first[...])
        stores.append(pltpu.make_async_copy(gates, gates_hbm.at[at], out_semaphores.at[1]))
        stores[-1].start()
        logits_grad = (signs * gates[:, 1:2] * gates[:, 2:3]).astype(BF16)
        router_ref[...] += dot_tn(logits_grad, rows[at])
        keep.wait()
        rows[at] = (total[...] + dot(logits_grad, router[...])).astype(BF16)
        keep = pltpu.make_async_copy(rows.at[at], back_hbm.at[at], out_semaphores.at[0])
        keep.start()
        for store in [*stores, keep]:
            store.wait()
        return carry

    lax.fori_loop(0, tiles_of(spans), tile, 0)
    unpick_rows(spans, places_ref, begin, rows, images)


def gradient_kernel(with_bias, spans, *refs):
    if with_bias:
        left_hbm, right_hbm, bias, grad_hbm, left, right, grad, in_semaphores, out_semaphores = refs
    else:
        left_hbm, right_hbm, grad_hbm, left, right, grad, in_semaphores, out_semaphores = refs
    parts = FF // D

    def work(tile, adds):
        at = tile_rows(tile)
        pairs = [(left_hbm.at[at], left)]
        for f in range(parts):
            pairs.append((right_hbm.at[at, pl.ds(f * D, D)], right.at[f]))
            if adds:
                pairs.append((grad_hbm.at[f], grad.at[f]))
        loads = [
            pltpu.make_async_copy(source, target, in_semaphores.at[i])
            for i, (source, target) in enumerate(pairs)
        ]
        for load in loads:
            load.start()
        if adds:
            for load in loads:
                load.wait()
        else:
            loads[0].wait()
        stores = []
        for f in range(parts):
            if not adds:
                loads[1 + f].wait()
            one = dot_tn(left[...], right[f])
            if adds:
                one = one + grad[f, 0:D].astype(F32)
            grad[f, 0:D] = one.astype(BF16)
            if with_bias:
                sums = jnp.sum(right[f].astype(F32), axis=0, keepdims=True)
                if adds:
                    sums = sums + grad[f, D : D + 16].astype(F32)[0:1]
                line = lax.broadcasted_iota(jnp.int32, (16, D), 0)
                grad[f, D:] = jnp.where(line == 0, sums, bias[f : f + 1]).astype(BF16)
            stores.append(pltpu.make_async_copy(grad.at[f], grad_hbm.at[f], out_semaphores.at[f]))
            stores[-1].start()
        for store in stores:
            store.wait()

    work(0, False)

    def more(tile, carry):
        work(tile, True)
        return carry

    lax.fori_loop(1, tiles_of(spans), more, 0)


def result_kernel(
    begin, spans, places_ref, hidden_hbm, gates_hbm, weights_hbm, second_bias, back_hbm, *refs
):
    images, result_hbm = refs[:-9], refs[-9]
    hidden, second, gates, total, finished, back, in_semaphores, out_semaphores = refs[-8:]
    parts = FF // D

    def work(tile, carry):
        at = tile_rows(tile)
        pairs = [(back_hbm.at[at], back.at[at]), (gates_hbm.at[at], gates)]
        for f in range(parts):
            pairs.append((hidden_hbm.at[at, pl.ds(f * D, D)], hidden.at[f]))
            pairs.append((weights_hbm.at[f, pl.ds(D, D)], second.at[f]))
        loads = [
            pltpu.make_async_copy(source, target, in_semaphores.at[i])
            for i, (source, target) in enumerate(pairs)
        ]
        for load in loads:
            load.start()
        loads[0].wait()
        loads[1].wait()
        for f in range(parts):
            loads[2 + 2 * f].wait()
            loads[3 + 2 * f].wait()
            result = dot_nt(hidden[f], second[f])
            if f:
                total[...] += result
            else:
                total[...] = gates[:, 0:1] * second_bias[0:1] + result
        finished[...] = total[...].astype(BF16)
        moved(out_semaphores, (finished, result_hbm.at[at]))
        return carry

    lax.fori_loop(0, tiles_of(spans), work, 0)
    unpick_rows(spans, places_ref, begin, back, images)


def finish_kernel(one, other, first, second, first_bias, second_bias):
    first[0] = one[0:D].astype(F32)
    second[0] = other[...].astype(F32)
    last = one[D:].astype(F32)
    first_bias[...] = last[0:1]
    second_bias[...] = last[1:2, :GROUP]


def output_kernel(residual, one, other, left, right, out):
    for i, mine in enumerate((one, other)):
        total = mine[0].astype(F32) + left[i].astype(F32) + right[i].astype(F32)
        out[i] = (residual[i] + total).astype(BF16)


def pack_kernel(first, second, small, out):
    out[0:D] = first[0]
    out[D : 2 * D] = second[0]
    out[2 * D :] = small[...]


def ring_add_kernel(is_first, *refs):
    outs = refs[-2:]

    def sums(one, other):
        return (one.astype(F32) + other.astype(F32)).astype(BF16)

    for k, out in enumerate(outs):
        first, second, received = refs[3 * k : 3 * k + 3]
        if is_first:
            out[k] = sums((first, second)[k][0], received[0])
            out[1 - k] = (first, second)[1 - k][0]
        else:
            out[0] = sums(first[0], received[0])
            out[1] = sums(second[0], received[1])


def sum_parts_kernel(one, other, *outs):
    start = 0
    for out in outs:
        part = slice(start, start + out.shape[0])
        out[...] = (one[part].astype(F32) + other[part].astype(F32)).astype(BF16)
        start += out.shape[0]


def tail_kernel(entries, *refs):
    outs = refs[-5:] if entries[0][1] == "both" else refs[-len(entries) :]
    refs = list(refs[: -len(outs)])
    near, far = refs.pop(0), refs.pop(0)
    for (index, kind), out in zip(entries, outs):
        whole = near[index].astype(F32) + far[index].astype(F32)
        if kind == "none":
            out[...] = whole.astype(BF16)
        elif kind == "full":
            out[...] = (whole + refs.pop(0)[...].astype(F32)).astype(BF16)
        else:
            whole = whole + refs[0][...].astype(F32) + refs[1][...].astype(F32)
            gains, shifts, router, queries, outward = outs
            rows, width = outward.shape[1], gains.shape[1]
            for i in range(3):
                queries[i] = whole[0:rows, GROUP * i : GROUP * (i + 1)]
            outward[...] = whole[0:rows, 3 * GROUP :].T
            low = whole[near.shape[1] - 16 :]
            mine = [low[:, 32 * i : 32 * i + width] for i in range(4)]
            mine = jnp.concatenate(mine, axis=0)
            gains[...] = mine[0:2]
            shifts[...] = mine[2:7]
            router[...] = mine[7 : 7 + router.shape[0]]


def nothing_kernel(*refs):
    pass


SMEM = pl.BlockSpec(memory_space=pltpu.SMEM)
VMEM = pl.BlockSpec(memory_space=pltpu.VMEM)
ANY = pl.BlockSpec(memory_space=pl.ANY)
HBM = pl.BlockSpec(memory_space=pltpu.HBM)


def shape(dims, kind=BF16):
    return jax.ShapeDtypeStruct(dims, kind)


def call(kernel, operands, specs, out_shape, out_specs, earlier=(), **settings):
    size = len(operands)
    waits = len(earlier)

    def stripped(*refs):
        kernel(*refs[:size], *refs[size + waits :])

    megabytes = settings.pop("megabytes", None)
    if megabytes is None:
        flat_specs = out_specs if isinstance(out_specs, list) else [out_specs]
        flat_shapes = out_shape if isinstance(out_shape, list) else [out_shape]
        held = [a for a, spec in zip(operands, specs) if spec is VMEM]
        held += [a for a, spec in zip(flat_shapes, flat_specs) if spec is VMEM]
        amount = sum(a.size * a.dtype.itemsize for a in held)
        for scratch in settings.get("scratch_shapes", ()):
            if len(scratch.shape) > 1:
                amount += math.prod(scratch.shape) * jnp.dtype(scratch.dtype).itemsize
        megabytes = -(-amount * 11 // (10 * MIB)) + settings.pop("slack", 3)
    work = settings.pop("work", (1e6, 1e6))
    if settings.pop("token", False):
        place = size + waits + len(out_shape)
        out_shape = list(out_shape) + [shape((8, 128), F32)]
        out_specs = list(out_specs) + [VMEM]

        def stripped(*refs):
            kernel(*refs[:size], *refs[size + waits : place], *refs[place + 1 :])
            refs[place][...] = jnp.zeros((8, 128), F32)

    return pl.pallas_call(
        stripped,
        in_specs=list(specs) + [ANY] * waits,
        out_specs=out_specs,
        out_shape=out_shape,
        compiler_params=params(megabytes),
        cost_estimate=cost(*work),
        **settings,
    )(*operands, *earlier)


def prepare(start, attn_weight, out_weight, gains, shifts, router, routes, rows_up):
    return call(
        functools.partial(prepare_kernel, attn_weight.shape[1], gains.shape[1]),
        [start, attn_weight, out_weight, gains, shifts, router, routes],
        [SMEM] + [VMEM] * 6,
        shape((rows_up + 16, D)),
        VMEM,
    )


def assemble(blocks, parts, sources, rows):
    count = len(blocks) + 1
    tall = blocks[0].shape[1]
    return call(
        functools.partial(assemble_kernel, count, rows),
        [sources, *blocks, *parts],
        [SMEM] + [VMEM] * (count + 1),
        [shape((count, rows, D))] * 2
        + [shape((2, count, tall - rows, 128)), shape((count, tall - rows, D))],
        [VMEM] * 4,
    )


def make_tables(mine, named):
    size = 2 * named.shape[0]
    return call(
        tables_kernel,
        [mine, named],
        [SMEM, VMEM],
        [
            shape((8, size), jnp.int32),
            shape((size, SEQ), jnp.int32),
            shape((size, SEQ, 128)),
        ],
        [VMEM] * 3,
        slack=8,
        work=(3e9, 1e6),
    )


def halves_kernel(left, right, first, second):
    first[0] = left[0]
    second[0] = right[1]


def halves(left, right, waits):
    return call(
        halves_kernel,
        [left, right],
        [VMEM] * 2,
        [shape((1, *left.shape[1:]))] * 2,
        [VMEM] * 2,
        waits,
    )


def gather_norms(place, own, beside, smalls, width):
    return call(
        functools.partial(norms_kernel, width),
        [place, own, beside],
        [SMEM, VMEM, VMEM],
        [shape((-(-smalls // 16) * 16, D), F32), shape((128, D)), shape((8, D), F32)],
        [VMEM] * 3,
    )


def attend(groups, tokens, norms, bias, weights, earlier, before=None):
    more = [] if before is None else [before[0], *before[3:5]]
    outs = [
        shape((2, len(groups), SEQ, D)),
        shape((2, len(groups), SEQ, 256)),
        shape((2, SEQ, 128), F32),
        shape((2, SEQ, D), F32),
    ]
    rows = [shape((2, SEQ, D))]
    return call(
        functools.partial(attend_kernel, groups, bool(more)),
        [tokens, norms, bias, *[weights[j] for j in groups], *more],
        [VMEM] * (3 + len(groups) + len(more)),
        outs + rows if more else rows + outs,
        [VMEM] * 5,
        earlier,
        slack=10,
        work=(8e9, 9e6),
    )


def attend_back(
    tokens, cotangent, index, parts, residual, sums, norms, weights, qkv, earlier, other=None
):
    more = [] if other is None else [other]
    return call(
        functools.partial(attend_back_kernel, index),
        [tokens, cotangent, *parts, residual, sums, norms, *weights, *qkv, *more],
        [VMEM] * (15 + len(more)),
        [
            shape((2, SEQ, D) if more else (SEQ, D), F32),
            shape((SEQ, D)),
            shape((4, SEQ, D)),
            shape((8, D), F32),
            shape((4, D), F32),
        ],
        [VMEM] * 5,
        earlier,
        megabytes=58,
        work=(3e10, 9e6),
    )


def weight_grads(
    normed, grads, branch, mixed, groups, places, sources, small, rows, rows_up, width, earlier
):
    return call(
        functools.partial(weight_grad_kernel, groups, places, rows, width),
        [sources, small, normed, *grads, *branch, mixed],
        [SMEM] + [VMEM] * 7,
        [shape((len(places), rows_up + 16, D))] * len(groups),
        [VMEM] * len(groups),
        earlier,
        scratch_shapes=[pltpu.VMEM((D, D), F32)],
        slack=12,
        work=(2e10, 5e6),
    )


def small_terms(place, backward, router, rows, earlier):
    return call(
        small_kernel,
        [place, backward[0][3], backward[1][3], backward[0][4], backward[1][4], router],
        [SMEM] + [VMEM] * 5,
        shape((rows, D), F32),
        VMEM,
        earlier,
    )


def sum_parts(one, other, sizes):
    return call(
        sum_parts_kernel,
        [one, other],
        [VMEM] * 2,
        [shape((size,) + one.shape[1:]) for size in sizes],
        [VMEM] * len(sizes),
    )


def tail(entries, near, far, received, last=None, earlier=()):
    outs = [shape((near.shape[1], D))] * len(entries)
    if last is not None:
        rows, width, experts = last
        outs = [
            shape((2, width), F32),
            shape((5, width), F32),
            shape((experts, width), F32),
            shape((3, rows, GROUP), F32),
            shape((GROUP, rows), F32),
        ]
    return call(
        functools.partial(tail_kernel, entries),
        [near, far, *received],
        [VMEM] * (2 + len(received)),
        outs,
        [VMEM] * len(outs),
        earlier,
    )


def finish(one, other):
    return call(
        finish_kernel,
        [one, other],
        [VMEM] * 2,
        [shape((1, D, D), F32)] * 2 + [shape((1, D), F32), shape((1, GROUP), F32)],
        [VMEM] * 4,
    )


def output(residual, parts):
    return call(
        output_kernel, [residual, *parts], [VMEM] * 5, shape((2, SEQ, D)), VMEM
    )


def pick(plan, tables, sources, widths, most, earlier=()):
    streams = len(widths)

    def kernel(*refs):
        last = refs[-2 * streams - 1 :]
        pick_kernel(
            plan, refs[0], refs[1], refs[2:], last[:streams], last[streams : 2 * streams], last[-1]
        )

    return call(
        kernel,
        [*tables, *sources],
        [SMEM, VMEM] + [VMEM] * len(sources),
        [shape((most, width)) for width in widths],
        [HBM] * streams,
        earlier,
        token=True,
        scratch_shapes=[pltpu.VMEM((most + WINDOW, width), BF16) for width in widths]
        + [pltpu.SemaphoreType.DMA((streams,))],
        slack=6,
        work=(6e9, 6e6),
    )


def unpick(begin, end, tables, array, earlier=()):
    images = end - begin
    return call(
        functools.partial(unpick_kernel, begin),
        [*tables, array],
        [SMEM, VMEM, HBM],
        [shape((1, SEQ, D))] * images,
        [VMEM] * images,
        earlier,
        scratch_shapes=[
            pltpu.VMEM((array.shape[0] + WINDOW, D), BF16), pltpu.SemaphoreType.DMA((1,))
        ],
        megabytes=50,
        work=(2e10, 6e6),
    )


def expert(plan, tables, near, grads, chosen, weights, second_bias, router, sources, earlier=()):
    most = near.shape[0]
    parts = FF // D
    images = len(plan)
    return call(
        functools.partial(expert_kernel, plan, len(sources)),
        [*tables, near, grads, chosen, weights, second_bias, router, *sources],
        [SMEM, VMEM, HBM, HBM, HBM, HBM, VMEM, VMEM] + [VMEM] * len(sources),
        [
            shape((most, D)),
            shape((most, FF)),
            shape((most, FF)),
            shape((most, 128), F32),
            shape((most, D)),
            shape((128, D), F32),
            shape((8, D), F32),
        ]
        + [shape((1, SEQ, D))] * images,
        [HBM] * 5 + [VMEM] * (2 + images),
        earlier,
        scratch_shapes=[
            pltpu.VMEM((most + WINDOW, D), BF16),
            pltpu.VMEM((parts, 2 * D + 16, D), BF16),
            pltpu.VMEM((SLOTS, D), BF16),
            pltpu.VMEM((SLOTS, 128), BF16),
            pltpu.VMEM((SLOTS, 128), F32),
            pltpu.VMEM((SLOTS, D), F32),
            pltpu.VMEM((parts, SLOTS, D), BF16),
            pltpu.VMEM((parts, SLOTS, D), BF16),
            pltpu.SemaphoreType.DMA((parts,)),
            pltpu.SemaphoreType.DMA((5,)),
            pltpu.SemaphoreType.DMA((2 + 2 * parts,)),
        ],
        megabytes=60,
        work=(2.5e10, 2e7),
    )


def gradient(spans, left, right, bias, earlier):
    parts = FF // D
    more = [] if bias is None else [bias]
    tall = D + 16 * len(more)
    return call(
        functools.partial(gradient_kernel, bool(more)),
        [spans, left, right, *more],
        [SMEM, HBM, HBM] + [VMEM] * len(more),
        [shape((parts, tall, D))],
        [HBM],
        earlier,
        token=True,
        scratch_shapes=[
            pltpu.VMEM((SLOTS, D), BF16),
            pltpu.VMEM((parts, SLOTS, D), BF16),
            pltpu.VMEM((parts, tall, D), BF16),
            pltpu.SemaphoreType.DMA((1 + 2 * parts,)),
            pltpu.SemaphoreType.DMA((parts,)),
        ],
        megabytes=50,
        work=(1.2e10, 3e7),
    )


def expert_result(begin, end, tables, hidden, gates, weights, second_bias, back, earlier):
    parts = FF // D
    most = hidden.shape[0]
    return call(
        functools.partial(result_kernel, begin),
        [*tables, hidden, gates, weights, second_bias, back],
        [SMEM, VMEM, HBM, HBM, HBM, VMEM, HBM],
        [shape((1, SEQ, D))] * (end - begin) + [shape((most, D))],
        [VMEM] * (end - begin) + [HBM],
        earlier,
        token=True,
        scratch_shapes=[
            pltpu.VMEM((parts, SLOTS, D), BF16),
            pltpu.VMEM((parts, D, D), BF16),
            pltpu.VMEM((SLOTS, 128), F32),
            pltpu.VMEM((SLOTS, D), F32),
            pltpu.VMEM((SLOTS, D), BF16),
            pltpu.VMEM((most + WINDOW, D), BF16),
            pltpu.SemaphoreType.DMA((2 + 2 * parts,)),
            pltpu.SemaphoreType.DMA((1,)),
        ],
        megabytes=50,
        work=(1.6e10, 3e7),
    )


def pack(first, second, small, earlier):
    return call(
        pack_kernel,
        [first, second, small],
        [VMEM] * 3,
        [shape((2 * D + 16, D))],
        [VMEM],
        earlier,
        token=True,
    )


def ring_add(blocks, received, is_first, earlier=()):
    return call(
        functools.partial(ring_add_kernel, is_first),
        [*blocks[0:2], received[0], *blocks[2:4], received[1]],
        [VMEM] * 6,
        [shape((2, SEQ, D))] * 2,
        [VMEM] * 2,
        earlier,
    )


def token_kernel(out):
    out[...] = jnp.zeros_like(out)


def token_of(*earlier):
    return call(token_kernel, [], [], shape((8, 128), F32), VMEM, earlier, work=(0, 0))


def after(value, *earlier, megabytes=None):
    return call(
        nothing_kernel,
        [value],
        [ANY],
        shape(value.shape, value.dtype),
        ANY,
        earlier,
        input_output_aliases={0: 0},
        megabytes=megabytes or 1,
        work=(0, 0),
    )


def body(
    count,
    tokens,
    norm_gains,
    shifts,
    attn_weight,
    out_weight,
    router_weight,
    expert_in,
    expert_in_bias,
    expert_down,
    expert_down_bias,
    routes,
    cotangent,
):
    ring = Ring(count)
    sources = ring.sources()
    wide, tp = lax.axis_index("wide"), lax.axis_index("tp")
    core, far = tp % 2, tp // 2
    rows = D // count
    rows_up = -(-rows // 16) * 16
    experts = router_weight.shape[0]
    group_rows = routes.shape[0]
    local_rows = tokens.shape[0]
    capacity = (10 * group_rows // (4 * experts) + 7) // 8 * 8
    most = -(-count * min(local_rows, capacity) // SLOTS) * SLOTS
    near_groups = count - 1
    smalls = 7 + experts
    columns = D // count

    own_columns = columns // 4
    start = (tp * local_rows).reshape(1).astype(jnp.int32)
    block = prepare(
        start, attn_weight, out_weight, norm_gains, shifts, router_weight, routes, rows_up
    )
    tall = block.shape[0]
    expert_block = jnp.concatenate(
        [
            expert_in_bias,
            jnp.pad(expert_down_bias, ((0, 0), (0, D - GROUP))),
            jnp.zeros((14, D), BF16),
        ],
        axis=0,
    )
    packed = []

    def meanwhile(step, found):
        if step == 1:
            packed.extend(pack(expert_in, expert_down, expert_block, found[:1]))
            return packed[1:]
        return ()

    tokens, cotangent = tokens.reshape(2, SEQ, D), cotangent.reshape(2, SEQ, D)
    begun = (ring.forward(cotangent), ring.backward(cotangent))
    both = after(jnp.stack([block, to_x(block)]), *begun)
    blocks, ends = ring.gather(both, halves, meanwhile)
    own, across, small, in_turn = assemble(blocks, ends, sources, rows_up)
    own, across = (array[:, :rows].reshape(D, D) for array in (own, across))
    expert_all = after(packed[0], *ends)
    expert_all = lax.all_gather(expert_all, "tp", axis=0, tiled=True).reshape(4, -1, D)
    second_bias = jnp.broadcast_to(
        expert_all[:, 2 * D + 1, :GROUP].reshape(1, D).astype(F32), (8, D)
    )
    beside, opposite = to_core(own), to_core(across)
    weights = (own, beside, across, opposite)
    place = tp.reshape(1).astype(jnp.int32)
    norms, router, bias = gather_norms(place, small, to_core(small), smalls, own_columns)

    spans, places, signs = make_tables(wide.reshape(1).astype(jnp.int32), in_turn)
    tables = (spans, places)

    first, second = [], []

    def meanwhile(step, found):
        if step == 1:
            return ends
        if step == 2:
            first.extend(attend((0, 1), tokens, norms, bias, weights, (spans,)))
            return first[3:4]
        if step == 3:
            second.extend(attend((2, 3), tokens, norms, bias, weights, found[3:5], first))
            return second[2:3]
        return ()

    grad_blocks, grad_ends = ring.gather(cotangent, halves, meanwhile, begun)
    qkv, mixed = (first[1], second[0]), (first[2], second[1])
    normed, sums, residual = first[0], second[2], second[3]

    def plan_of(groups):
        plan = []
        for at, group in enumerate(groups):
            plan += [(at, 0), (at, 1)] if group < count - 1 else [(at, 0), (at + 1, 0)]
        return plan

    everything = [plan_of(range(count)), [(count + 1, k) for k in range(2 * count)]]
    grad_slots, sign_slots, picked = pick(
        everything, tables, [*grad_blocks, *grad_ends, signs], (D, 128), most, [second[2]]
    )
    def meanwhile(step, found):
        if step == 0:
            return grad_ends
        if step == 1:
            return (picked,)
        return ()

    row_blocks, row_ends = ring.gather(second[4], halves, meanwhile)
    near = pick([plan_of(range(near_groups))], tables, row_blocks, (D,), most, (picked,))
    rows_, hidden, pre, gates, back, router_grad, bias_grad, *far_back = expert(
        plan_of(range(near_groups, count)), tables, near[0], grad_slots, sign_slots, expert_all,
        second_bias, router, [*row_blocks[near_groups:], *row_ends],
    )
    bias_rows = jnp.pad(bias_grad[0].reshape(4, GROUP), ((0, 4), (0, D - GROUP)))
    first_images = 2 * count - 6
    images = [None] * (2 * near_groups) + list(far_back)

    def send_back(images, waits, meanwhile):
        first, second = images[-2:]
        if waits:
            first, second = after(first, *waits), after(second, *waits)
        pair = ring.scatter_first(first, second)
        waits = meanwhile(0, (first, second))
        for step in range(1, ring.half):
            at = ring.half - step
            total = ring_add(images[4 * at - 2 : 4 * at + 2], pair, step == 1, waits)
            pair = ring.scatter_next(total)
            waits = meanwhile(step, total)
        return (images[0], images[1], pair[0], pair[1])

    kept = {}

    def meanwhile(step, waits):
        if step == 0:
            images[first_images:-2] = unpick(first_images, 2 * near_groups, tables, back, waits)
            kept["first"] = gradient(spans, rows_, pre, bias_rows, images[first_images : first_images + 1])
            return kept["first"][1:]
        if step == 1:
            kept["one"] = scatter_over_tp(after(kept["first"][0], waits[0], megabytes=50))
            *images[:first_images], kept["result"], token = expert_result(
                0, first_images, tables, hidden, gates, expert_all, second_bias, back, waits
            )
            return (token,)
        if step == 2:
            kept["second"] = gradient(spans, grad_slots, hidden, None, waits)
            return kept["second"][1:]
        if step == 3:
            kept["other"] = scatter_over_tp(after(kept["second"][0], waits[0], megabytes=50))
            kept["results"] = unpick(0, 2 * count, tables, kept["result"], waits)
        return ()

    def scatter_over_tp(grad):
        return lax.psum_scatter(grad.reshape(-1, D), "tp", scatter_dimension=0, tiled=True)

    returned = send_back(images, (), meanwhile)
    results = kept["results"]

    order = [count - 1]
    for step in range(ring.half - 1, 0, -1):
        order += [2 * step - 1, 2 * step]
    order.append(0)
    backward = []
    grads = []
    sources_tp = jnp.concatenate([sources, tp.reshape(1).astype(jnp.int32)])

    def meanwhile(step, waits):
        if step < 2:
            backward.append(
                attend_back(
                    tokens, cotangent, step, returned, residual, sums, norms, weights, qkv, waits,
                    backward[0][0] if step else None,
                )
            )
            return (backward[step][1],)
        if step == 2:
            small = [small_terms(place, backward, router_grad, -(-smalls // 16) * 16, waits)]
            for groups in ((3, 2), (1, 0)):
                grads.extend(
                    weight_grads(
                        normed, [b[2] for b in backward[:2]], [b[1] for b in backward[:2]],
                        mixed[groups[0] // 2], groups, order, sources_tp, small[0], rows, rows_up,
                        own_columns, grads[1:] or waits,
                    )
                )
            return (grads[3],)
        if step == 3:
            grads[:] = [after(grad, waits[0]) for grad in grads]
        return ()

    result = send_back(results, returned[2:], meanwhile)
    outputs = output(residual, result).reshape(-1, D)

    opposite, across, beside, own = grads
    sizes = (3 * count // 8, count // 4, count - 3 * count // 8 - count // 4)
    far_parts = [to_x(part) for part in sum_parts(across, to_core(opposite), sizes)]
    near_parts = sum_parts(own, to_core(beside), sizes)
    finished = finish(kept["one"], kept["other"])

    found = [(part, i) for part in range(3) for i in range(sizes[part])]

    def step_of(entries, received, earlier=()):
        part = found[entries[0][0]][0]
        return tail(
            [(found[at][1], how) for at, how in entries],
            near_parts[part],
            far_parts[part],
            received,
            None,
            earlier,
        )

    pair = [ring.backward(step_of([(0, "none")], [])[0])]
    for step in range(ring.half - 1):
        how = ("full", "none" if step == 0 else "full")
        waits = (outputs,) if step == 1 else ()
        total = step_of([(2 * step + 1, how[0]), (2 * step + 2, how[1])], pair, waits)
        pair = ring.scatter_next(total)
    gains_grad, shifts_grad, router_grad, attn_grad, out_grad = tail(
        [(found[count - 1][1], "both")],
        near_parts[2],
        far_parts[2],
        pair,
        (rows, own_columns, experts),
        finished[2:3],
    )
    return (
        outputs,
        backward[1][0].reshape(-1, D),
        gains_grad,
        shifts_grad,
        attn_grad,
        out_grad,
        router_grad,
        finished[0],
        finished[2],
        finished[1],
        finished[3],
    )


def solution(mesh):
    both = ("wide", "tp")
    return jax.shard_map(
        functools.partial(body, mesh.shape["wide"]),
        mesh=mesh,
        in_specs=(
            P(both, None),
            P(None, both),
            P(None, both),
            P(None, "wide", "tp"),
            P("tp", "wide"),
            P(None, both),
            P("wide", None, "tp"),
            P("wide", "tp"),
            P("wide", None, "tp"),
            P("wide", "tp"),
            P("wide", None),
            P(both, None),
        ),
        out_specs=(
            P(both, None),
            P(both, None),
            P(None, both),
            P(None, both),
            P(None, "wide", "tp"),
            P("tp", "wide"),
            P(None, both),
            P("wide", None, "tp"),
            P("wide", "tp"),
            P("wide", None, "tp"),
            P("wide", "tp"),
        ),
        check_vma=False,
    )
```

```python
import functools
import math

import jax
import jax.numpy as jnp
from jax import lax
from jax.experimental import pallas as pl
from jax.experimental.pallas import tpu as pltpu
from jax.sharding import PartitionSpec as P

D = 768
FF = 3072
HD = 64
SEQ = 200
VALID = 197
GROUP = 192
SLOTS = 960
WINDOW = 224
NARROW = 96
EPSILON = 1e-06
MASKED = -1000000000.0
F32 = jnp.float32
BF16 = jnp.bfloat16
VALID_LANE = 64
MIB = 1 << 20


def params(megabytes, sizes=None):
    semantics = None if sizes is None else ("arbitrary",) * sizes
    return pltpu.CompilerParams(
        vmem_limit_bytes=megabytes * MIB, dimension_semantics=semantics
    )


def cost(flops, moved, slow=0):
    return pl.CostEstimate(flops=int(flops), bytes_accessed=int(moved), transcendentals=int(slow))


def dot(left, right):
    return jnp.dot(left, right, preferred_element_type=F32)


def dot_nt(left, right):
    return lax.dot_general(left, right, (((1,), (1,)), ((), ())), preferred_element_type=F32)


def dot_tn(left, right):
    return lax.dot_general(left, right, (((0,), (0,)), ((), ())), preferred_element_type=F32)


def standardize(inputs):
    average = jnp.mean(inputs, axis=-1, keepdims=True)
    centered = inputs - average
    inverse = lax.rsqrt(jnp.mean(centered * centered, axis=-1, keepdims=True) + EPSILON)
    return centered * inverse, inverse


def norm_back(upstream, scaled, inverse, gain):
    grad_hat = upstream * gain
    mean_grad = jnp.mean(grad_hat, axis=-1, keepdims=True)
    mean_cross = jnp.mean(grad_hat * scaled, axis=-1, keepdims=True)
    return inverse * (grad_hat - mean_grad - scaled * mean_cross)


class Ring:
    def __init__(self, count):
        self.count = count
        self.half = count // 2
        self.order = list(range(0, count, 2)) + list(range(count - 1, 0, -2))
        self.ahead = [(self.order[i], self.order[(i + 1) % count]) for i in range(count)]
        self.behind = [(self.order[i], self.order[i - 1]) for i in range(count)]

    def sources(self):
        me = lax.axis_index("wide")
        place = jnp.where(me % 2 == 0, me // 2, self.count - 1 - me // 2)

        def at(position):
            position = position % self.count
            return jnp.where(
                position < self.half, 2 * position, 2 * (self.count - 1 - position) + 1
            )

        found = [at(place)]
        for step in range(1, self.half):
            found += [at(place - step), at(place + step)]
        return jnp.stack(found + [at(place + self.half)]).astype(jnp.int32)

    def forward(self, block):
        return lax.ppermute(block, "wide", self.ahead)

    def backward(self, block):
        return lax.ppermute(block, "wide", self.behind)

    def gather(self, block, ends, meanwhile=lambda step, found: (), begun=None):
        found = [block]
        left = right = block
        waits = meanwhile(0, found)
        for step in range(1, self.half):
            if waits and step == 1:
                left = right = found[0] = after(block, *waits)
            elif waits:
                left, right = found[-2:] = after(left, *waits), after(right, *waits)
            if step == 1 and begun is not None:
                left, right = begun
            else:
                left, right = self.forward(left), self.backward(right)
            found += [left, right]
            waits = meanwhile(step, found)
        first, second = ends(left, right, waits)
        return found, (self.forward(first), self.backward(second))

    def scatter_first(self, first, second):
        return self.backward(first), self.forward(second)

    def scatter_next(self, pair):
        return self.backward(pair[0]), self.forward(pair[1])


def to_core(block):
    return lax.ppermute(block, "tp", [(i, i ^ 1) for i in range(4)])


def to_x(block):
    return lax.ppermute(block, "tp", [(i, i ^ 2) for i in range(4)])


def prepare_kernel(
    rows, width, start, queries, outward, gains, shifts, router, routes, out
):
    square = jnp.concatenate(
        [queries[i].astype(F32) for i in range(3)] + [outward[...].astype(F32).T], axis=1
    )
    missing = out.shape[0] - 16 - rows
    if missing:
        square = jnp.concatenate([square, jnp.zeros((missing, D), F32)], axis=0)
    out[0 : rows + missing] = square.astype(BF16)
    small = jnp.concatenate(
        [gains[...].astype(F32), shifts[...].astype(F32), router[...].astype(F32)], axis=0
    )
    amount = small.shape[0]
    small = jnp.concatenate([small, jnp.zeros((-amount % 16, width), F32)], axis=0)
    parts = []
    for i in range(0, amount, 16):
        parts += [small[i : i + 16], jnp.zeros((16, 32 - width), F32)]
    filled = 32 * len(range(0, amount, 16))
    parts.append(jnp.zeros((16, 128 - filled), F32))
    chosen = routes[pl.ds(pl.multiple_of(start[0], 8), 2 * SEQ)].astype(F32).T
    chosen = jnp.concatenate([chosen, jnp.zeros((14, 2 * SEQ), F32)], axis=0)
    parts += [chosen, jnp.zeros((16, D - 128 - 2 * SEQ), F32)]
    out[rows + missing :] = jnp.concatenate(parts, axis=1).astype(BF16)


def assemble_kernel(count, rows, source_ref, *refs):
    blocks, first, second = refs[: count - 1], refs[count - 1], refs[count]
    own, across, small, in_turn = refs[count + 1 :]
    for i in range(count):
        place = source_ref[i]
        for k, weights in enumerate((own, across)):
            block = blocks[i].at[k] if i < count - 1 else (first, second)[k].at[0]
            weights[place] = block[0:rows]
            small[k, place] = block[rows:, 0:128]
            if k == 0:
                in_turn[i] = block[rows:]


def tables_kernel(mine, named, spans, places, signs):
    count = named.shape[0]
    size = 2 * count
    parts = [named[i].astype(F32) for i in range(count)]
    one, other = (
        jnp.concatenate(
            [part[j : j + 1, 128 + SEQ * k : 128 + SEQ * (k + 1)] for part in parts for k in range(2)], axis=0
        )
        for j in (0, 1)
    )
    expert_id = mine[0].astype(F32)
    is_chosen = (one == expert_id) | (other == expert_id)
    other = jnp.where(one == expert_id, other, one).astype(BF16)
    chosen = is_chosen.astype(F32).astype(BF16)
    row = lax.broadcasted_iota(jnp.int32, (SEQ, SEQ), 0)
    column = lax.broadcasted_iota(jnp.int32, (SEQ, SEQ), 1)
    rank = dot(chosen, (row < column).astype(F32).astype(BF16))
    counts = dot_nt(jnp.ones((8, SEQ), BF16), chosen)
    row = lax.broadcasted_iota(jnp.int32, (size, size), 0)
    column = lax.broadcasted_iota(jnp.int32, (size, size), 1)
    starts = dot(counts.astype(BF16), (row < column).astype(F32).astype(BF16))
    line = lax.broadcasted_iota(jnp.int32, (8, size), 0)
    spans[...] = jnp.where(line == 0, starts, starts + counts).astype(jnp.int32)
    amounts = jnp.sum(chosen.astype(F32), axis=1, keepdims=True).astype(BF16)
    lower = (column < row).astype(F32).astype(BF16)
    starts = dot(lower, jnp.broadcast_to(amounts, (size, 128)))[:, 0:1]
    places[...] = jnp.where(is_chosen, starts + rank, -1.0).astype(jnp.int32)
    turned = dot_tn(other, (row == column).astype(F32).astype(BF16))
    lane = lax.broadcasted_iota(jnp.int32, (SEQ, 128), 1).astype(F32)
    is_valid = (lax.broadcasted_iota(jnp.int32, (SEQ, 128), 0) < VALID).astype(F32)
    for i in range(size):
        sign = (lane == expert_id).astype(F32) - (lane == turned[:, i : i + 1]).astype(F32)
        signs[i] = jnp.where(lane == VALID_LANE, is_valid, sign).astype(BF16)


def norms_kernel(width, place, own, beside, norms, router, bias):
    tp = place[0]
    blocks, count = norms.shape[0] // 16, own.shape[1]
    found = [[] for _ in range(blocks)]
    for w in range(count):
        for t in range(4):
            far = t // 2 + (1 - 2 * (t // 2)) * (tp // 2)
            here = t % 2 + (1 - 2 * (t % 2)) * (tp % 2)
            values = jnp.where(
                here == 0, own[far, w].astype(F32), beside[far, w].astype(F32)
            )
            for k in range(blocks):
                found[k].append(values[:, 32 * k : 32 * k + width])
    for k in range(blocks):
        norms[16 * k : 16 * k + 16] = jnp.concatenate(found[k], axis=1)
    router[...] = jnp.zeros_like(router)
    rows = jnp.concatenate([norms[7:], jnp.zeros((7, D), F32)], axis=0)
    router[0 : 16 * blocks] = rows.astype(BF16)
    nothing = jnp.zeros((1, GROUP), F32)
    for j in range(4):
        t = tp + (1 - 2 * (tp % 2)) * (j % 2)
        t = t + (2 - 4 * (t // 2)) * (j // 2)
        queries, values = (
            pltpu.roll(norms[k : k + 1], D - t * GROUP, 1)[:, 0:GROUP] for k in (3, 4)
        )
        bias[j : j + 1] = jnp.concatenate([queries, nothing, values, nothing], axis=1)


def attend_kernel(groups, is_last, tokens, norms, bias, *refs):
    weights, refs = refs[: len(groups)], refs[len(groups) :]
    key_valid = lax.broadcasted_iota(jnp.int32, (SEQ, SEQ), 1) < VALID
    lane = lax.broadcasted_iota(jnp.int32, (SEQ, 128), 1)
    if is_last:
        normed_ref, sums_in, residual_in, qkv_ref, mixed_ref, sums_ref, residual_ref, second_ref = (
            refs
        )
    else:
        normed_ref, qkv_ref, mixed_ref, sums_ref, residual_ref = refs
    for i in range(2):
        if is_last:
            normed, residual, sums = normed_ref[i], residual_in[i], sums_in[i]
        else:
            inputs = tokens[i].astype(F32)
            scaled, _ = standardize(inputs)
            normed = (scaled * norms[0:1] + norms[2:3]).astype(BF16)
            normed_ref[i] = normed
            residual = inputs + norms[5:6]
            sums = jnp.zeros((SEQ, 128), F32)
        for k, j in enumerate(groups):
            projected = (dot(normed, weights[k][...]) + bias[j : j + 1]).astype(BF16)
            qkv_ref[i, k] = projected
            mixed = [jnp.zeros((SEQ, HD), BF16)]
            for h in range(3):
                query = projected[:, HD * h : HD * (h + 1)]
                key_rows = projected[:, GROUP + HD * h : GROUP + HD * (h + 1)]
                value = projected[:, 2 * GROUP + HD * h : 2 * GROUP + HD * (h + 1)]
                scores = jnp.where(key_valid, dot_nt(query, key_rows) * HD ** (-0.5), MASKED)
                row_max = jnp.max(scores, axis=-1, keepdims=True)
                exponent = jnp.exp(scores - row_max)
                row_sum = jnp.sum(exponent, axis=-1, keepdims=True)
                attention = (exponent / row_sum).astype(BF16)
                mixed.append(dot(attention, value).astype(BF16))
                sums = jnp.where(lane == 3 * j + h, row_max + jnp.log(row_sum), sums)
            mixed = jnp.concatenate(mixed, axis=1)
            mixed_ref[i, k] = mixed
            residual = residual + dot_nt(mixed, weights[k][:, D - 256 :])
        sums_ref[i] = sums
        residual_ref[i] = residual
        if is_last:
            scaled_two, _ = standardize(residual)
            second_ref[i] = (scaled_two * norms[1:2] + norms[6:7]).astype(BF16)


def attend_back_kernel(
    index, tokens, cotangent, one, other, left, right, residual_ref, sums_ref, norms, *refs
):
    weights = refs[:4]
    residual, sums_ref = residual_ref[index], sums_ref.at[index]
    halves_ = refs[4:6]
    input_grad, branch_ref, grads_ref, small_ref, bias_ref = refs[-5:]
    grad_two = (one, other)[index][0].astype(F32) + left[index].astype(F32) + right[index].astype(F32)
    scaled_two, inverse_two = standardize(residual)
    grad_mid = cotangent[index].astype(F32) + norm_back(
        grad_two, scaled_two, inverse_two, norms[1:2]
    )
    branch = grad_mid.astype(BF16)
    branch_ref[...] = branch
    key_valid = lax.broadcasted_iota(jnp.int32, (SEQ, SEQ), 1) < VALID
    grad_one = jnp.zeros((SEQ, D), F32)
    scale = HD ** (-0.5)
    for j in range(4):
        qkv_ref = halves_[j // 2].at[index, j % 2]
        upstream = dot(branch, weights[j][:, D - 256 :]).astype(BF16)
        grads = [[], [], []]
        for h in range(3):
            query = qkv_ref[:, HD * h : HD * (h + 1)]
            key_rows = qkv_ref[:, GROUP + HD * h : GROUP + HD * (h + 1)]
            value = qkv_ref[:, 2 * GROUP + HD * h : 2 * GROUP + HD * (h + 1)]
            up = upstream[:, HD * (h + 1) : HD * (h + 2)]
            scores = jnp.where(key_valid, dot_nt(query, key_rows) * scale, MASKED)
            attention = jnp.exp(scores - sums_ref[:, 3 * j + h : 3 * j + h + 1])
            grad_attn = dot_nt(up, value)
            inner = jnp.sum(attention * grad_attn, axis=-1, keepdims=True)
            grad_scores = (attention * (grad_attn - inner)).astype(BF16)
            grads[0].append((dot(grad_scores, key_rows) * scale).astype(BF16))
            grads[1].append((dot_tn(grad_scores, query) * scale).astype(BF16))
            grads[2].append(dot_tn(attention.astype(BF16), up).astype(BF16))
        whole = jnp.concatenate(
            grads[0] + grads[1] + grads[2] + [jnp.zeros((SEQ, GROUP), BF16)], axis=1
        )
        grads_ref[j] = whole
        bias_ref[j : j + 1] = jnp.sum(whole.astype(F32), axis=0, keepdims=True)
        grad_one = grad_one + dot_nt(whole, weights[j][...])
    scaled_one, inverse_one = standardize(tokens[index].astype(F32))
    input_back = grad_mid + norm_back(grad_one, scaled_one, inverse_one, norms[0:1])
    if index:
        input_grad[0] = refs[6][...]
        input_grad[1] = input_back
    else:
        input_grad[...] = input_back
    small_ref[...] = jnp.concatenate(
        [
            jnp.sum(part, axis=0, keepdims=True)
            for part in (
                grad_one * scaled_one,
                grad_two * scaled_two,
                grad_one,
                grad_mid,
                grad_two,
            )
        ]
        + [jnp.zeros((3, D), F32)],
        axis=0,
    )


def small_kernel(place, sums_one, sums_two, bias_one, bias_two, router, out):
    sums = sums_one[...] + sums_two[...]
    tp = place[0]
    queries, values = [], []
    for t in range(4):
        first = t % 2 + (1 - 2 * (t % 2)) * (tp % 2)
        second = t // 2 + (1 - 2 * (t // 2)) * (tp // 2)
        row = pl.ds(2 * second + first, 1)
        both = bias_one[row] + bias_two[row]
        queries.append(both[:, 0:GROUP])
        values.append(both[:, 2 * GROUP : 3 * GROUP])
    rows = [
        sums[0:3],
        jnp.concatenate(queries, axis=1),
        jnp.concatenate(values, axis=1),
        sums[3:5],
        router[0 : out.shape[0] - 7],
    ]
    out[...] = jnp.concatenate(rows, axis=0)


def weight_grad_kernel(groups, places, rows, width, sources, small, normed, grads_one, grads_two, *refs):
    grads, branch, mixed = (grads_one, grads_two), refs[0:2], refs[2]
    outs, whole = refs[3:-1], refs[-1]
    for out, j in zip(outs, groups):
        whole[...] = dot_tn(normed[0], grads[0][j]) + dot_tn(normed[1], grads[1][j])
        whole[:, D - 256 :] += dot_tn(branch[0][...], mixed[0, j % 2]) + dot_tn(
            branch[1][...], mixed[1, j % 2]
        )
        tp = sources[len(places)]
        tp = tp + (1 - 2 * (tp % 2)) * (j % 2)
        tp = tp + (2 - 4 * (tp // 2)) * (j // 2)
        missing = out.shape[1] - rows - 16
        for i, place in enumerate(places):
            start = pl.multiple_of(sources[place] * rows, 8)
            block = whole[pl.ds(start, rows)]
            if missing:
                block = jnp.concatenate([block, jnp.zeros((missing, D), F32)], axis=0)
            out[i, 0 : rows + missing] = block.astype(BF16)
            turned = pltpu.roll(small[...], D - (sources[place] * 4 + tp) * width, 1)
            low = [turned[k : k + 16, 0:32] for k in range(0, small.shape[0], 16)]
            low.append(jnp.zeros((16, D - 32 * len(low)), F32))
            out[i, rows + missing :] = jnp.concatenate(low, axis=1).astype(BF16)


def tile_rows(tile):
    return pl.ds(pl.multiple_of(tile * SLOTS, 16), SLOTS)


def moved(semaphores, *pairs):
    copies = [
        pltpu.make_async_copy(source, target, semaphores.at[i])
        for i, (source, target) in enumerate(pairs)
    ]
    for copy in copies:
        copy.start()
    for copy in copies:
        copy.wait()


def window_of(spans, image):
    return pl.multiple_of(spans[0, image] // 16 * 16, 16)


def any_wide(spans, images):
    found = jnp.int32(0)
    for i in images:
        found = jnp.maximum(found, spans[1, i] - window_of(spans, i))
    return found > NARROW


def pick_rows(spans, places_ref, begin, plan, sources, held):
    def some(i, start, height):
        slot = lax.broadcasted_iota(jnp.int32, (height, SEQ), 0) + start
        chosen = (places_ref[i : i + 1] == slot).astype(F32).astype(BF16)
        for target, stream in zip(held, plan):
            which, index = stream[i - begin]
            window = target.at[pl.ds(start, height)]
            window[...] += dot(chosen, sources[which][index]).astype(BF16)

    images = range(begin, begin + len(plan[0]))
    for i in images:
        some(i, window_of(spans, i), NARROW)

    @pl.when(any_wide(spans, images))
    def _():
        for i in images:
            more = pl.multiple_of(window_of(spans, i) + NARROW, 16)
            pl.when(spans[1, i] > more)(functools.partial(some, i, more, WINDOW - NARROW))


def unpick_rows(spans, places_ref, begin, held, outs):
    total = total_of(spans)

    def some(i, start, height):
        slot = lax.broadcasted_iota(jnp.int32, (height, SEQ), 0) + start
        chosen = (places_ref[i : i + 1] == slot).astype(F32).astype(BF16)
        row = lax.broadcasted_iota(jnp.int32, (height, D), 0) + start
        window = held[pl.ds(start, height)]
        window = jnp.where(row < total, window, jnp.zeros_like(window))
        return dot_tn(chosen, window).astype(BF16)

    images = range(begin, begin + len(outs))
    for i in images:
        outs[i - begin][0] = some(i, window_of(spans, i), NARROW)

    @pl.when(any_wide(spans, images))
    def _():
        for i in images:
            more = pl.multiple_of(window_of(spans, i) + NARROW, 16)

            @pl.when(spans[1, i] > more)
            def _(i=i, more=more):
                outs[i - begin][0] += some(i, more, WINDOW - NARROW)


def total_of(spans):
    return spans[1, spans.shape[1] - 1]


def tiles_of(spans):
    return jnp.maximum(1, (total_of(spans) + SLOTS - 1) // SLOTS)


def clear_rows(spans, held):
    def clear(tile, carry):
        for target in held:
            target[tile_rows(tile)] = jnp.zeros((SLOTS, target.shape[1]), BF16)
        return carry

    lax.fori_loop(0, tiles_of(spans), clear, 0)


def pick_kernel(plan, spans, places_ref, sources, outs, scratch, semaphores):
    clear_rows(spans, scratch)
    pick_rows(spans, places_ref, 0, plan, sources, scratch)

    def store(tile, carry):
        at = tile_rows(tile)
        moved(semaphores, *[(held.at[at], out.at[at]) for held, out in zip(scratch, outs)])
        return carry

    lax.fori_loop(0, tiles_of(spans), store, 0)


def unpick_kernel(begin, spans, places_ref, array, *refs):
    outs, scratch, semaphores = refs[:-2], refs[-2], refs[-1]

    def load(tile, carry):
        at = tile_rows(tile)
        moved(semaphores, (array.at[at], scratch.at[at]))
        return carry

    lax.fori_loop(0, tiles_of(spans), load, 0)
    unpick_rows(spans, places_ref, begin, scratch, outs)


def expert_kernel(
    plan, count, spans, places_ref, near_hbm, grads_hbm, chosen_hbm, weights_hbm, second_bias,
    router, *refs,
):
    sources = refs[:count]
    (
        rows, weights, grads, chosen, gates, total, hidden, pre_back,
        weight_semaphores, in_semaphores, out_semaphores,
    ) = refs[-11:]
    rows_hbm, hidden_hbm, pre_hbm, gates_hbm, back_hbm, router_ref, bias_ref, *images = refs[
        count : -11
    ]
    begin = spans.shape[1] - len(plan)
    parts = FF // D
    loads = [
        pltpu.make_async_copy(weights_hbm.at[f], weights.at[f], weight_semaphores.at[f])
        for f in range(parts)
    ]
    start = tile_rows(0)
    early = [
        pltpu.make_async_copy(source.at[start], target, in_semaphores.at[2 + i])
        for i, (source, target) in enumerate(
            ((near_hbm, rows.at[start]), (chosen_hbm, chosen), (grads_hbm, grads))
        )
    ]
    early[0].start()
    loads[0].start()
    early[1].start()
    early[2].start()
    for load in loads[1:]:
        load.start()
    router_ref[...] = jnp.zeros_like(router_ref)
    bias_ref[...] = jnp.zeros_like(bias_ref)

    def fetch(tile, carry):
        at = tile_rows(tile)
        moved(in_semaphores, (near_hbm.at[at], rows.at[at]))
        return carry

    early[0].wait()
    lax.fori_loop(1, tiles_of(spans), fetch, 0)
    pick_rows(spans, places_ref, begin, [plan], sources, [rows])
    for load in loads + early[1:]:
        load.wait()

    def tile(m, carry):
        at = tile_rows(m)
        keep = pltpu.make_async_copy(rows.at[at], rows_hbm.at[at], out_semaphores.at[0])
        keep.start()

        @pl.when(m > 0)
        def _():
            moved(in_semaphores, (grads_hbm.at[at], grads), (chosen_hbm.at[at], chosen))

        lane = lax.broadcasted_iota(jnp.int32, (SLOTS, 128), 1)
        signs = jnp.where(lane < VALID_LANE, chosen[...].astype(F32), 0.0)
        is_valid = chosen[:, VALID_LANE : VALID_LANE + 1].astype(F32)
        gap = jnp.sum(dot_nt(rows[at], router[...]) * signs, axis=1, keepdims=True)
        weight = is_valid / (1.0 + jnp.exp(-gap))
        slope = weight / (1.0 + jnp.exp(gap))
        upstream = grads[...].astype(F32)
        direct = jnp.sum(upstream * second_bias[0:1], axis=1, keepdims=True)
        gates[...] = jnp.where(lane == 0, weight, jnp.where(lane == 1, slope, direct))
        bias_ref[0:1] += jnp.sum(weight * upstream, axis=0, keepdims=True)
        stores = []
        for f in range(parts):
            first, second = weights.at[f, 0:D], weights.at[f, D : 2 * D]
            bias = weights[f, 2 * D : 2 * D + 16][0:1].astype(F32)
            pre = dot(rows[at], first[...]) + bias
            upward = dot(grads[...], second[...])
            below = 0.5 * (1.0 + lax.erf(pre * 0.5**0.5))
            density = jnp.exp(-0.5 * pre * pre) * (0.5 / 3.141592653589793) ** 0.5
            activation = pre * below
            weight = gates[:, 0:1]
            added = jnp.sum(activation * upward, axis=1, keepdims=True)
            hidden[f] = (weight * activation).astype(BF16)
            pre_back[f] = (weight * upward * (below + pre * density)).astype(BF16)
            for k, (held, target) in enumerate(((hidden, hidden_hbm), (pre_back, pre_hbm))):
                stores.append(
                    pltpu.make_async_copy(
                        held.at[f],
                        target.at[at, pl.ds(f * D, D)],
                        out_semaphores.at[2 + 2 * f + k],
                    )
                )
                stores[-1].start()
            gates[...] += jnp.where(lane == 2, added, 0.0)
            if f:
                total[...] += dot_nt(pre_back[f], first[...])
            else:
                total[...] = dot_nt(pre_back[f], first[...])
        stores.append(pltpu.make_async_copy(gates, gates_hbm.at[at], out_semaphores.at[1]))
        stores[-1].start()
        logits_grad = (signs * gates[:, 1:2] * gates[:, 2:3]).astype(BF16)
        router_ref[...] += dot_tn(logits_grad, rows[at])
        keep.wait()
        rows[at] = (total[...] + dot(logits_grad, router[...])).astype(BF16)
        keep = pltpu.make_async_copy(rows.at[at], back_hbm.at[at], out_semaphores.at[0])
        keep.start()
        for store in [*stores, keep]:
            store.wait()
        return carry

    lax.fori_loop(0, tiles_of(spans), tile, 0)
    unpick_rows(spans, places_ref, begin, rows, images)


def gradient_kernel(with_bias, spans, *refs):
    if with_bias:
        left_hbm, right_hbm, bias, grad_hbm, left, right, grad, in_semaphores, out_semaphores = refs
    else:
        left_hbm, right_hbm, grad_hbm, left, right, grad, in_semaphores, out_semaphores = refs
    parts = FF // D

    def work(tile, adds):
        at = tile_rows(tile)
        pairs = [(left_hbm.at[at], left)]
        for f in range(parts):
            pairs.append((right_hbm.at[at, pl.ds(f * D, D)], right.at[f]))
            if adds:
                pairs.append((grad_hbm.at[f], grad.at[f]))
        loads = [
            pltpu.make_async_copy(source, target, in_semaphores.at[i])
            for i, (source, target) in enumerate(pairs)
        ]
        for load in loads:
            load.start()
        if adds:
            for load in loads:
                load.wait()
        else:
            loads[0].wait()
        stores = []
        for f in range(parts):
            if not adds:
                loads[1 + f].wait()
            one = dot_tn(left[...], right[f])
            if adds:
                one = one + grad[f, 0:D].astype(F32)
            grad[f, 0:D] = one.astype(BF16)
            if with_bias:
                sums = jnp.sum(right[f].astype(F32), axis=0, keepdims=True)
                if adds:
                    sums = sums + grad[f, D : D + 16].astype(F32)[0:1]
                line = lax.broadcasted_iota(jnp.int32, (16, D), 0)
                grad[f, D:] = jnp.where(line == 0, sums, bias[f : f + 1]).astype(BF16)
            stores.append(pltpu.make_async_copy(grad.at[f], grad_hbm.at[f], out_semaphores.at[f]))
            stores[-1].start()
        for store in stores:
            store.wait()

    work(0, False)

    def more(tile, carry):
        work(tile, True)
        return carry

    lax.fori_loop(1, tiles_of(spans), more, 0)


def result_kernel(
    begin, spans, places_ref, hidden_hbm, gates_hbm, weights_hbm, second_bias, back_hbm, *refs
):
    images, result_hbm = refs[:-9], refs[-9]
    hidden, second, gates, total, finished, back, in_semaphores, out_semaphores = refs[-8:]
    parts = FF // D

    def work(tile, carry):
        at = tile_rows(tile)
        pairs = [(back_hbm.at[at], back.at[at]), (gates_hbm.at[at], gates)]
        for f in range(parts):
            pairs.append((hidden_hbm.at[at, pl.ds(f * D, D)], hidden.at[f]))
            pairs.append((weights_hbm.at[f, pl.ds(D, D)], second.at[f]))
        loads = [
            pltpu.make_async_copy(source, target, in_semaphores.at[i])
            for i, (source, target) in enumerate(pairs)
        ]
        for load in loads:
            load.start()
        loads[0].wait()
        loads[1].wait()
        for f in range(parts):
            loads[2 + 2 * f].wait()
            loads[3 + 2 * f].wait()
            result = dot_nt(hidden[f], second[f])
            if f:
                total[...] += result
            else:
                total[...] = gates[:, 0:1] * second_bias[0:1] + result
        finished[...] = total[...].astype(BF16)
        moved(out_semaphores, (finished, result_hbm.at[at]))
        return carry

    lax.fori_loop(0, tiles_of(spans), work, 0)
    unpick_rows(spans, places_ref, begin, back, images)


def finish_kernel(one, other, first, second, first_bias, second_bias):
    first[0] = one[0:D].astype(F32)
    second[0] = other[...].astype(F32)
    last = one[D:].astype(F32)
    first_bias[...] = last[0:1]
    second_bias[...] = last[1:2, :GROUP]


def output_kernel(residual, one, other, left, right, out):
    for i, mine in enumerate((one, other)):
        total = mine[0].astype(F32) + left[i].astype(F32) + right[i].astype(F32)
        out[i] = (residual[i] + total).astype(BF16)


def pack_kernel(first, second, small, out):
    out[0:D] = first[0]
    out[D : 2 * D] = second[0]
    out[2 * D :] = small[...]


def ring_add_kernel(is_first, *refs):
    outs = refs[-2:]

    def sums(one, other):
        return (one.astype(F32) + other.astype(F32)).astype(BF16)

    for k, out in enumerate(outs):
        first, second, received = refs[3 * k : 3 * k + 3]
        if is_first:
            out[k] = sums((first, second)[k][0], received[0])
            out[1 - k] = (first, second)[1 - k][0]
        else:
            out[0] = sums(first[0], received[0])
            out[1] = sums(second[0], received[1])


def sum_parts_kernel(one, other, *outs):
    start = 0
    for out in outs:
        part = slice(start, start + out.shape[0])
        out[...] = (one[part].astype(F32) + other[part].astype(F32)).astype(BF16)
        start += out.shape[0]


def tail_kernel(entries, *refs):
    outs = refs[-5:] if entries[0][1] == "both" else refs[-len(entries) :]
    refs = list(refs[: -len(outs)])
    near, far = refs.pop(0), refs.pop(0)
    for (index, kind), out in zip(entries, outs):
        whole = near[index].astype(F32) + far[index].astype(F32)
        if kind == "none":
            out[...] = whole.astype(BF16)
        elif kind == "full":
            out[...] = (whole + refs.pop(0)[...].astype(F32)).astype(BF16)
        else:
            whole = whole + refs[0][...].astype(F32) + refs[1][...].astype(F32)
            gains, shifts, router, queries, outward = outs
            rows, width = outward.shape[1], gains.shape[1]
            for i in range(3):
                queries[i] = whole[0:rows, GROUP * i : GROUP * (i + 1)]
            outward[...] = whole[0:rows, 3 * GROUP :].T
            low = whole[near.shape[1] - 16 :]
            mine = [low[:, 32 * i : 32 * i + width] for i in range(4)]
            mine = jnp.concatenate(mine, axis=0)
            gains[...] = mine[0:2]
            shifts[...] = mine[2:7]
            router[...] = mine[7 : 7 + router.shape[0]]


def nothing_kernel(*refs):
    pass


SMEM = pl.BlockSpec(memory_space=pltpu.SMEM)
VMEM = pl.BlockSpec(memory_space=pltpu.VMEM)
ANY = pl.BlockSpec(memory_space=pl.ANY)
HBM = pl.BlockSpec(memory_space=pltpu.HBM)


def shape(dims, kind=BF16):
    return jax.ShapeDtypeStruct(dims, kind)


def call(kernel, operands, specs, out_shape, out_specs, earlier=(), **settings):
    size = len(operands)
    waits = len(earlier)

    def stripped(*refs):
        kernel(*refs[:size], *refs[size + waits :])

    megabytes = settings.pop("megabytes", None)
    if megabytes is None:
        flat_specs = out_specs if isinstance(out_specs, list) else [out_specs]
        flat_shapes = out_shape if isinstance(out_shape, list) else [out_shape]
        held = [a for a, spec in zip(operands, specs) if spec is VMEM]
        held += [a for a, spec in zip(flat_shapes, flat_specs) if spec is VMEM]
        amount = sum(a.size * a.dtype.itemsize for a in held)
        for scratch in settings.get("scratch_shapes", ()):
            if len(scratch.shape) > 1:
                amount += math.prod(scratch.shape) * jnp.dtype(scratch.dtype).itemsize
        megabytes = -(-amount * 11 // (10 * MIB)) + settings.pop("slack", 3)
    work = settings.pop("work", (1e6, 1e6))
    if settings.pop("token", False):
        place = size + waits + len(out_shape)
        out_shape = list(out_shape) + [shape((8, 128), F32)]
        out_specs = list(out_specs) + [VMEM]

        def stripped(*refs):
            kernel(*refs[:size], *refs[size + waits : place], *refs[place + 1 :])
            refs[place][...] = jnp.zeros((8, 128), F32)

    return pl.pallas_call(
        stripped,
        in_specs=list(specs) + [ANY] * waits,
        out_specs=out_specs,
        out_shape=out_shape,
        compiler_params=params(megabytes),
        cost_estimate=cost(*work),
        **settings,
    )(*operands, *earlier)


def prepare(start, attn_weight, out_weight, gains, shifts, router, routes, rows_up):
    return call(
        functools.partial(prepare_kernel, attn_weight.shape[1], gains.shape[1]),
        [start, attn_weight, out_weight, gains, shifts, router, routes],
        [SMEM] + [VMEM] * 6,
        shape((rows_up + 16, D)),
        VMEM,
    )


def assemble(blocks, parts, sources, rows):
    count = len(blocks) + 1
    tall = blocks[0].shape[1]
    return call(
        functools.partial(assemble_kernel, count, rows),
        [sources, *blocks, *parts],
        [SMEM] + [VMEM] * (count + 1),
        [shape((count, rows, D))] * 2
        + [shape((2, count, tall - rows, 128)), shape((count, tall - rows, D))],
        [VMEM] * 4,
    )


def make_tables(mine, named):
    size = 2 * named.shape[0]
    return call(
        tables_kernel,
        [mine, named],
        [SMEM, VMEM],
        [
            shape((8, size), jnp.int32),
            shape((size, SEQ), jnp.int32),
            shape((size, SEQ, 128)),
        ],
        [VMEM] * 3,
        slack=8,
        work=(3e9, 1e6),
    )


def halves_kernel(left, right, first, second):
    first[0] = left[0]
    second[0] = right[1]


def halves(left, right, waits):
    return call(
        halves_kernel,
        [left, right],
        [VMEM] * 2,
        [shape((1, *left.shape[1:]))] * 2,
        [VMEM] * 2,
        waits,
    )


def gather_norms(place, own, beside, smalls, width):
    return call(
        functools.partial(norms_kernel, width),
        [place, own, beside],
        [SMEM, VMEM, VMEM],
        [shape((-(-smalls // 16) * 16, D), F32), shape((128, D)), shape((8, D), F32)],
        [VMEM] * 3,
    )


def attend(groups, tokens, norms, bias, weights, earlier, before=None):
    more = [] if before is None else [before[0], *before[3:5]]
    outs = [
        shape((2, len(groups), SEQ, D)),
        shape((2, len(groups), SEQ, 256)),
        shape((2, SEQ, 128), F32),
        shape((2, SEQ, D), F32),
    ]
    rows = [shape((2, SEQ, D))]
    return call(
        functools.partial(attend_kernel, groups, bool(more)),
        [tokens, norms, bias, *[weights[j] for j in groups], *more],
        [VMEM] * (3 + len(groups) + len(more)),
        outs + rows if more else rows + outs,
        [VMEM] * 5,
        earlier,
        slack=10,
        work=(8e9, 9e6),
    )


def attend_back(
    tokens, cotangent, index, parts, residual, sums, norms, weights, qkv, earlier, other=None
):
    more = [] if other is None else [other]
    return call(
        functools.partial(attend_back_kernel, index),
        [tokens, cotangent, *parts, residual, sums, norms, *weights, *qkv, *more],
        [VMEM] * (15 + len(more)),
        [
            shape((2, SEQ, D) if more else (SEQ, D), F32),
            shape((SEQ, D)),
            shape((4, SEQ, D)),
            shape((8, D), F32),
            shape((4, D), F32),
        ],
        [VMEM] * 5,
        earlier,
        megabytes=58,
        work=(3e10, 9e6),
    )


def weight_grads(
    normed, grads, branch, mixed, groups, places, sources, small, rows, rows_up, width, earlier
):
    return call(
        functools.partial(weight_grad_kernel, groups, places, rows, width),
        [sources, small, normed, *grads, *branch, mixed],
        [SMEM] + [VMEM] * 7,
        [shape((len(places), rows_up + 16, D))] * len(groups),
        [VMEM] * len(groups),
        earlier,
        scratch_shapes=[pltpu.VMEM((D, D), F32)],
        slack=12,
        work=(2e10, 5e6),
    )


def small_terms(place, backward, router, rows, earlier):
    return call(
        small_kernel,
        [place, backward[0][3], backward[1][3], backward[0][4], backward[1][4], router],
        [SMEM] + [VMEM] * 5,
        shape((rows, D), F32),
        VMEM,
        earlier,
    )


def sum_parts(one, other, sizes):
    return call(
        sum_parts_kernel,
        [one, other],
        [VMEM] * 2,
        [shape((size,) + one.shape[1:]) for size in sizes],
        [VMEM] * len(sizes),
    )


def tail(entries, near, far, received, last=None, earlier=()):
    outs = [shape((near.shape[1], D))] * len(entries)
    if last is not None:
        rows, width, experts = last
        outs = [
            shape((2, width), F32),
            shape((5, width), F32),
            shape((experts, width), F32),
            shape((3, rows, GROUP), F32),
            shape((GROUP, rows), F32),
        ]
    return call(
        functools.partial(tail_kernel, entries),
        [near, far, *received],
        [VMEM] * (2 + len(received)),
        outs,
        [VMEM] * len(outs),
        earlier,
    )


def finish(one, other):
    return call(
        finish_kernel,
        [one, other],
        [VMEM] * 2,
        [shape((1, D, D), F32)] * 2 + [shape((1, D), F32), shape((1, GROUP), F32)],
        [VMEM] * 4,
    )


def output(residual, parts):
    return call(
        output_kernel, [residual, *parts], [VMEM] * 5, shape((2, SEQ, D)), VMEM
    )


def pick(plan, tables, sources, widths, most, earlier=()):
    streams = len(widths)

    def kernel(*refs):
        last = refs[-2 * streams - 1 :]
        pick_kernel(
            plan, refs[0], refs[1], refs[2:], last[:streams], last[streams : 2 * streams], last[-1]
        )

    return call(
        kernel,
        [*tables, *sources],
        [SMEM, VMEM] + [VMEM] * len(sources),
        [shape((most, width)) for width in widths],
        [HBM] * streams,
        earlier,
        token=True,
        scratch_shapes=[pltpu.VMEM((most + WINDOW, width), BF16) for width in widths]
        + [pltpu.SemaphoreType.DMA((streams,))],
        slack=6,
        work=(6e9, 6e6),
    )


def unpick(begin, end, tables, array, earlier=()):
    images = end - begin
    return call(
        functools.partial(unpick_kernel, begin),
        [*tables, array],
        [SMEM, VMEM, HBM],
        [shape((1, SEQ, D))] * images,
        [VMEM] * images,
        earlier,
        scratch_shapes=[
            pltpu.VMEM((array.shape[0] + WINDOW, D), BF16), pltpu.SemaphoreType.DMA((1,))
        ],
        megabytes=50,
        work=(2e10, 6e6),
    )


def expert(plan, tables, near, grads, chosen, weights, second_bias, router, sources, earlier=()):
    most = near.shape[0]
    parts = FF // D
    images = len(plan)
    return call(
        functools.partial(expert_kernel, plan, len(sources)),
        [*tables, near, grads, chosen, weights, second_bias, router, *sources],
        [SMEM, VMEM, HBM, HBM, HBM, HBM, VMEM, VMEM] + [VMEM] * len(sources),
        [
            shape((most, D)),
            shape((most, FF)),
            shape((most, FF)),
            shape((most, 128), F32),
            shape((most, D)),
            shape((128, D), F32),
            shape((8, D), F32),
        ]
        + [shape((1, SEQ, D))] * images,
        [HBM] * 5 + [VMEM] * (2 + images),
        earlier,
        scratch_shapes=[
            pltpu.VMEM((most + WINDOW, D), BF16),
            pltpu.VMEM((parts, 2 * D + 16, D), BF16),
            pltpu.VMEM((SLOTS, D), BF16),
            pltpu.VMEM((SLOTS, 128), BF16),
            pltpu.VMEM((SLOTS, 128), F32),
            pltpu.VMEM((SLOTS, D), F32),
            pltpu.VMEM((parts, SLOTS, D), BF16),
            pltpu.VMEM((parts, SLOTS, D), BF16),
            pltpu.SemaphoreType.DMA((parts,)),
            pltpu.SemaphoreType.DMA((5,)),
            pltpu.SemaphoreType.DMA((2 + 2 * parts,)),
        ],
        megabytes=60,
        work=(2.5e10, 2e7),
    )


def gradient(spans, left, right, bias, earlier):
    parts = FF // D
    more = [] if bias is None else [bias]
    tall = D + 16 * len(more)
    return call(
        functools.partial(gradient_kernel, bool(more)),
        [spans, left, right, *more],
        [SMEM, HBM, HBM] + [VMEM] * len(more),
        [shape((parts, tall, D))],
        [HBM],
        earlier,
        token=True,
        scratch_shapes=[
            pltpu.VMEM((SLOTS, D), BF16),
            pltpu.VMEM((parts, SLOTS, D), BF16),
            pltpu.VMEM((parts, tall, D), BF16),
            pltpu.SemaphoreType.DMA((1 + 2 * parts,)),
            pltpu.SemaphoreType.DMA((parts,)),
        ],
        megabytes=50,
        work=(1.2e10, 3e7),
    )


def expert_result(begin, end, tables, hidden, gates, weights, second_bias, back, earlier):
    parts = FF // D
    most = hidden.shape[0]
    return call(
        functools.partial(result_kernel, begin),
        [*tables, hidden, gates, weights, second_bias, back],
        [SMEM, VMEM, HBM, HBM, HBM, VMEM, HBM],
        [shape((1, SEQ, D))] * (end - begin) + [shape((most, D))],
        [VMEM] * (end - begin) + [HBM],
        earlier,
        token=True,
        scratch_shapes=[
            pltpu.VMEM((parts, SLOTS, D), BF16),
            pltpu.VMEM((parts, D, D), BF16),
            pltpu.VMEM((SLOTS, 128), F32),
            pltpu.VMEM((SLOTS, D), F32),
            pltpu.VMEM((SLOTS, D), BF16),
            pltpu.VMEM((most + WINDOW, D), BF16),
            pltpu.SemaphoreType.DMA((2 + 2 * parts,)),
            pltpu.SemaphoreType.DMA((1,)),
        ],
        megabytes=50,
        work=(1.6e10, 3e7),
    )


def pack(first, second, small, earlier):
    return call(
        pack_kernel,
        [first, second, small],
        [VMEM] * 3,
        [shape((2 * D + 16, D))],
        [VMEM],
        earlier,
        token=True,
    )


def ring_add(blocks, received, is_first, earlier=()):
    return call(
        functools.partial(ring_add_kernel, is_first),
        [*blocks[0:2], received[0], *blocks[2:4], received[1]],
        [VMEM] * 6,
        [shape((2, SEQ, D))] * 2,
        [VMEM] * 2,
        earlier,
    )


def token_kernel(out):
    out[...] = jnp.zeros_like(out)


def token_of(*earlier):
    return call(token_kernel, [], [], shape((8, 128), F32), VMEM, earlier, work=(0, 0))


def after(value, *earlier, megabytes=None):
    return call(
        nothing_kernel,
        [value],
        [ANY],
        shape(value.shape, value.dtype),
        ANY,
        earlier,
        input_output_aliases={0: 0},
        megabytes=megabytes or 1,
        work=(0, 0),
    )


def body(
    count,
    tokens,
    norm_gains,
    shifts,
    attn_weight,
    out_weight,
    router_weight,
    expert_in,
    expert_in_bias,
    expert_down,
    expert_down_bias,
    routes,
    cotangent,
):
    ring = Ring(count)
    sources = ring.sources()
    wide, tp = lax.axis_index("wide"), lax.axis_index("tp")
    core, far = tp % 2, tp // 2
    rows = D // count
    rows_up = -(-rows // 16) * 16
    experts = router_weight.shape[0]
    group_rows = routes.shape[0]
    local_rows = tokens.shape[0]
    capacity = (10 * group_rows // (4 * experts) + 7) // 8 * 8
    most = -(-count * min(local_rows, capacity) // SLOTS) * SLOTS
    near_groups = count - 1
    smalls = 7 + experts
    columns = D // count

    own_columns = columns // 4
    start = (tp * local_rows).reshape(1).astype(jnp.int32)
    block = prepare(
        start, attn_weight, out_weight, norm_gains, shifts, router_weight, routes, rows_up
    )
    tall = block.shape[0]
    expert_block = jnp.concatenate(
        [
            expert_in_bias,
            jnp.pad(expert_down_bias, ((0, 0), (0, D - GROUP))),
            jnp.zeros((14, D), BF16),
        ],
        axis=0,
    )
    packed = []

    def meanwhile(step, found):
        if step == 1:
            packed.extend(pack(expert_in, expert_down, expert_block, found[:1]))
            return packed[1:]
        return ()

    tokens, cotangent = tokens.reshape(2, SEQ, D), cotangent.reshape(2, SEQ, D)
    begun = (ring.forward(cotangent), ring.backward(cotangent))
    both = after(jnp.stack([block, to_x(block)]), *begun)
    blocks, ends = ring.gather(both, halves, meanwhile)
    own, across, small, in_turn = assemble(blocks, ends, sources, rows_up)
    own, across = (array[:, :rows].reshape(D, D) for array in (own, across))
    expert_all = after(packed[0], *ends)
    expert_all = lax.all_gather(expert_all, "tp", axis=0, tiled=True).reshape(4, -1, D)
    second_bias = jnp.broadcast_to(
        expert_all[:, 2 * D + 1, :GROUP].reshape(1, D).astype(F32), (8, D)
    )
    beside, opposite = to_core(own), to_core(across)
    weights = (own, beside, across, opposite)
    place = tp.reshape(1).astype(jnp.int32)
    norms, router, bias = gather_norms(place, small, to_core(small), smalls, own_columns)

    spans, places, signs = make_tables(wide.reshape(1).astype(jnp.int32), in_turn)
    tables = (spans, places)

    first, second = [], []

    def meanwhile(step, found):
        if step == 1:
            return ends
        if step == 2:
            first.extend(attend((0, 1), tokens, norms, bias, weights, (spans,)))
            return first[3:4]
        if step == 3:
            second.extend(attend((2, 3), tokens, norms, bias, weights, found[3:5], first))
            return second[2:3]
        return ()

    grad_blocks, grad_ends = ring.gather(cotangent, halves, meanwhile, begun)
    qkv, mixed = (first[1], second[0]), (first[2], second[1])
    normed, sums, residual = first[0], second[2], second[3]

    def plan_of(groups):
        plan = []
        for at, group in enumerate(groups):
            plan += [(at, 0), (at, 1)] if group < count - 1 else [(at, 0), (at + 1, 0)]
        return plan

    everything = [plan_of(range(count)), [(count + 1, k) for k in range(2 * count)]]
    grad_slots, sign_slots, picked = pick(
        everything, tables, [*grad_blocks, *grad_ends, signs], (D, 128), most, [second[2]]
    )
    def meanwhile(step, found):
        if step == 0:
            return grad_ends
        if step == 1:
            return (picked,)
        return ()

    row_blocks, row_ends = ring.gather(second[4], halves, meanwhile)
    near = pick([plan_of(range(near_groups))], tables, row_blocks, (D,), most, (picked,))
    rows_, hidden, pre, gates, back, router_grad, bias_grad, *far_back = expert(
        plan_of(range(near_groups, count)), tables, near[0], grad_slots, sign_slots, expert_all,
        second_bias, router, [*row_blocks[near_groups:], *row_ends],
    )
    bias_rows = jnp.pad(bias_grad[0].reshape(4, GROUP), ((0, 4), (0, D - GROUP)))
    first_images = 2 * count - 6
    images = [None] * (2 * near_groups) + list(far_back)

    def send_back(images, waits, meanwhile):
        first, second = images[-2:]
        if waits:
            first, second = after(first, *waits), after(second, *waits)
        pair = ring.scatter_first(first, second)
        waits = meanwhile(0, (first, second))
        for step in range(1, ring.half):
            at = ring.half - step
            total = ring_add(images[4 * at - 2 : 4 * at + 2], pair, step == 1, waits)
            pair = ring.scatter_next(total)
            waits = meanwhile(step, total)
        return (images[0], images[1], pair[0], pair[1])

    kept = {}

    def meanwhile(step, waits):
        if step == 0:
            images[first_images:-2] = unpick(first_images, 2 * near_groups, tables, back, waits)
            kept["first"] = gradient(spans, rows_, pre, bias_rows, images[first_images : first_images + 1])
            return kept["first"][1:]
        if step == 1:
            kept["one"] = scatter_over_tp(after(kept["first"][0], waits[0], megabytes=50))
            *images[:first_images], kept["result"], token = expert_result(
                0, first_images, tables, hidden, gates, expert_all, second_bias, back, waits
            )
            return (token,)
        if step == 2:
            kept["second"] = gradient(spans, grad_slots, hidden, None, waits)
            return kept["second"][1:]
        if step == 3:
            kept["other"] = scatter_over_tp(after(kept["second"][0], waits[0], megabytes=50))
            kept["results"] = unpick(0, 2 * count, tables, kept["result"], waits)
        return ()

    def scatter_over_tp(grad):
        return lax.psum_scatter(grad.reshape(-1, D), "tp", scatter_dimension=0, tiled=True)

    returned = send_back(images, (), meanwhile)
    results = kept["results"]

    order = [count - 1]
    for step in range(ring.half - 1, 0, -1):
        order += [2 * step - 1, 2 * step]
    order.append(0)
    backward = []
    grads = []
    sources_tp = jnp.concatenate([sources, tp.reshape(1).astype(jnp.int32)])

    def meanwhile(step, waits):
        if step < 2:
            backward.append(
                attend_back(
                    tokens, cotangent, step, returned, residual, sums, norms, weights, qkv, waits,
                    backward[0][0] if step else None,
                )
            )
            return (backward[step][1],)
        if step == 2:
            small = [small_terms(place, backward, router_grad, -(-smalls // 16) * 16, waits)]
            for groups in ((3, 2), (1, 0)):
                grads.extend(
                    weight_grads(
                        normed, [b[2] for b in backward[:2]], [b[1] for b in backward[:2]],
                        mixed[groups[0] // 2], groups, order, sources_tp, small[0], rows, rows_up,
                        own_columns, grads[1:] or waits,
                    )
                )
            return (grads[3],)
        if step == 3:
            grads[:] = [after(grad, waits[0]) for grad in grads]
        return ()

    result = send_back(results, returned[2:], meanwhile)
    outputs = output(residual, result).reshape(-1, D)

    opposite, across, beside, own = grads
    sizes = (1, count // 2, count // 2 - 1)
    far_parts = [to_x(part) for part in sum_parts(across, to_core(opposite), sizes)]
    near_parts = sum_parts(own, to_core(beside), sizes)
    finished = finish(kept["one"], kept["other"])

    found = [(part, i) for part in range(3) for i in range(sizes[part])]

    def step_of(entries, received, earlier=()):
        part = found[entries[0][0]][0]
        return tail(
            [(found[at][1], how) for at, how in entries],
            near_parts[part],
            far_parts[part],
            received,
            None,
            earlier,
        )

    pair = [ring.backward(step_of([(0, "none")], [])[0])]
    for step in range(ring.half - 1):
        how = ("full", "none" if step == 0 else "full")
        waits = (outputs,) if step == 1 else ()
        total = step_of([(2 * step + 1, how[0]), (2 * step + 2, how[1])], pair, waits)
        pair = ring.scatter_next(total)
    gains_grad, shifts_grad, router_grad, attn_grad, out_grad = tail(
        [(found[count - 1][1], "both")],
        near_parts[2],
        far_parts[2],
        pair,
        (rows, own_columns, experts),
        finished[2:3],
    )
    return (
        outputs,
        backward[1][0].reshape(-1, D),
        gains_grad,
        shifts_grad,
        attn_grad,
        out_grad,
        router_grad,
        finished[0],
        finished[2],
        finished[1],
        finished[3],
    )


def solution(mesh):
    both = ("wide", "tp")
    return jax.shard_map(
        functools.partial(body, mesh.shape["wide"]),
        mesh=mesh,
        in_specs=(
            P(both, None),
            P(None, both),
            P(None, both),
            P(None, "wide", "tp"),
            P("tp", "wide"),
            P(None, both),
            P("wide", None, "tp"),
            P("wide", "tp"),
            P("wide", None, "tp"),
            P("wide", "tp"),
            P("wide", None),
            P(both, None),
        ),
        out_specs=(
            P(both, None),
            P(both, None),
            P(None, both),
            P(None, both),
            P(None, "wide", "tp"),
            P("tp", "wide"),
            P(None, both),
            P("wide", None, "tp"),
            P("wide", "tp"),
            P("wide", None, "tp"),
            P("wide", "tp"),
        ),
        check_vma=False,
    )
```
